128 devices in a mesh: gx: 8 (over x_hi, y), gy: 4 (over x_lo, core), gz: 4 (over z).
Axes of the slice: x: 4 (x_hi: 2, x_lo: 2; x = x_hi * 2 + x_lo), y: 4, z: 4, core: 2. Of those that a mesh axis runs over, the one named last changes fastest.
Arguments:
- state: float32 [2, 8, 16, 64, 9, 512], P(None, 'gx', 'gy', 'gz'), may hold values from -6 to 6
- deriv: bfloat16 [512, 1536], replicated, may hold values from -0.25 to 0.25
- lift: bfloat16 [384, 512], replicated, may hold values from -0.3125 to 0.3125
- material: float32 [3, 8, 16, 64], P(None, 'gx', 'gy', 'gz'), may hold values from 0.5 to 2
- stored: float32 [8, 16, 64, 9, 384], P('gx', 'gy', 'gz'), may hold values from -6 to 6
- orient: int32 [8, 16, 64, 6], P('gx', 'gy', 'gz'), may hold values from 0 to 7, as said below
- flags: int32 [8, 16, 64, 6], P('gx', 'gy', 'gz'), may hold values 0 or 1
Outputs:
- advanced: float32 [2, 8, 16, 64, 9, 512], P(None, 'gx', 'gy', 'gz')
- kernel: float32 [8, 16, 64, 9], P('gx', 'gy', 'gz')
The draws below stay inside these ranges and needn't reach their ends.
Inputs may be any that keep to these rules, and one draw needn't show every extreme that they name: `orient`: codes of the lower face (even s) of an element are the inverse symmetry of the code on the matching upper face of the element before it along that direction, taken cyclically over the whole grid.
All inputs are finite; a program needn't handle non-finite values. No bound on the sum of `flags` on one device may be relied on, other than what follows from the above.
Results may differ from the reference program's by a relative error of at most 0.0013.
Values sent between devices are 32-bit elements; how exact they have to be, the bound alone decides.
No kernel may reach another device: no remote copies, remote signals or barrier semaphores. Data moves between devices by JAX's collectives and lax.ppermute only.
A program may use at most 192 MiB of HBM per device.

```python
import math
import jax
import jax.numpy as jnp
from jax import lax

NP = 8
ELEMENT_NODES = 512
FACE_NODE_COUNT = 64
ELEMENTS_FIRST = 8
ELEMENTS_SECOND = 16
ELEMENTS_RADIAL = 64


def inverse_code(orient_code):
    swapped = 4 + orient_code // 2 % 2 + orient_code % 2 * 2
    return jnp.where(orient_code >= 4, swapped, orient_code)


def draw_orient(key, part):
    upper_faces = jax.random.randint(key, (ELEMENTS_FIRST, ELEMENTS_SECOND, ELEMENTS_RADIAL, 3), 0, 8, dtype=jnp.int32)
    lowers = [jnp.roll(inverse_code(upper_faces[..., d]), 1, axis=d) for d in range(3)]
    return jnp.stack([lowers[0], upper_faces[..., 0], lowers[1], upper_faces[..., 1], lowers[2], upper_faces[..., 2]], axis=-1)


def with_ends(entries, rng, smallest, top_value):
    dims = entries.shape
    spot = [jax.random.randint(jax.random.fold_in(rng, axis), (), 0, dims[axis]) for axis in range(len(dims))]
    entries = entries.at[tuple(spot)].set(smallest)
    longest = dims.index(max(dims))
    spot[longest] = (spot[longest] + 1) % dims[longest]
    return entries.at[tuple(spot)].set(top_value)


def shard_levels(key, shape, pieces, least, largest):
    def one(dim, blocks):
        draws = jax.random.uniform(jax.random.fold_in(jax.random.fold_in(key, 6), dim), (blocks,), jnp.float32, least / len(pieces), largest / len(pieces))
        return jnp.repeat(jnp.exp(draws), shape[dim] // blocks).reshape((-1,) + (1,) * (len(shape) - dim - 1))

    level = one(*pieces[0])
    for cut in pieces[1:]:
        level = level * one(*cut)
    return level


def scatter_about(key, extent, width, most, split=(), kind=jnp.bfloat16):
    factor_of = shard_levels(key, extent, split, -0.22, 0.18) if split else 1.0
    values = jax.random.normal(key, extent, jnp.float32) * width * factor_of
    return jnp.minimum(jnp.maximum(values, -most), most).astype(kind)


def setup_inputs(seed: int = 0) -> dict:
    seeds = jax.random.split(jax.random.key(seed), 8)
    state = scatter_about(seeds[0], (2, ELEMENTS_FIRST, ELEMENTS_SECOND, ELEMENTS_RADIAL, 9, ELEMENT_NODES), 1.0, 6.0, ((1, 8), (2, 4), (3, 4)), jnp.float32)
    deriv = scatter_about(seeds[1], (ELEMENT_NODES, 3 * ELEMENT_NODES), ELEMENT_NODES ** -0.5, 0.25)
    lift = scatter_about(seeds[2], (6 * FACE_NODE_COUNT, ELEMENT_NODES), (6 * FACE_NODE_COUNT) ** -0.5, 0.3125)
    material = jnp.clip(jnp.exp(math.log(2.0) - 1.3862944 * jax.random.uniform(seeds[3], (3, ELEMENTS_FIRST, ELEMENTS_SECOND, ELEMENTS_RADIAL), jnp.float32) ** shard_levels(seeds[3], (3, ELEMENTS_FIRST, ELEMENTS_SECOND, ELEMENTS_RADIAL), ((1, 8), (2, 4), (3, 4)), -0.2, 0.2)), 0.5, 2.0)
    stored = scatter_about(seeds[4], (ELEMENTS_FIRST, ELEMENTS_SECOND, ELEMENTS_RADIAL, 9, 6 * FACE_NODE_COUNT), 1.0, 6.0, ((0, 8), (1, 4), (2, 4)), jnp.float32)
    orient = draw_orient(jax.random.fold_in(seeds[7], 71), 0)
    flags = with_ends((jax.random.randint(seeds[6], (ELEMENTS_FIRST, ELEMENTS_SECOND, ELEMENTS_RADIAL, 6), 0, 2) < 1).astype(jnp.int32), jax.random.fold_in(seeds[6], 1), 0, 1)
    return dict(state=state, deriv=deriv, lift=lift, material=material, stored=stored, orient=orient, flags=flags)


step_size = 0.15
stress_slot = ((3, 8, 7), (8, 4, 6), (7, 6, 5))
pair_list = ((0, 0), (1, 1), (2, 2), (1, 2), (0, 2), (0, 1))

def face_of(values, face_index):
    node_cube = values.reshape(values.shape[:-1] + (NP, NP, NP))
    layer_index = 0 if face_index % 2 == 0 else NP - 1
    if face_index // 2 == 0:
        face_nodes = node_cube[..., layer_index, :, :]
    elif face_index // 2 == 1:
        face_nodes = node_cube[..., :, layer_index, :]
    else:
        face_nodes = node_cube[..., :, :, layer_index]
    return face_nodes.reshape(values.shape[:-1] + (FACE_NODE_COUNT,))

def reorient(trace, codes):
    square = trace.reshape(trace.shape[:-1] + (NP, NP))
    turned = jnp.swapaxes(square, -1, -2)
    result = jnp.zeros_like(trace)
    for code in range(8):
        if code >= 4:
            variant = turned
            if code % 2 == 1:
                variant = jnp.flip(variant, -1)
            if code // 2 % 2 == 1:
                variant = jnp.flip(variant, -2)
        else:
            variant = square
            if code % 2 == 1:
                variant = jnp.flip(variant, -2)
            if code // 2 % 2 == 1:
                variant = jnp.flip(variant, -1)
        result = jnp.where((codes == code)[..., None, None], variant.reshape(trace.shape), result)
    return result

def jacobian(fields, direction, first_lame, shear_mod, inv_density):
    velocity = [inv_density * fields[..., stress_slot[i][direction], :] for i in range(3)]
    along = fields[..., direction, :]
    stresses = []
    for i, j in pair_list:
        component = jnp.zeros_like(along)
        if i == j:
            component = component + first_lame * along
        if j == direction:
            component = component + shear_mod * fields[..., i, :]
        if i == direction:
            component = component + shear_mod * fields[..., j, :]
        stresses.append(component)
    return jnp.stack(velocity + stresses, axis=-2)

def exterior(inside, surface_flag):
    mirrored = jnp.concatenate([inside[..., :3, :], -inside[..., 3:, :]], axis=-2)
    return jnp.where(surface_flag == 1, mirrored, 0.0)

def section_terms(state, outside, material, stored, orient, flags, element_edges, deriv, lift):
    medium = material[:, None, :, :, :, None]
    first_lame = medium[0]
    shear_mod = medium[1]
    inv_density = 1.0 / medium[2]
    wave_speed = jnp.sqrt((first_lame + 2.0 * shear_mod) * inv_density)[..., None, :]
    fluxes = []
    adj_jumps = []
    for face_index in range(6):
        inside = face_of(state, face_index)
        outside_trace = reorient(outside[face_index], orient[None, :, :, :, face_index])
        if element_edges[face_index] is not None:
            surface_flag = flags[None, :, :, :, face_index, None, None]
            outside_trace = jnp.where(element_edges[face_index], exterior(inside, surface_flag), outside_trace)
        jump_trace = outside_trace - inside
        normal_sign = 1.0 if face_index % 2 == 1 else -1.0
        fluxes.append(0.5 * normal_sign * jacobian(jump_trace, face_index // 2, first_lame, shear_mod, inv_density) + 0.5 * wave_speed * jump_trace)
        adj_jumps.append(jump_trace[1])
    face_flux = jnp.stack(fluxes, axis=-2).astype(jnp.bfloat16)
    full_shape = state.shape
    row_count = full_shape[0] * full_shape[1] * full_shape[2] * full_shape[3] * full_shape[4]
    lifted = jnp.dot(face_flux.reshape(row_count, 6 * FACE_NODE_COUNT), lift, preferred_element_type=jnp.float32).reshape(full_shape)
    state_low = state.astype(jnp.bfloat16)
    gradients = jnp.dot(state_low.reshape(row_count, ELEMENT_NODES), deriv, preferred_element_type=jnp.float32).reshape(full_shape[:-1] + (3, ELEMENT_NODES))
    tendency = lifted
    for direction in range(3):
        tendency = tendency + jacobian(gradients[..., direction, :], direction, first_lame, shear_mod, inv_density)
    step_sizes = jnp.array([step_size, -step_size], jnp.float32).reshape(2, 1, 1, 1, 1, 1)
    advanced = state + step_sizes * tendency
    stored_faces = stored.reshape(stored.shape[:-1] + (6, FACE_NODE_COUNT))
    kernel = lax.optimization_barrier(jnp.sum(stored_faces * jnp.stack(adj_jumps, axis=-2), axis=(-2, -1))) / FACE_NODE_COUNT
    return (advanced, kernel)

def reference(state, deriv, lift, material, stored, orient, flags):
    upper_x = face_of(state, 1)
    lower_x = face_of(state, 0)
    second_position = jnp.arange(ELEMENTS_SECOND, dtype=jnp.int32).reshape(1, 1, ELEMENTS_SECOND, 1, 1, 1)
    radial_position = jnp.arange(ELEMENTS_RADIAL, dtype=jnp.int32).reshape(1, 1, 1, ELEMENTS_RADIAL, 1, 1)
    element_edges = [None, None, second_position == 0, second_position == ELEMENTS_SECOND - 1, radial_position == 0, radial_position == ELEMENTS_RADIAL - 1]

    def one_plane(plane_index):
        state_slab = lax.dynamic_index_in_dim(state, plane_index, 1, True)
        behind = lax.dynamic_index_in_dim(upper_x, (plane_index + ELEMENTS_FIRST - 1) % ELEMENTS_FIRST, 1, True)
        ahead_x = lax.dynamic_index_in_dim(lower_x, (plane_index + 1) % ELEMENTS_FIRST, 1, True)
        outside = [behind, ahead_x, jnp.roll(face_of(state_slab, 3), 1, axis=2), jnp.roll(face_of(state_slab, 2), -1, axis=2), jnp.roll(face_of(state_slab, 5), 1, axis=3), jnp.roll(face_of(state_slab, 4), -1, axis=3)]
        return section_terms(state_slab, outside, lax.dynamic_index_in_dim(material, plane_index, 1, True), lax.dynamic_index_in_dim(stored, plane_index, 0, True), lax.dynamic_index_in_dim(orient, plane_index, 0, True), lax.dynamic_index_in_dim(flags, plane_index, 0, True), element_edges, deriv, lift)
    advanced, kernel = lax.map(one_plane, jnp.arange(ELEMENTS_FIRST, dtype=jnp.int32))
    advanced = jnp.transpose(advanced[:, :, 0], (1, 0, 2, 3, 4, 5))
    return (advanced, kernel[:, 0])
```

```python
import jax
import jax.numpy as jnp
import numpy as np
from functools import partial
from jax import lax
from jax.experimental import pallas as pl
from jax.experimental.pallas import tpu as pltpu
from jax.sharding import PartitionSpec as P

NP = 8
FACE = NP * NP
LANES = 128
step_size = 0.15
stress_slot = ((3, 8, 7), (8, 4, 6), (7, 6, 5))
shear_pairs = ((6, 1, 2), (7, 0, 2), (8, 0, 1))
LIMIT = 56 * 1024 * 1024


def trace_table():
    table = np.zeros((NP**3, 4 * FACE), np.float32)
    for first in range(NP):
        for second in range(NP):
            m = first * NP + second
            table[first * 64 + second, m] = 1.0
            table[first * 64 + 56 + second, FACE + m] = 1.0
            table[first * 64 + second * 8, 2 * FACE + m] = 1.0
            table[first * 64 + second * 8 + 7, 3 * FACE + m] = 1.0
    return table


def lane_index(shape):
    return lax.broadcasted_iota(jnp.int32, shape, len(shape) - 1)


def merged(forward, adjoint, upper):
    rows = forward.shape[:-1]
    flat = (-1, LANES)
    turned = pltpu.roll(adjoint.reshape(flat), FACE, 1)
    own = (lane_index(turned.shape) >= FACE) == upper
    return jnp.where(own, forward.reshape(flat), turned).reshape(rows + (LANES,))


def pack_kernel(parity_ref, low_ref, high_ref, far_ref, near_ref):
    low = merged(low_ref[0, 0], low_ref[1, 0], False)
    high = merged(high_ref[0, 0], high_ref[1, 0], True)
    odd = parity_ref[0] == 1
    far_ref[0] = jnp.where(odd, high, low)
    near_ref[0] = jnp.where(odd, low, high)


def pack_faces(parity, state):
    _, count_y, fields, count_z, nodes = state.shape
    tiles = nodes // LANES
    block = (2, 1, fields, count_z, LANES)
    message = jax.ShapeDtypeStruct((count_y, fields, count_z, LANES), jnp.float32)
    out_spec = pl.BlockSpec((1, fields, count_z, LANES), lambda y, p: (y, 0, 0, 0))
    return pl.pallas_call(
        pack_kernel,
        out_shape=(message, message),
        grid_spec=pltpu.PrefetchScalarGridSpec(
            num_scalar_prefetch=1,
            grid=(count_y,),
            in_specs=[
                pl.BlockSpec(block, lambda y, p: (0, y, 0, 0, 0)),
                pl.BlockSpec(block, lambda y, p: (0, y, 0, 0, tiles - 1)),
            ],
            out_specs=(out_spec, out_spec),
        ),
        cost_estimate=pl.CostEstimate(flops=10**6, bytes_accessed=2 * 10**6, transcendentals=0),
        name="pack_faces",
    )(parity, state, state)


def trace_kernel(parity_ref, state_ref, table_ref, trace_ref, y_two, y_one, z_two, z_one):
    y = pl.program_id(0)
    _, _, fields, count_z, nodes = state_ref.shape
    table = table_ref[...]
    for s in range(2):
        values = state_ref[s, 0].reshape(fields * count_z, nodes)
        high = values.astype(jnp.bfloat16)
        low = (values - high.astype(jnp.float32)).astype(jnp.bfloat16)
        picked = jnp.dot(high, table, preferred_element_type=jnp.float32)
        picked = picked + jnp.dot(low, table, preferred_element_type=jnp.float32)
        trace_ref[s, 0] = picked.reshape(fields, count_z, 2 * LANES)
    odd_y = parity_ref[1] == 1
    odd_z = parity_ref[2] == 1

    @pl.when(y == 0)
    def _():
        down = merged(trace_ref[0, 0, :, :, :LANES], trace_ref[1, 0, :, :, :LANES], False)

        @pl.when(odd_y)
        def _():
            y_one[...] = down

        @pl.when(jnp.logical_not(odd_y))
        def _():
            y_two[...] = down

    @pl.when(y == pl.num_programs(0) - 1)
    def _():
        up = merged(trace_ref[0, 0, :, :, :LANES], trace_ref[1, 0, :, :, :LANES], True)

        @pl.when(odd_y)
        def _():
            y_two[...] = up

        @pl.when(jnp.logical_not(odd_y))
        def _():
            y_one[...] = up

    first = merged(trace_ref[0, 0, :, 0, LANES:], trace_ref[1, 0, :, 0, LANES:], False)
    last = merged(
        trace_ref[0, 0, :, count_z - 1, LANES:], trace_ref[1, 0, :, count_z - 1, LANES:], True
    )
    z_two[y] = jnp.where(odd_z, last, first)
    z_one[y] = jnp.where(odd_z, first, last)


def extract_traces(parity, state, table):
    _, count_y, fields, count_z, nodes = state.shape
    f32 = jnp.float32
    y_message = jax.ShapeDtypeStruct((fields, count_z, LANES), f32)
    z_message = jax.ShapeDtypeStruct((count_y, fields, LANES), f32)
    y_spec = pl.BlockSpec(y_message.shape, lambda y, p: (0, 0, 0))
    z_spec = pl.BlockSpec(z_message.shape, lambda y, p: (0, 0, 0))
    return pl.pallas_call(
        trace_kernel,
        out_shape=(
            jax.ShapeDtypeStruct((2, count_y, fields, count_z, 2 * LANES), f32),
            y_message,
            y_message,
            z_message,
            z_message,
        ),
        grid_spec=pltpu.PrefetchScalarGridSpec(
            num_scalar_prefetch=1,
            grid=(count_y,),
            in_specs=[
                pl.BlockSpec((2, 1, fields, count_z, nodes), lambda y, p: (0, y, 0, 0, 0)),
                pl.BlockSpec(table.shape, lambda y, p: (0, 0)),
            ],
            out_specs=(
                pl.BlockSpec((2, 1, fields, count_z, 2 * LANES), lambda y, p: (0, y, 0, 0, 0)),
                y_spec,
                y_spec,
                z_spec,
                z_spec,
            ),
        ),
        cost_estimate=pl.CostEstimate(flops=6 * 10**8, bytes_accessed=4 * 10**6, transcendentals=0),
        name="extract_traces",
    )(parity, state, table)


def spread(columns, rows, pick):
    return lax.dot_general(
        columns,
        pick,
        (((0,), (0,)), ((), ())),
        precision=lax.Precision.HIGHEST,
        preferred_element_type=jnp.float32,
    )


def volume_kernel(
    ends_ref, state_ref, d0_ref, d1_ref, d2_ref, material_ref, orient_ref, flags_ref,
    partial_ref, coef_ref, source_ref, edge_ref,
    low_ref, grad_ref, div_ref, wide_ref,
):
    step = pl.program_id(0)
    _, count_y, fields, count_z, _ = state_ref.shape
    rows = 2 * count_y * count_z
    width = partial_ref.shape[-1]

    @pl.when(step == 0)
    def _():
        for f in range(fields):
            low_ref[f] = state_ref[:, :, f].reshape(rows, -1).astype(jnp.bfloat16)
        lanes = lane_index((3 * count_y, 3 * count_y * LANES))
        row = lax.broadcasted_iota(jnp.int32, lanes.shape, 0)
        pick = (lanes // LANES == row).astype(jnp.float32)
        medium = spread(material_ref[...].reshape(3 * count_y, count_z), 3 * count_y, pick)
        lanes = lane_index((6 * count_y, 3 * count_y * LANES))
        row = lax.broadcasted_iota(jnp.int32, lanes.shape, 0)
        block = lanes // LANES
        face = 2 * (block // count_y) + (lanes % LANES) // FACE
        pick = (face * count_y + block % count_y == row).astype(jnp.float32)
        codes = spread(
            orient_ref[...].reshape(6 * count_y, count_z).astype(jnp.float32), 6 * count_y, pick
        )
        kinds = spread(
            flags_ref[...].reshape(6 * count_y, count_z).astype(jnp.float32), 6 * count_y, pick
        )
        lane = lane_index((count_z, LANES))
        upper = lane >= FACE
        half_sign = jnp.where(upper, 0.5, -0.5)
        node = lane % FACE
        near, far = (node // NP, node % NP)
        z_pos = lax.broadcasted_iota(jnp.int32, lane.shape, 0)
        for y in range(count_y):
            lam = medium[:, y * LANES : (y + 1) * LANES]
            mu = medium[:, (count_y + y) * LANES : (count_y + y + 1) * LANES]
            rho = medium[:, (2 * count_y + y) * LANES : (2 * count_y + y + 1) * LANES]
            inv = 1.0 / rho
            wide_ref[0, y] = lam
            wide_ref[1, y] = mu
            wide_ref[2, y] = inv
            coef_ref[0, y] = half_sign * lam
            coef_ref[1, y] = half_sign * mu
            coef_ref[2, y] = half_sign * inv
            coef_ref[3, y] = 0.5 * jnp.sqrt((lam + 2.0 * mu) * inv)
            for d in range(3):
                at = (d * count_y + y) * LANES
                code = jnp.round(codes[:, at : at + LANES]).astype(jnp.int32)
                swap = code >= 4
                lead = jnp.where(swap, far, near)
                trail = jnp.where(swap, near, far)
                lead = jnp.where(code % 2 == 1, NP - 1 - lead, lead)
                trail = jnp.where((code // 2) % 2 == 1, NP - 1 - trail, trail)
                source_ref[d, y] = lead * NP + trail + jnp.where(upper, 0, FACE)
                if d > 0:
                    free = jnp.where(jnp.round(kinds[:, at : at + LANES]) == 1.0, 1.0, 0.0)
                    if d == 1:
                        low_end = (ends_ref[0] == 1) if y == 0 else False
                        high_end = (ends_ref[1] == 1) if y == count_y - 1 else False
                        rim = jnp.where(
                            upper,
                            jnp.where(high_end, 1.0, 0.0),
                            jnp.where(low_end, 1.0, 0.0),
                        )
                    else:
                        low_rim = jnp.where(z_pos == 0, jnp.where(ends_ref[2] == 1, 1.0, 0.0), 0.0)
                        high_rim = jnp.where(
                            z_pos == count_z - 1, jnp.where(ends_ref[3] == 1, 1.0, 0.0), 0.0
                        )
                        rim = jnp.where(upper, high_rim, low_rim)
                    edge_ref[d - 1, 0, y] = rim
                    edge_ref[d - 1, 1, y] = free

    derivs = (d0_ref, d1_ref, d2_ref)
    velocity = jnp.concatenate([low_ref[i] for i in range(3)], axis=0)
    for d in range(3):
        grad_ref[d] = jnp.dot(
            velocity, derivs[d][...], preferred_element_type=jnp.float32
        )
    total = None
    for d in range(3):
        stress = jnp.concatenate([low_ref[stress_slot[i][d]] for i in range(3)], axis=0)
        part = jnp.dot(stress, derivs[d][...], preferred_element_type=jnp.float32)
        total = part if total is None else total + part
    div_ref[...] = total
    base = pl.multiple_of(step * width, LANES)
    for s in range(2):
        scale = step_size if s == 0 else -step_size
        for y in range(count_y):
            at = (s * count_y + y) * count_z
            for tile in range(width // LANES):
                columns = slice(tile * LANES, (tile + 1) * LANES)
                lam = scale * wide_ref[0, y]
                mu = scale * wide_ref[1, y]
                inv = scale * wide_ref[2, y]

                def g(d, i):
                    return grad_ref[d, i * rows + at : i * rows + at + count_z, columns]

                def put(f, term):
                    old = state_ref[s, y, f, :, pl.ds(base + tile * LANES, LANES)]
                    partial_ref[s, y, f, :, columns] = old + term

                for i in range(3):
                    put(i, inv * div_ref[i * rows + at : i * rows + at + count_z, columns])
                diag = [g(i, i) for i in range(3)]
                common = lam * (diag[0] + diag[1] + diag[2])
                for i in range(3):
                    put(3 + i, common + (mu + mu) * diag[i])
                for f, i, j in shear_pairs:
                    put(f, mu * (g(j, i) + g(i, j)))


def volume(ends, state, deriv, material, orient, flags):
    _, count_y, fields, count_z, nodes = state.shape
    f32 = jnp.float32
    width = 256
    parts = nodes // width
    rows = 2 * count_y * count_z
    whole = lambda shape: pl.BlockSpec(shape, lambda n, e: (0,) * len(shape))
    deriv_spec = lambda d: pl.BlockSpec((nodes, width), lambda n, e: (0, d * parts + n))
    outs = (
        jax.ShapeDtypeStruct(state.shape, f32),
        jax.ShapeDtypeStruct((4, count_y, count_z, LANES), f32),
        jax.ShapeDtypeStruct((3, count_y, count_z, LANES), jnp.int32),
        jax.ShapeDtypeStruct((2, 2, count_y, count_z, LANES), f32),
    )
    return pl.pallas_call(
        volume_kernel,
        out_shape=outs,
        grid_spec=pltpu.PrefetchScalarGridSpec(
            num_scalar_prefetch=1,
            grid=(parts,),
            in_specs=[
                whole(state.shape),
                deriv_spec(0),
                deriv_spec(1),
                deriv_spec(2),
                whole(material.shape),
                whole(orient.shape),
                whole(flags.shape),
            ],
            out_specs=(
                pl.BlockSpec(
                    (2, count_y, fields, count_z, width), lambda n, e: (0, 0, 0, 0, n)
                ),
                whole(outs[1].shape),
                whole(outs[2].shape),
                whole(outs[3].shape),
            ),
            scratch_shapes=[
                pltpu.VMEM((fields, rows, nodes), jnp.bfloat16),
                pltpu.VMEM((3, 3 * rows, width), f32),
                pltpu.VMEM((3 * rows, width), f32),
                pltpu.VMEM((3, count_y, count_z, LANES), f32),
            ],
        ),
        compiler_params=pltpu.CompilerParams(vmem_limit_bytes=LIMIT),
        cost_estimate=pl.CostEstimate(
            flops=12 * 10**8 * 3, bytes_accessed=8 * 10**6, transcendentals=0
        ),
        name="volume",
    )(ends, state, deriv, deriv, deriv, material, orient, flags)


def final_kernel(
    parity_ref, low_x_ref, high_x_ref, trace_ref, far_ref, near_ref, y_two, y_one, z_two, z_one,
    coef_ref, source_ref, edge_ref, partial_ref, stored_ref, lift_ref,
    advanced_ref, kernel_ref,
    flux_ref, sum_ref,
):
    y = pl.program_id(0)
    last_y = pl.num_programs(0) - 1
    fields, count_z = (partial_ref.shape[2], partial_ref.shape[3])
    odd_x = parity_ref[0] == 1
    odd_y = parity_ref[1] == 1
    odd_z = parity_ref[2] == 1
    lane = lane_index((count_z, LANES))
    upper = lane >= FACE
    z_pos = lax.broadcasted_iota(jnp.int32, lane.shape, 0)
    lam, mu, inv, speed = [coef_ref[k, 0] for k in range(4)]
    below = jnp.maximum(y - 1, 0)
    above = jnp.minimum(y + 1, last_y)
    take_near = upper == odd_x
    for s in range(2):
        for d in range(3):
            source = source_ref[d, 0]
            if d == 0 and s == 1:
                source = (source + FACE) % LANES
            if d > 0:
                rim = edge_ref[d - 1, 0, 0] > 0.0
                free = edge_ref[d - 1, 1, 0]
                keep_velocity = free - 1.0
                keep_stress = -free - 1.0
            jumps = []
            for f in range(fields):
                if d == 0:
                    inside = jnp.where(upper, high_x_ref[s, 0, f], low_x_ref[s, 0, f])
                    near, far = (near_ref[0, f], far_ref[0, f])
                    mixed = jnp.where(take_near, near, far) if s == 0 else jnp.where(take_near, far, near)
                elif d == 1:
                    inside = trace_ref[s, y, f, :, :LANES]
                    two, one = (y_two[f], y_one[f])
                    from_below = jnp.where(odd_y, one, two)
                    from_above = jnp.where(odd_y, two, one)
                    if s == 1:
                        from_below = pltpu.roll(from_below, FACE, 1)
                        from_above = pltpu.roll(from_above, FACE, 1)
                    lower = jnp.where(y == 0, from_below, trace_ref[s, below, f, :, :LANES])
                    higher = jnp.where(y == last_y, from_above, trace_ref[s, above, f, :, :LANES])
                    mixed = jnp.where(upper, lower, higher)
                else:
                    inside = trace_ref[s, y, f, :, LANES:]
                    two = jnp.broadcast_to(z_two[0, f : f + 1, :], lane.shape)
                    one = jnp.broadcast_to(z_one[0, f : f + 1, :], lane.shape)
                    from_below = jnp.where(odd_z, one, two)
                    from_above = jnp.where(odd_z, two, one)
                    if s == 1:
                        from_below = pltpu.roll(from_below, FACE, 1)
                        from_above = pltpu.roll(from_above, FACE, 1)
                    lower = jnp.where(z_pos == 0, from_below, pltpu.roll(inside, 1, 0))
                    higher = jnp.where(
                        z_pos == count_z - 1, from_above, pltpu.roll(inside, count_z - 1, 0)
                    )
                    mixed = jnp.where(upper, lower, higher)
                turned = jnp.take_along_axis(mixed, source, axis=1)
                jump = turned - inside
                if d > 0:
                    keep = keep_velocity if f < 3 else keep_stress
                    jump = jnp.where(rim, inside * keep, jump)
                jumps.append(jump)
                if s == 1:
                    term = stored_ref[0, f, :, d * LANES : (d + 1) * LANES] * jump
                    if d == 0:
                        sum_ref[f] = term
                    else:
                        sum_ref[f] += term
            flux = [speed * jump for jump in jumps]
            for i in range(3):
                flux[i] = flux[i] + inv * jumps[stress_slot[i][d]]
            common = lam * jumps[d]
            for i in range(3):
                flux[3 + i] = flux[3 + i] + common
            for i, j, f in ((0, 0, 3), (1, 1, 4), (2, 2, 5), (1, 2, 6), (0, 2, 7), (0, 1, 8)):
                if j == d:
                    flux[f] = flux[f] + mu * jumps[i]
                if i == d:
                    flux[f] = flux[f] + mu * jumps[j]
            for f in range(fields):
                flux_ref[s, f, :, d * LANES : (d + 1) * LANES] = flux[f].astype(jnp.bfloat16)
        lifted = jnp.dot(
            flux_ref[s].reshape(fields * count_z, 3 * LANES),
            lift_ref[...],
            preferred_element_type=jnp.float32,
        ).reshape(fields, count_z, -1)
        scale = step_size if s == 0 else -step_size
        advanced_ref[s, 0] = partial_ref[s, 0] + scale * lifted
    row = lax.broadcasted_iota(jnp.int32, (8, LANES), 0)
    ones = jnp.where(row == y, 1.0 / FACE, 0.0)
    for f in range(fields):
        sums = lax.dot_general(
            ones,
            sum_ref[f],
            (((1,), (1,)), ((), ())),
            precision=lax.Precision.HIGHEST,
            preferred_element_type=jnp.float32,
        )[: kernel_ref.shape[1]]

        @pl.when(y == 0)
        def _():
            kernel_ref[f] = sums

        @pl.when(y > 0)
        def _():
            kernel_ref[f] += sums


def finish(
    parity, state, traces, far, near, y_two, y_one, z_two, z_one, coef, source, edge, part, stored, lift
):
    _, count_y, fields, count_z, nodes = state.shape
    tiles = nodes // LANES
    f32 = jnp.float32
    whole = lambda a: pl.BlockSpec(a.shape, lambda y, p: (0,) * a.ndim)
    outs = (
        jax.ShapeDtypeStruct(state.shape, f32),
        jax.ShapeDtypeStruct((fields, count_y, count_z), f32),
    )
    by_y = lambda lead, rest: pl.BlockSpec(
        lead + (1,) + rest, lambda y, p: (0,) * len(lead) + (y,) + (0,) * len(rest)
    )
    return pl.pallas_call(
        final_kernel,
        out_shape=outs,
        grid_spec=pltpu.PrefetchScalarGridSpec(
            num_scalar_prefetch=1,
            grid=(count_y,),
            in_specs=[
                pl.BlockSpec((2, 1, fields, count_z, LANES), lambda y, p: (0, y, 0, 0, 0)),
                pl.BlockSpec((2, 1, fields, count_z, LANES), lambda y, p: (0, y, 0, 0, tiles - 1)),
                whole(traces),
                by_y((), (fields, count_z, LANES)),
                by_y((), (fields, count_z, LANES)),
                whole(y_two),
                whole(y_one),
                by_y((), (fields, LANES)),
                by_y((), (fields, LANES)),
                by_y((4,), (count_z, LANES)),
                by_y((3,), (count_z, LANES)),
                by_y((2, 2), (count_z, LANES)),
                by_y((2,), (fields, count_z, nodes)),
                by_y((), (fields, count_z, 3 * LANES)),
                whole(lift),
            ],
            out_specs=(
                by_y((2,), (fields, count_z, nodes)),
                pl.BlockSpec(outs[1].shape, lambda y, p: (0, 0, 0)),
            ),
            scratch_shapes=[
                pltpu.VMEM((2, fields, count_z, 3 * LANES), jnp.bfloat16),
                pltpu.VMEM((fields, count_z, LANES), f32),
            ],
        ),
        compiler_params=pltpu.CompilerParams(vmem_limit_bytes=LIMIT),
        cost_estimate=pl.CostEstimate(flops=9 * 10**8, bytes_accessed=10**7, transcendentals=0),
        name="finish",
    )(parity, state, state, traces, far, near, y_two, y_one, z_two, z_one, coef, source, edge, part, stored, lift)


def swaps(count, start, wrap):
    pairs = []
    for i in range(start, count if wrap else count - 1, 2):
        j = (i + 1) % count
        pairs += [(i, j), (j, i)]
    return pairs


def local(state, deriv, lift, material, stored, orient, flags):
    view = jnp.transpose(state[:, 0], (0, 1, 3, 2, 4))
    stored_view = jnp.transpose(stored[0], (0, 2, 1, 3))
    orient_view = jnp.transpose(orient[0], (2, 0, 1))
    flags_view = jnp.transpose(flags[0], (2, 0, 1))
    ix, iy, iz = (lax.axis_index(a) for a in ("gx", "gy", "gz"))
    nx, ny, nz = (lax.axis_size(a) for a in ("gx", "gy", "gz"))
    parity = jnp.stack([ix % 2, iy % 2, iz % 2]).astype(jnp.int32)
    ends = jnp.stack([iy == 0, iy == ny - 1, iz == 0, iz == nz - 1]).astype(jnp.int32)
    far, near = pack_faces(parity, view)
    far_in = lax.ppermute(far, "gx", swaps(nx, 1, True))
    near_in = lax.ppermute(near, "gx", swaps(nx, 0, True))
    table = jnp.asarray(trace_table(), jnp.bfloat16)
    traces, y_two, y_one, z_two, z_one = extract_traces(parity, view, table)
    y_two = lax.ppermute(y_two, "gy", swaps(ny, 1, False))
    y_one = lax.ppermute(y_one, "gy", swaps(ny, 0, False))
    z_two = lax.ppermute(z_two, "gz", swaps(nz, 1, False))
    z_one = lax.ppermute(z_one, "gz", swaps(nz, 0, False))
    part, coef, source, edge = volume(ends, view, deriv, material[:, 0], orient_view, flags_view)
    advanced, kernel = finish(
        parity, view, traces, far_in, near_in, y_two, y_one, z_two, z_one, coef, source, edge, part,
        stored_view, lift,
    )
    return (
        jnp.transpose(advanced, (0, 1, 3, 2, 4))[:, None],
        jnp.transpose(kernel, (1, 2, 0))[None],
    )


def solution(mesh):
    placed = (
        P(None, "gx", "gy", "gz", None, None),
        P(),
        P(),
        P(None, "gx", "gy", "gz"),
        P("gx", "gy", "gz", None, None),
        P("gx", "gy", "gz", None),
        P("gx", "gy", "gz", None),
    )
    return jax.shard_map(
        local,
        mesh=mesh,
        in_specs=placed,
        out_specs=(P(None, "gx", "gy", "gz", None, None), P("gx", "gy", "gz", None)),
        check_vma=False,
    )
```

```python
import jax
import jax.numpy as jnp
import numpy as np
from functools import partial
from jax import lax
from jax.experimental import pallas as pl
from jax.experimental.pallas import tpu as pltpu
from jax.sharding import PartitionSpec as P

NP = 8
FACE = NP * NP
LANES = 128
step_size = 0.15
stress_slot = ((3, 8, 7), (8, 4, 6), (7, 6, 5))
shear_pairs = ((6, 1, 2), (7, 0, 2), (8, 0, 1))
LIMIT = 20 * 1024 * 1024


def trace_table():
    table = np.zeros((NP**3, 4 * FACE), np.float32)
    for first in range(NP):
        for second in range(NP):
            m = first * NP + second
            table[first * 64 + second, m] = 1.0
            table[first * 64 + 56 + second, FACE + m] = 1.0
            table[first * 64 + second * 8, 2 * FACE + m] = 1.0
            table[first * 64 + second * 8 + 7, 3 * FACE + m] = 1.0
    return table


def lane_index(shape):
    return lax.broadcasted_iota(jnp.int32, shape, len(shape) - 1)


def merged(forward, adjoint, upper):
    rows = forward.shape[:-1]
    flat = (-1, LANES)
    turned = pltpu.roll(adjoint.reshape(flat), FACE, 1)
    own = (lane_index(turned.shape) >= FACE) == upper
    return jnp.where(own, forward.reshape(flat), turned).reshape(rows + (LANES,))


def odd_position(axis):
    return lax.axis_index(axis) % 2 == 1


def pack_kernel(low_ref, high_ref, far_ref, near_ref):
    odd = odd_position("gx")
    for y in range(far_ref.shape[0]):
        low = merged(low_ref[0, y], low_ref[1, y], False)
        high = merged(high_ref[0, y], high_ref[1, y], True)
        far_ref[y] = jnp.where(odd, high, low)
        near_ref[y] = jnp.where(odd, low, high)


def pack_faces(state):
    _, count_y, fields, count_z, nodes = state.shape
    tiles = nodes // LANES
    part = count_y // 2
    block = (2, part, fields, count_z, LANES)
    message = jax.ShapeDtypeStruct((count_y, fields, count_z, LANES), jnp.float32)
    out_spec = pl.BlockSpec((part, fields, count_z, LANES), lambda y: (y, 0, 0, 0))
    return pl.pallas_call(
        pack_kernel,
        out_shape=(message, message),
        grid=(2,),
        in_specs=[
            pl.BlockSpec(block, lambda y: (0, y, 0, 0, 0)),
            pl.BlockSpec(block, lambda y: (0, y, 0, 0, tiles - 1)),
        ],
        out_specs=(out_spec, out_spec),
        compiler_params=pltpu.CompilerParams(vmem_limit_bytes=LIMIT),
        cost_estimate=pl.CostEstimate(flops=10**6, bytes_accessed=2 * 10**6, transcendentals=0),
        name="pack_faces",
    )(state, state)


def spread(columns, rows, pick):
    return lax.dot_general(
        columns,
        pick,
        (((0,), (0,)), ((), ())),
        precision=lax.Precision.HIGHEST,
        preferred_element_type=jnp.float32,
    )


def volume_kernel(
    state_ref, d0_ref, d1_ref, d2_ref, material_ref, orient_ref, flags_ref, table_ref,
    partial_ref, coef_ref, source_ref, edge_ref, trace_ref, y_two, y_one, z_two, z_one,
    low_ref, grad_ref, div_ref, wide_ref,
):
    step = pl.program_id(0)
    _, count_y, fields, count_z, _ = state_ref.shape
    rows = 2 * count_y * count_z
    width = partial_ref.shape[-1]
    ends = [
        lax.axis_index("gy") == 0,
        lax.axis_index("gy") == lax.axis_size("gy") - 1,
        lax.axis_index("gz") == 0,
        lax.axis_index("gz") == lax.axis_size("gz") - 1,
    ]

    values = state_ref[step].reshape(count_y * fields * count_z, -1)
    high = values.astype(jnp.bfloat16)
    low = (values - high.astype(jnp.float32)).astype(jnp.bfloat16)
    table = table_ref[...]
    picked = jnp.dot(high, table, preferred_element_type=jnp.float32)
    picked = picked + jnp.dot(low, table, preferred_element_type=jnp.float32)
    trace_ref[step] = picked.reshape(count_y, fields, count_z, 2 * LANES)

    @pl.when(step == 1)
    def _():
        odd_y = odd_position("gy")
        odd_z = odd_position("gz")
        end = count_y - 1
        down = merged(trace_ref[0, 0, :, :, :LANES], trace_ref[1, 0, :, :, :LANES], False)
        up = merged(trace_ref[0, end, :, :, :LANES], trace_ref[1, end, :, :, :LANES], True)
        y_two[...] = jnp.where(odd_y, up, down)
        y_one[...] = jnp.where(odd_y, down, up)
        for y in range(count_y):
            first = merged(trace_ref[0, y, :, 0, LANES:], trace_ref[1, y, :, 0, LANES:], False)
            last = merged(
                trace_ref[0, y, :, count_z - 1, LANES:], trace_ref[1, y, :, count_z - 1, LANES:], True
            )
            z_two[y] = jnp.where(odd_z, last, first)
            z_one[y] = jnp.where(odd_z, first, last)

    @pl.when(step == 0)
    def _():
        for f in range(fields):
            low_ref[f] = state_ref[:, :, f].reshape(rows, -1).astype(jnp.bfloat16)
        lanes = lane_index((3 * count_y, 3 * count_y * LANES))
        row = lax.broadcasted_iota(jnp.int32, lanes.shape, 0)
        pick = (lanes // LANES == row).astype(jnp.float32)
        medium = spread(material_ref[...].reshape(3 * count_y, count_z), 3 * count_y, pick)
        lanes = lane_index((6 * count_y, 3 * count_y * LANES))
        row = lax.broadcasted_iota(jnp.int32, lanes.shape, 0)
        block = lanes // LANES
        face = 2 * (block // count_y) + (lanes % LANES) // FACE
        pick = (face * count_y + block % count_y == row).astype(jnp.float32)
        codes = spread(
            orient_ref[...].reshape(6 * count_y, count_z).astype(jnp.float32), 6 * count_y, pick
        )
        kinds = spread(
            flags_ref[...].reshape(6 * count_y, count_z).astype(jnp.float32), 6 * count_y, pick
        )
        lane = lane_index((count_z, LANES))
        upper = lane >= FACE
        half_sign = jnp.where(upper, 0.5, -0.5)
        node = lane % FACE
        near, far = (node // NP, node % NP)
        z_pos = lax.broadcasted_iota(jnp.int32, lane.shape, 0)
        for y in range(count_y):
            lam = medium[:, y * LANES : (y + 1) * LANES]
            mu = medium[:, (count_y + y) * LANES : (count_y + y + 1) * LANES]
            rho = medium[:, (2 * count_y + y) * LANES : (2 * count_y + y + 1) * LANES]
            inv = 1.0 / rho
            wide_ref[0, y] = lam
            wide_ref[1, y] = mu
            wide_ref[2, y] = inv
            coef_ref[0, y] = half_sign * lam
            coef_ref[1, y] = half_sign * mu
            coef_ref[2, y] = half_sign * inv
            coef_ref[3, y] = 0.5 * jnp.sqrt((lam + 2.0 * mu) * inv)
            for d in range(3):
                at = (d * count_y + y) * LANES
                code = jnp.round(codes[:, at : at + LANES]).astype(jnp.int32)
                swap = code >= 4
                lead = jnp.where(swap, far, near)
                trail = jnp.where(swap, near, far)
                lead = jnp.where(code % 2 == 1, NP - 1 - lead, lead)
                trail = jnp.where((code // 2) % 2 == 1, NP - 1 - trail, trail)
                source_ref[d, y] = lead * NP + trail + jnp.where(upper, 0, FACE)
                if d > 0:
                    free = jnp.where(jnp.round(kinds[:, at : at + LANES]) == 1.0, 1.0, 0.0)
                    if d == 1:
                        low_end = (ends[0]) if y == 0 else False
                        high_end = (ends[1]) if y == count_y - 1 else False
                        rim = jnp.where(
                            upper,
                            jnp.where(high_end, 1.0, 0.0),
                            jnp.where(low_end, 1.0, 0.0),
                        )
                    else:
                        low_rim = jnp.where(z_pos == 0, jnp.where(ends[2], 1.0, 0.0), 0.0)
                        high_rim = jnp.where(
                            z_pos == count_z - 1, jnp.where(ends[3], 1.0, 0.0), 0.0
                        )
                        rim = jnp.where(upper, high_rim, low_rim)
                    edge_ref[d - 1, 0, y] = rim
                    edge_ref[d - 1, 1, y] = free

    derivs = (d0_ref, d1_ref, d2_ref)
    velocity = jnp.concatenate([low_ref[i] for i in range(3)], axis=0)
    for d in range(3):
        grad_ref[d] = jnp.dot(
            velocity, derivs[d][...], preferred_element_type=jnp.float32
        )
    total = None
    for d in range(3):
        stress = jnp.concatenate([low_ref[stress_slot[i][d]] for i in range(3)], axis=0)
        part = jnp.dot(stress, derivs[d][...], preferred_element_type=jnp.float32)
        total = part if total is None else total + part
    div_ref[...] = total
    base = pl.multiple_of(step * width, LANES)
    for s in range(2):
        scale = step_size if s == 0 else -step_size
        for y in range(count_y):
            at = (s * count_y + y) * count_z
            for tile in range(width // LANES):
                columns = slice(tile * LANES, (tile + 1) * LANES)
                lam = scale * wide_ref[0, y]
                mu = scale * wide_ref[1, y]
                inv = scale * wide_ref[2, y]

                def g(d, i):
                    return grad_ref[d, i * rows + at : i * rows + at + count_z, columns]

                def put(f, term):
                    old = state_ref[s, y, f, :, pl.ds(base + tile * LANES, LANES)]
                    partial_ref[s, y, f, :, columns] = old + term

                for i in range(3):
                    put(i, inv * div_ref[i * rows + at : i * rows + at + count_z, columns])
                diag = [g(i, i) for i in range(3)]
                common = lam * (diag[0] + diag[1] + diag[2])
                for i in range(3):
                    put(3 + i, common + (mu + mu) * diag[i])
                for f, i, j in shear_pairs:
                    put(f, mu * (g(j, i) + g(i, j)))


def volume(state, deriv, material, orient, flags, table):
    _, count_y, fields, count_z, nodes = state.shape
    f32 = jnp.float32
    parts = 2
    width = nodes // parts
    rows = 2 * count_y * count_z
    whole = lambda shape: pl.BlockSpec(shape, lambda n: (0,) * len(shape))
    deriv_spec = lambda d: pl.BlockSpec((nodes, width), lambda n: (0, d * parts + n))
    y_message = jax.ShapeDtypeStruct((fields, count_z, LANES), f32)
    z_message = jax.ShapeDtypeStruct((count_y, fields, LANES), f32)
    outs = (
        jax.ShapeDtypeStruct(state.shape, f32),
        jax.ShapeDtypeStruct((4, count_y, count_z, LANES), f32),
        jax.ShapeDtypeStruct((3, count_y, count_z, LANES), jnp.int32),
        jax.ShapeDtypeStruct((2, 2, count_y, count_z, LANES), f32),
        jax.ShapeDtypeStruct((2, count_y, fields, count_z, 2 * LANES), f32),
        y_message,
        y_message,
        z_message,
        z_message,
    )
    return pl.pallas_call(
        volume_kernel,
        out_shape=outs,
        grid=(parts,),
        in_specs=[
            whole(state.shape),
            deriv_spec(0),
            deriv_spec(1),
            deriv_spec(2),
            whole(material.shape),
            whole(orient.shape),
            whole(flags.shape),
            whole(table.shape),
        ],
        out_specs=(
            pl.BlockSpec((2, count_y, fields, count_z, width), lambda n: (0, 0, 0, 0, n)),
        )
        + tuple(whole(out.shape) for out in outs[1:]),
        scratch_shapes=[
            pltpu.VMEM((fields, rows, nodes), jnp.bfloat16),
            pltpu.VMEM((3, 3 * rows, width), f32),
            pltpu.VMEM((3 * rows, width), f32),
            pltpu.VMEM((3, count_y, count_z, LANES), f32),
        ],
        compiler_params=pltpu.CompilerParams(vmem_limit_bytes=LIMIT),
        cost_estimate=pl.CostEstimate(
            flops=42 * 10**8, bytes_accessed=12 * 10**6, transcendentals=0
        ),
        name="volume",
    )(state, deriv, deriv, deriv, material, orient, flags, table)


def final_kernel(
    low_x_ref, high_x_ref, trace_ref, far_ref, near_ref, y_two, y_one, z_two, z_one,
    coef_ref, source_ref, edge_ref, partial_ref, stored_ref, lift_ref,
    advanced_ref, kernel_ref,
    flux_ref, sum_ref,
):
    y = pl.program_id(0)
    last_y = pl.num_programs(0) - 1
    fields, count_z = (partial_ref.shape[2], partial_ref.shape[3])
    odd_x = odd_position("gx")
    odd_y = odd_position("gy")
    odd_z = odd_position("gz")
    lane = lane_index((count_z, LANES))
    upper = lane >= FACE
    z_pos = lax.broadcasted_iota(jnp.int32, lane.shape, 0)
    lam, mu, inv, speed = [coef_ref[k, 0] for k in range(4)]
    below = jnp.maximum(y - 1, 0)
    above = jnp.minimum(y + 1, last_y)
    take_near = upper == odd_x
    for s in range(2):
        for d in range(3):
            source = source_ref[d, 0]
            if d == 0 and s == 1:
                source = (source + FACE) % LANES
            if d > 0:
                rim = edge_ref[d - 1, 0, 0] > 0.0
                free = edge_ref[d - 1, 1, 0]
                keep_velocity = free - 1.0
                keep_stress = -free - 1.0
            jumps = []
            for f in range(fields):
                if d == 0:
                    inside = jnp.where(upper, high_x_ref[s, 0, f], low_x_ref[s, 0, f])
                    near, far = (near_ref[0, f], far_ref[0, f])
                    mixed = jnp.where(take_near, near, far) if s == 0 else jnp.where(take_near, far, near)
                elif d == 1:
                    inside = trace_ref[s, y, f, :, :LANES]
                    two, one = (y_two[f], y_one[f])
                    from_below = jnp.where(odd_y, one, two)
                    from_above = jnp.where(odd_y, two, one)
                    if s == 1:
                        from_below = pltpu.roll(from_below, FACE, 1)
                        from_above = pltpu.roll(from_above, FACE, 1)
                    lower = jnp.where(y == 0, from_below, trace_ref[s, below, f, :, :LANES])
                    higher = jnp.where(y == last_y, from_above, trace_ref[s, above, f, :, :LANES])
                    mixed = jnp.where(upper, lower, higher)
                else:
                    inside = trace_ref[s, y, f, :, LANES:]
                    two = jnp.broadcast_to(z_two[0, f : f + 1, :], lane.shape)
                    one = jnp.broadcast_to(z_one[0, f : f + 1, :], lane.shape)
                    from_below = jnp.where(odd_z, one, two)
                    from_above = jnp.where(odd_z, two, one)
                    if s == 1:
                        from_below = pltpu.roll(from_below, FACE, 1)
                        from_above = pltpu.roll(from_above, FACE, 1)
                    lower = jnp.where(z_pos == 0, from_below, pltpu.roll(inside, 1, 0))
                    higher = jnp.where(
                        z_pos == count_z - 1, from_above, pltpu.roll(inside, count_z - 1, 0)
                    )
                    mixed = jnp.where(upper, lower, higher)
                turned = jnp.take_along_axis(mixed, source, axis=1)
                jump = turned - inside
                if d > 0:
                    keep = keep_velocity if f < 3 else keep_stress
                    jump = jnp.where(rim, inside * keep, jump)
                jumps.append(jump)
                if s == 1:
                    term = stored_ref[0, f, :, d * LANES : (d + 1) * LANES] * jump
                    if d == 0:
                        sum_ref[f] = term
                    else:
                        sum_ref[f] += term
            flux = [speed * jump for jump in jumps]
            for i in range(3):
                flux[i] = flux[i] + inv * jumps[stress_slot[i][d]]
            common = lam * jumps[d]
            for i in range(3):
                flux[3 + i] = flux[3 + i] + common
            for i, j, f in ((0, 0, 3), (1, 1, 4), (2, 2, 5), (1, 2, 6), (0, 2, 7), (0, 1, 8)):
                if j == d:
                    flux[f] = flux[f] + mu * jumps[i]
                if i == d:
                    flux[f] = flux[f] + mu * jumps[j]
            for f in range(fields):
                flux_ref[s, f, :, d * LANES : (d + 1) * LANES] = flux[f].astype(jnp.bfloat16)
        lifted = jnp.dot(
            flux_ref[s].reshape(fields * count_z, 3 * LANES),
            lift_ref[...],
            preferred_element_type=jnp.float32,
        ).reshape(fields, count_z, -1)
        scale = step_size if s == 0 else -step_size
        advanced_ref[s, 0] = partial_ref[s, 0] + scale * lifted
    for f in range(fields):
        sums = jnp.sum(sum_ref[f], axis=1, keepdims=True) * (1.0 / FACE)
        across = jnp.sum(jnp.where(z_pos == lane, sums, 0.0), axis=0, keepdims=True)
        kernel_ref[f, pl.ds(y, 1), :] = across[:, :count_z]


def finish(
    state, traces, far, near, y_two, y_one, z_two, z_one, coef, source, edge, part, stored, lift
):
    _, count_y, fields, count_z, nodes = state.shape
    tiles = nodes // LANES
    f32 = jnp.float32
    whole = lambda a: pl.BlockSpec(a.shape, lambda y: (0,) * a.ndim)
    outs = (
        jax.ShapeDtypeStruct(state.shape, f32),
        jax.ShapeDtypeStruct((fields, count_y, count_z), f32),
    )
    by_y = lambda lead, rest: pl.BlockSpec(
        lead + (1,) + rest, lambda y: (0,) * len(lead) + (y,) + (0,) * len(rest)
    )
    return pl.pallas_call(
        final_kernel,
        out_shape=outs,
        grid=(count_y,),
        in_specs=[
            pl.BlockSpec((2, 1, fields, count_z, LANES), lambda y: (0, y, 0, 0, 0)),
            pl.BlockSpec((2, 1, fields, count_z, LANES), lambda y: (0, y, 0, 0, tiles - 1)),
            whole(traces),
            by_y((), (fields, count_z, LANES)),
            by_y((), (fields, count_z, LANES)),
            whole(y_two),
            whole(y_one),
            by_y((), (fields, LANES)),
            by_y((), (fields, LANES)),
            by_y((4,), (count_z, LANES)),
            by_y((3,), (count_z, LANES)),
            by_y((2, 2), (count_z, LANES)),
            by_y((2,), (fields, count_z, nodes)),
            by_y((), (fields, count_z, 3 * LANES)),
            whole(lift),
        ],
        out_specs=(
            by_y((2,), (fields, count_z, nodes)),
            pl.BlockSpec(outs[1].shape, lambda y: (0, 0, 0)),
        ),
        scratch_shapes=[
            pltpu.VMEM((2, fields, count_z, 3 * LANES), jnp.bfloat16),
            pltpu.VMEM((fields, count_z, LANES), f32),
        ],
        compiler_params=pltpu.CompilerParams(vmem_limit_bytes=LIMIT),
        cost_estimate=pl.CostEstimate(flops=9 * 10**8, bytes_accessed=10**7, transcendentals=0),
        name="finish",
    )(state, state, traces, far, near, y_two, y_one, z_two, z_one, coef, source, edge, part, stored, lift)


def swaps(count, start, wrap):
    pairs = []
    for i in range(start, count if wrap else count - 1, 2):
        j = (i + 1) % count
        pairs += [(i, j), (j, i)]
    return pairs


def local(state, deriv, lift, material, stored, orient, flags):
    view = jnp.transpose(state[:, 0], (0, 1, 3, 2, 4))
    stored_view = jnp.transpose(stored[0], (0, 2, 1, 3))
    orient_view = jnp.transpose(orient[0], (2, 0, 1))
    flags_view = jnp.transpose(flags[0], (2, 0, 1))
    nx, ny, nz = (lax.axis_size(a) for a in ("gx", "gy", "gz"))
    far, near = pack_faces(view)
    far_in = lax.ppermute(far, "gx", swaps(nx, 1, True))
    near_in = lax.ppermute(near, "gx", swaps(nx, 0, True))
    table = jnp.asarray(trace_table(), jnp.bfloat16)
    part, coef, source, edge, traces, y_two, y_one, z_two, z_one = volume(
        view, deriv, material[:, 0], orient_view, flags_view, table
    )
    y_two = lax.ppermute(y_two, "gy", swaps(ny, 1, False))
    y_one = lax.ppermute(y_one, "gy", swaps(ny, 0, False))
    z_two = lax.ppermute(z_two, "gz", swaps(nz, 1, False))
    z_one = lax.ppermute(z_one, "gz", swaps(nz, 0, False))
    advanced, kernel = finish(
        view, traces, far_in, near_in, y_two, y_one, z_two, z_one, coef, source, edge, part,
        stored_view, lift,
    )
    return (
        jnp.transpose(advanced, (0, 1, 3, 2, 4))[:, None],
        jnp.transpose(kernel, (1, 2, 0))[None],
    )


def solution(mesh):
    placed = (
        P(None, "gx", "gy", "gz", None, None),
        P(),
        P(),
        P(None, "gx", "gy", "gz"),
        P("gx", "gy", "gz", None, None),
        P("gx", "gy", "gz", None),
        P("gx", "gy", "gz", None),
    )
    return jax.shard_map(
        local,
        mesh=mesh,
        in_specs=placed,
        out_specs=(P(None, "gx", "gy", "gz", None, None), P("gx", "gy", "gz", None)),
        check_vma=False,
    )
```

```python
import jax
import jax.numpy as jnp
import numpy as np
from functools import partial
from jax import lax
from jax.experimental import pallas as pl
from jax.experimental.pallas import tpu as pltpu
from jax.sharding import PartitionSpec as P

NP = 8
FACE = NP * NP
LANES = 128
step_size = 0.15
stress_slot = ((3, 8, 7), (8, 4, 6), (7, 6, 5))
shear_pairs = ((6, 1, 2), (7, 0, 2), (8, 0, 1))
LIMIT = 20 * 1024 * 1024


def trace_table():
    table = np.zeros((NP**3, 4 * FACE), np.float32)
    for first in range(NP):
        for second in range(NP):
            m = first * NP + second
            table[first * 64 + second, m] = 1.0
            table[first * 64 + 56 + second, FACE + m] = 1.0
            table[first * 64 + second * 8, 2 * FACE + m] = 1.0
            table[first * 64 + second * 8 + 7, 3 * FACE + m] = 1.0
    return table


def lane_index(shape):
    return lax.broadcasted_iota(jnp.int32, shape, len(shape) - 1)


def merged(forward, adjoint, upper):
    rows = forward.shape[:-1]
    flat = (-1, LANES)
    turned = pltpu.roll(adjoint.reshape(flat), FACE, 1)
    own = (lane_index(turned.shape) >= FACE) == upper
    return jnp.where(own, forward.reshape(flat), turned).reshape(rows + (LANES,))


def odd_position(axis):
    return lax.axis_index(axis) % 2 == 1


def pack_kernel(low_ref, high_ref, far_ref, near_ref):
    odd = odd_position("gx")
    for y in range(far_ref.shape[0]):
        low = merged(low_ref[0, y], low_ref[1, y], False)
        high = merged(high_ref[0, y], high_ref[1, y], True)
        far_ref[y] = jnp.where(odd, high, low)
        near_ref[y] = jnp.where(odd, low, high)


def pack_faces(state):
    _, count_y, fields, count_z, nodes = state.shape
    tiles = nodes // LANES
    part = count_y // 2
    block = (2, part, fields, count_z, LANES)
    message = jax.ShapeDtypeStruct((count_y, fields, count_z, LANES), jnp.float32)
    out_spec = pl.BlockSpec((part, fields, count_z, LANES), lambda y: (y, 0, 0, 0))
    return pl.pallas_call(
        pack_kernel,
        out_shape=(message, message),
        grid=(2,),
        in_specs=[
            pl.BlockSpec(block, lambda y: (0, y, 0, 0, 0)),
            pl.BlockSpec(block, lambda y: (0, y, 0, 0, tiles - 1)),
        ],
        out_specs=(out_spec, out_spec),
        compiler_params=pltpu.CompilerParams(vmem_limit_bytes=LIMIT),
        cost_estimate=pl.CostEstimate(flops=10**6, bytes_accessed=2 * 10**6, transcendentals=0),
        name="pack_faces",
    )(state, state)


def spread(columns, rows, pick):
    return lax.dot_general(
        columns,
        pick,
        (((0,), (0,)), ((), ())),
        precision=lax.Precision.HIGHEST,
        preferred_element_type=jnp.float32,
    )


def volume_kernel(
    state_ref, d0_ref, d1_ref, d2_ref, material_ref, orient_ref, flags_ref, table_ref,
    partial_ref, coef_ref, source_ref, edge_ref, trace_ref, y_two, y_one, z_two, z_one,
    low_ref, grad_ref, div_ref, wide_ref,
):
    step = pl.program_id(0)
    _, count_y, fields, count_z, _ = state_ref.shape
    rows = 2 * count_y * count_z
    width = partial_ref.shape[-1]
    ends = [
        lax.axis_index("gy") == 0,
        lax.axis_index("gy") == lax.axis_size("gy") - 1,
        lax.axis_index("gz") == 0,
        lax.axis_index("gz") == lax.axis_size("gz") - 1,
    ]

    values = state_ref[step].reshape(count_y * fields * count_z, -1)
    high = values.astype(jnp.bfloat16)
    low = (values - high.astype(jnp.float32)).astype(jnp.bfloat16)
    table = table_ref[...]
    picked = jnp.dot(high, table, preferred_element_type=jnp.float32)
    picked = picked + jnp.dot(low, table, preferred_element_type=jnp.float32)
    trace_ref[step] = picked.reshape(count_y, fields, count_z, 2 * LANES)

    @pl.when(step == 1)
    def _():
        odd_y = odd_position("gy")
        odd_z = odd_position("gz")
        end = count_y - 1
        down = merged(trace_ref[0, 0, :, :, :LANES], trace_ref[1, 0, :, :, :LANES], False)
        up = merged(trace_ref[0, end, :, :, :LANES], trace_ref[1, end, :, :, :LANES], True)
        y_two[...] = jnp.where(odd_y, up, down)
        y_one[...] = jnp.where(odd_y, down, up)
        for y in range(count_y):
            first = merged(trace_ref[0, y, :, 0, LANES:], trace_ref[1, y, :, 0, LANES:], False)
            last = merged(
                trace_ref[0, y, :, count_z - 1, LANES:], trace_ref[1, y, :, count_z - 1, LANES:], True
            )
            z_two[y] = jnp.where(odd_z, last, first)
            z_one[y] = jnp.where(odd_z, first, last)

    @pl.when(step == 0)
    def _():
        for f in range(fields):
            low_ref[f] = state_ref[:, :, f].reshape(rows, -1).astype(jnp.bfloat16)
        lanes = lane_index((3 * count_y, 3 * count_y * LANES))
        row = lax.broadcasted_iota(jnp.int32, lanes.shape, 0)
        pick = (lanes // LANES == row).astype(jnp.float32)
        medium = spread(material_ref[...].reshape(3 * count_y, count_z), 3 * count_y, pick)
        lanes = lane_index((6 * count_y, 3 * count_y * LANES))
        row = lax.broadcasted_iota(jnp.int32, lanes.shape, 0)
        block = lanes // LANES
        face = 2 * (block // count_y) + (lanes % LANES) // FACE
        pick = (face * count_y + block % count_y == row).astype(jnp.float32)
        codes = spread(
            orient_ref[...].reshape(6 * count_y, count_z).astype(jnp.float32), 6 * count_y, pick
        )
        kinds = spread(
            flags_ref[...].reshape(6 * count_y, count_z).astype(jnp.float32), 6 * count_y, pick
        )
        lane = lane_index((count_z, LANES))
        upper = lane >= FACE
        half_sign = jnp.where(upper, 0.5, -0.5)
        node = lane % FACE
        near, far = (node // NP, node % NP)
        z_pos = lax.broadcasted_iota(jnp.int32, lane.shape, 0)
        for y in range(count_y):
            lam = medium[:, y * LANES : (y + 1) * LANES]
            mu = medium[:, (count_y + y) * LANES : (count_y + y + 1) * LANES]
            rho = medium[:, (2 * count_y + y) * LANES : (2 * count_y + y + 1) * LANES]
            inv = 1.0 / rho
            wide_ref[0, y] = lam
            wide_ref[1, y] = mu
            wide_ref[2, y] = inv
            coef_ref[0, y] = half_sign * lam
            coef_ref[1, y] = half_sign * mu
            coef_ref[2, y] = half_sign * inv
            coef_ref[3, y] = 0.5 * jnp.sqrt((lam + 2.0 * mu) * inv)
            for d in range(3):
                at = (d * count_y + y) * LANES
                code = jnp.round(codes[:, at : at + LANES]).astype(jnp.int32)
                swap = code >= 4
                lead = jnp.where(swap, far, near)
                trail = jnp.where(swap, near, far)
                lead = jnp.where(code % 2 == 1, NP - 1 - lead, lead)
                trail = jnp.where((code // 2) % 2 == 1, NP - 1 - trail, trail)
                source_ref[d, y] = lead * NP + trail + jnp.where(upper, 0, FACE)
                if d > 0:
                    free = jnp.where(jnp.round(kinds[:, at : at + LANES]) == 1.0, 1.0, 0.0)
                    if d == 1:
                        low_end = (ends[0]) if y == 0 else False
                        high_end = (ends[1]) if y == count_y - 1 else False
                        rim = jnp.where(
                            upper,
                            jnp.where(high_end, 1.0, 0.0),
                            jnp.where(low_end, 1.0, 0.0),
                        )
                    else:
                        low_rim = jnp.where(z_pos == 0, jnp.where(ends[2], 1.0, 0.0), 0.0)
                        high_rim = jnp.where(
                            z_pos == count_z - 1, jnp.where(ends[3], 1.0, 0.0), 0.0
                        )
                        rim = jnp.where(upper, high_rim, low_rim)
                    edge_ref[d - 1, 0, y] = rim
                    edge_ref[d - 1, 1, y] = free

    derivs = (d0_ref, d1_ref, d2_ref)
    velocity = jnp.concatenate([low_ref[i] for i in range(3)], axis=0)
    for d in range(3):
        grad_ref[d] = jnp.dot(
            velocity, derivs[d][...], preferred_element_type=jnp.float32
        )
    total = None
    for d in range(3):
        stress = jnp.concatenate([low_ref[stress_slot[i][d]] for i in range(3)], axis=0)
        part = jnp.dot(stress, derivs[d][...], preferred_element_type=jnp.float32)
        total = part if total is None else total + part
    div_ref[...] = total
    base = pl.multiple_of(step * width, LANES)
    for s in range(2):
        scale = step_size if s == 0 else -step_size
        for y in range(count_y):
            at = (s * count_y + y) * count_z
            for tile in range(width // LANES):
                columns = slice(tile * LANES, (tile + 1) * LANES)
                lam = scale * wide_ref[0, y]
                mu = scale * wide_ref[1, y]
                inv = scale * wide_ref[2, y]

                def g(d, i):
                    return grad_ref[d, i * rows + at : i * rows + at + count_z, columns]

                def put(f, term):
                    old = state_ref[s, y, f, :, pl.ds(base + tile * LANES, LANES)]
                    partial_ref[s, y, f, :, columns] = old + term

                for i in range(3):
                    put(i, inv * div_ref[i * rows + at : i * rows + at + count_z, columns])
                diag = [g(i, i) for i in range(3)]
                common = lam * (diag[0] + diag[1] + diag[2])
                for i in range(3):
                    put(3 + i, common + (mu + mu) * diag[i])
                for f, i, j in shear_pairs:
                    put(f, mu * (g(j, i) + g(i, j)))


def volume(state, deriv, material, orient, flags, table):
    _, count_y, fields, count_z, nodes = state.shape
    f32 = jnp.float32
    parts = 2
    width = nodes // parts
    rows = 2 * count_y * count_z
    whole = lambda shape: pl.BlockSpec(shape, lambda n: (0,) * len(shape))
    deriv_spec = lambda d: pl.BlockSpec((nodes, width), lambda n: (0, d * parts + n))
    y_message = jax.ShapeDtypeStruct((fields, count_z, LANES), f32)
    z_message = jax.ShapeDtypeStruct((count_y, fields, LANES), f32)
    outs = (
        jax.ShapeDtypeStruct(state.shape, f32),
        jax.ShapeDtypeStruct((4, count_y, count_z, LANES), f32),
        jax.ShapeDtypeStruct((3, count_y, count_z, LANES), jnp.int32),
        jax.ShapeDtypeStruct((2, 2, count_y, count_z, LANES), f32),
        jax.ShapeDtypeStruct((2, count_y, fields, count_z, 2 * LANES), f32),
        y_message,
        y_message,
        z_message,
        z_message,
    )
    return pl.pallas_call(
        volume_kernel,
        out_shape=outs,
        grid=(parts,),
        in_specs=[
            whole(state.shape),
            deriv_spec(0),
            deriv_spec(1),
            deriv_spec(2),
            whole(material.shape),
            whole(orient.shape),
            whole(flags.shape),
            whole(table.shape),
        ],
        out_specs=(
            pl.BlockSpec((2, count_y, fields, count_z, width), lambda n: (0, 0, 0, 0, n)),
        )
        + tuple(whole(out.shape) for out in outs[1:]),
        scratch_shapes=[
            pltpu.VMEM((fields, rows, nodes), jnp.bfloat16),
            pltpu.VMEM((3, 3 * rows, width), f32),
            pltpu.VMEM((3 * rows, width), f32),
            pltpu.VMEM((3, count_y, count_z, LANES), f32),
        ],
        compiler_params=pltpu.CompilerParams(vmem_limit_bytes=LIMIT),
        cost_estimate=pl.CostEstimate(
            flops=42 * 10**8, bytes_accessed=12 * 10**6, transcendentals=0
        ),
        name="volume",
    )(state, deriv, deriv, deriv, material, orient, flags, table)


def final_kernel(
    state_ref, trace_ref, far_ref, near_ref, y_two, y_one, z_two, z_one,
    coef_ref, source_ref, edge_ref, partial_ref, stored_ref, lift_ref,
    advanced_ref, kernel_ref,
    flux_ref, sum_ref, out_ref, out_sem,
):
    count_y, fields, count_z, nodes = state_ref.shape[1:]
    last_y = count_y - 1
    odd_x = odd_position("gx")
    odd_y = odd_position("gy")
    odd_z = odd_position("gz")
    lane = lane_index((count_z, LANES))
    upper = lane >= FACE
    z_pos = lax.broadcasted_iota(jnp.int32, lane.shape, 0)
    take_near = upper == odd_x

    def write(y):
        return pltpu.make_async_copy(out_ref.at[:, y], advanced_ref.at[:, y], out_sem.at[y])

    def row(y, carry):
        below = jnp.maximum(y - 1, 0)
        above = jnp.minimum(y + 1, last_y)
        lam, mu, inv, speed = [coef_ref[k, y] for k in range(4)]
        for s in range(2):
            for d in range(3):
                source = source_ref[d, y]
                if d == 0 and s == 1:
                    source = (source + FACE) % LANES
                if d > 0:
                    rim = edge_ref[d - 1, 0, y] > 0.0
                    free = edge_ref[d - 1, 1, y]
                    keep_velocity = free - 1.0
                    keep_stress = -free - 1.0
                jumps = []
                for f in range(fields):
                    if d == 0:
                        inside = jnp.where(
                            upper, state_ref[s, y, f, :, nodes - LANES :], state_ref[s, y, f, :, :LANES]
                        )
                        near, far = (near_ref[y, f], far_ref[y, f])
                        if s == 1:
                            near, far = (far, near)
                        mixed = jnp.where(take_near, near, far)
                    elif d == 1:
                        inside = trace_ref[s, y, f, :, :LANES]
                        two, one = (y_two[f], y_one[f])
                        from_below = jnp.where(odd_y, one, two)
                        from_above = jnp.where(odd_y, two, one)
                        if s == 1:
                            from_below = pltpu.roll(from_below, FACE, 1)
                            from_above = pltpu.roll(from_above, FACE, 1)
                        lower = jnp.where(y == 0, from_below, trace_ref[s, below, f, :, :LANES])
                        higher = jnp.where(y == last_y, from_above, trace_ref[s, above, f, :, :LANES])
                        mixed = jnp.where(upper, lower, higher)
                    else:
                        inside = trace_ref[s, y, f, :, LANES:]
                        two = jnp.broadcast_to(z_two[y, f : f + 1, :], lane.shape)
                        one = jnp.broadcast_to(z_one[y, f : f + 1, :], lane.shape)
                        from_below = jnp.where(odd_z, one, two)
                        from_above = jnp.where(odd_z, two, one)
                        if s == 1:
                            from_below = pltpu.roll(from_below, FACE, 1)
                            from_above = pltpu.roll(from_above, FACE, 1)
                        lower = jnp.where(z_pos == 0, from_below, pltpu.roll(inside, 1, 0))
                        higher = jnp.where(
                            z_pos == count_z - 1, from_above, pltpu.roll(inside, count_z - 1, 0)
                        )
                        mixed = jnp.where(upper, lower, higher)
                    turned = jnp.take_along_axis(mixed, source, axis=1)
                    jump = turned - inside
                    if d > 0:
                        keep = keep_velocity if f < 3 else keep_stress
                        jump = jnp.where(rim, inside * keep, jump)
                    jumps.append(jump)
                    if s == 1:
                        term = stored_ref[y, f, :, d * LANES : (d + 1) * LANES] * jump
                        if d == 0:
                            sum_ref[f] = term
                        else:
                            sum_ref[f] += term
                flux = [speed * jump for jump in jumps]
                for i in range(3):
                    flux[i] = flux[i] + inv * jumps[stress_slot[i][d]]
                common = lam * jumps[d]
                for i in range(3):
                    flux[3 + i] = flux[3 + i] + common
                for i, j, f in ((0, 0, 3), (1, 1, 4), (2, 2, 5), (1, 2, 6), (0, 2, 7), (0, 1, 8)):
                    if j == d:
                        flux[f] = flux[f] + mu * jumps[i]
                    if i == d:
                        flux[f] = flux[f] + mu * jumps[j]
                for f in range(fields):
                    flux_ref[s, f, :, d * LANES : (d + 1) * LANES] = flux[f].astype(jnp.bfloat16)
        lifted = jnp.dot(
            flux_ref[...].reshape(2 * fields * count_z, 3 * LANES),
            lift_ref[...],
            preferred_element_type=jnp.float32,
        ).reshape(2, fields, count_z, nodes)
        for s in range(2):
            scale = step_size if s == 0 else -step_size
            out_ref[s, y] = partial_ref[s, y] + scale * lifted[s]
        write(y).start()
        for f in range(fields):
            sums = jnp.sum(sum_ref[f], axis=1, keepdims=True) * (1.0 / FACE)
            across = jnp.sum(jnp.where(z_pos == lane, sums, 0.0), axis=0, keepdims=True)
            kernel_ref[f, pl.ds(y, 1), :] = across[:, :count_z]
        return carry

    lax.fori_loop(0, count_y, row, 0)
    for y in range(count_y):
        write(y).wait()


def finish(
    state, traces, far, near, y_two, y_one, z_two, z_one, coef, source, edge, part, stored, lift
):
    _, count_y, fields, count_z, nodes = state.shape
    f32 = jnp.float32
    outs = (
        jax.ShapeDtypeStruct(state.shape, f32),
        jax.ShapeDtypeStruct((fields, count_y, count_z), f32),
    )
    return pl.pallas_call(
        final_kernel,
        out_shape=outs,
        in_specs=[pl.BlockSpec(memory_space=pltpu.VMEM)] * 14,
        out_specs=(pl.BlockSpec(memory_space=pl.ANY), pl.BlockSpec(memory_space=pltpu.VMEM)),
        scratch_shapes=[
            pltpu.VMEM((2, fields, count_z, 3 * LANES), jnp.bfloat16),
            pltpu.VMEM((fields, count_z, LANES), f32),
            pltpu.VMEM(state.shape, f32),
            pltpu.SemaphoreType.DMA((count_y,)),
        ],
        compiler_params=pltpu.CompilerParams(vmem_limit_bytes=LIMIT),
        cost_estimate=pl.CostEstimate(flops=9 * 10**8, bytes_accessed=10**7, transcendentals=0),
        name="finish",
    )(state, traces, far, near, y_two, y_one, z_two, z_one, coef, source, edge, part, stored, lift)


def swaps(count, start, wrap):
    pairs = []
    for i in range(start, count if wrap else count - 1, 2):
        j = (i + 1) % count
        pairs += [(i, j), (j, i)]
    return pairs


def local(state, deriv, lift, material, stored, orient, flags):
    view = jnp.transpose(state[:, 0], (0, 1, 3, 2, 4))
    stored_view = jnp.transpose(stored[0], (0, 2, 1, 3))
    orient_view = jnp.transpose(orient[0], (2, 0, 1))
    flags_view = jnp.transpose(flags[0], (2, 0, 1))
    nx, ny, nz = (lax.axis_size(a) for a in ("gx", "gy", "gz"))
    far, near = pack_faces(view)
    far_in = lax.ppermute(far, "gx", swaps(nx, 1, True))
    near_in = lax.ppermute(near, "gx", swaps(nx, 0, True))
    table = jnp.asarray(trace_table(), jnp.bfloat16)
    part, coef, source, edge, traces, y_two, y_one, z_two, z_one = volume(
        view, deriv, material[:, 0], orient_view, flags_view, table
    )
    y_two = lax.ppermute(y_two, "gy", swaps(ny, 1, False))
    y_one = lax.ppermute(y_one, "gy", swaps(ny, 0, False))
    z_two = lax.ppermute(z_two, "gz", swaps(nz, 1, False))
    z_one, y_one = lax.optimization_barrier((z_one, y_one))
    z_one = lax.ppermute(z_one, "gz", swaps(nz, 0, False))
    advanced, kernel = finish(
        view, traces, far_in, near_in, y_two, y_one, z_two, z_one, coef, source, edge, part,
        stored_view, lift,
    )
    return (
        jnp.transpose(advanced, (0, 1, 3, 2, 4))[:, None],
        jnp.transpose(kernel, (1, 2, 0))[None],
    )


def solution(mesh):
    placed = (
        P(None, "gx", "gy", "gz", None, None),
        P(),
        P(),
        P(None, "gx", "gy", "gz"),
        P("gx", "gy", "gz", None, None),
        P("gx", "gy", "gz", None),
        P("gx", "gy", "gz", None),
    )
    return jax.shard_map(
        local,
        mesh=mesh,
        in_specs=placed,
        out_specs=(P(None, "gx", "gy", "gz", None, None), P("gx", "gy", "gz", None)),
        check_vma=False,
    )
```

```python
import jax
import jax.numpy as jnp
import numpy as np
from functools import partial
from jax import lax
from jax.experimental import pallas as pl
from jax.experimental.pallas import tpu as pltpu
from jax.sharding import PartitionSpec as P

NP = 8
FACE = NP * NP
LANES = 128
step_size = 0.15
stress_slot = ((3, 8, 7), (8, 4, 6), (7, 6, 5))
shear_pairs = ((6, 1, 2), (7, 0, 2), (8, 0, 1))
LIMIT = 20 * 1024 * 1024
PACK_LIMIT = 56 * 1024 * 1024


def trace_table():
    table = np.zeros((NP**3, 4 * FACE), np.float32)
    for first in range(NP):
        for second in range(NP):
            m = first * NP + second
            table[first * 64 + second, m] = 1.0
            table[first * 64 + 56 + second, FACE + m] = 1.0
            table[first * 64 + second * 8, 2 * FACE + m] = 1.0
            table[first * 64 + second * 8 + 7, 3 * FACE + m] = 1.0
    return table


def lane_index(shape):
    return lax.broadcasted_iota(jnp.int32, shape, len(shape) - 1)


def merged(forward, adjoint, upper):
    rows = forward.shape[:-1]
    flat = (-1, LANES)
    turned = pltpu.roll(adjoint.reshape(flat), FACE, 1)
    own = (lane_index(turned.shape) >= FACE) == upper
    return jnp.where(own, forward.reshape(flat), turned).reshape(rows + (LANES,))


def odd_position(axis):
    return lax.axis_index(axis) % 2 == 1


def pack_kernel(state_ref, far_ref, near_ref, held_ref, ready_ref, sem, out_sem):
    odd = odd_position("gx")
    last = state_ref.shape[-1] - LANES
    part = held_ref.shape[3]
    chunks = [(h, c) for h in range(2) for c in range(2)]

    def fetch(h, c):
        first_tile = odd if h == 1 else jnp.logical_not(odd)
        at = pl.multiple_of(jnp.where(first_tile, 0, last), LANES)
        return pltpu.make_async_copy(
            state_ref.at[:, pl.ds(c * part, part), :, :, pl.ds(at, LANES)],
            held_ref.at[h, c],
            sem.at[h, c],
        )

    def deliver(h, c):
        target = (far_ref, near_ref)[h]
        return pltpu.make_async_copy(
            ready_ref.at[h, c], target.at[pl.ds(c * part, part)], out_sem.at[h, c]
        )

    for h, c in chunks:
        fetch(h, c).start()
    for h, c in chunks:
        fetch(h, c).wait()
        upper = jnp.logical_not(odd) if h == 1 else odd
        ready_ref[h, c] = merged(held_ref[h, c, 0], held_ref[h, c, 1], upper)
        deliver(h, c).start()
    for h, c in chunks:
        deliver(h, c).wait()


def pack_faces(state):
    _, count_y, fields, count_z, nodes = state.shape
    message = jax.ShapeDtypeStruct((count_y, fields, count_z, LANES), jnp.float32)
    return pl.pallas_call(
        pack_kernel,
        out_shape=(message, message),
        in_specs=[pl.BlockSpec(memory_space=pl.ANY)],
        out_specs=(pl.BlockSpec(memory_space=pl.ANY),) * 2,
        scratch_shapes=[
            pltpu.VMEM((2, 2, 2, count_y // 2, fields, count_z, LANES), jnp.float32),
            pltpu.VMEM((2, 2, count_y // 2, fields, count_z, LANES), jnp.float32),
            pltpu.SemaphoreType.DMA((2, 2)),
            pltpu.SemaphoreType.DMA((2, 2)),
        ],
        compiler_params=pltpu.CompilerParams(vmem_limit_bytes=PACK_LIMIT),
        cost_estimate=pl.CostEstimate(flops=10**6, bytes_accessed=2 * 10**6, transcendentals=0),
        name="pack_faces",
    )(state)


def trace_kernel(state_ref, table_ref, trace_ref, y_two, y_one, z_two, z_one):
    _, count_y, fields, count_z, _ = state_ref.shape

    def one_state(s, carry):
        values = state_ref[s].reshape(count_y * fields * count_z, -1)
        high = values.astype(jnp.bfloat16)
        low = (values - high.astype(jnp.float32)).astype(jnp.bfloat16)
        table = table_ref[...]
        picked = jnp.dot(high, table, preferred_element_type=jnp.float32)
        picked = picked + jnp.dot(low, table, preferred_element_type=jnp.float32)
        trace_ref[s] = picked.reshape(count_y, fields, count_z, 2 * LANES)
        return carry

    lax.fori_loop(0, 2, one_state, 0)
    odd_y = odd_position("gy")
    odd_z = odd_position("gz")
    end = count_y - 1
    down = merged(trace_ref[0, 0, :, :, :LANES], trace_ref[1, 0, :, :, :LANES], False)
    up = merged(trace_ref[0, end, :, :, :LANES], trace_ref[1, end, :, :, :LANES], True)
    y_two[...] = jnp.where(odd_y, up, down)
    y_one[...] = jnp.where(odd_y, down, up)
    for y in range(count_y):
        first = merged(trace_ref[0, y, :, 0, LANES:], trace_ref[1, y, :, 0, LANES:], False)
        last = merged(
            trace_ref[0, y, :, count_z - 1, LANES:], trace_ref[1, y, :, count_z - 1, LANES:], True
        )
        z_two[y] = jnp.where(odd_z, last, first)
        z_one[y] = jnp.where(odd_z, first, last)


def extract_traces(state, table):
    _, count_y, fields, count_z, nodes = state.shape
    f32 = jnp.float32
    y_message = jax.ShapeDtypeStruct((fields, count_z, LANES), f32)
    z_message = jax.ShapeDtypeStruct((count_y, fields, LANES), f32)
    return pl.pallas_call(
        trace_kernel,
        out_shape=(
            jax.ShapeDtypeStruct((2, count_y, fields, count_z, 2 * LANES), f32),
            y_message,
            y_message,
            z_message,
            z_message,
        ),
        in_specs=[pl.BlockSpec(memory_space=pltpu.VMEM)] * 2,
        out_specs=(pl.BlockSpec(memory_space=pltpu.VMEM),) * 5,
        compiler_params=pltpu.CompilerParams(vmem_limit_bytes=LIMIT),
        cost_estimate=pl.CostEstimate(flops=6 * 10**8, bytes_accessed=4 * 10**6, transcendentals=0),
        name="extract_traces",
    )(state, table)


def spread(columns, rows, pick):
    return lax.dot_general(
        columns,
        pick,
        (((0,), (0,)), ((), ())),
        precision=lax.Precision.HIGHEST,
        preferred_element_type=jnp.float32,
    )


def volume_kernel(
    state_ref, deriv_ref, material_ref, orient_ref, flags_ref,
    partial_ref, coef_ref, source_ref, edge_ref,
    low_ref, grad_ref, div_ref, wide_ref,
):
    _, count_y, fields, count_z, _ = state_ref.shape
    rows = 2 * count_y * count_z
    nodes = partial_ref.shape[-1]
    width = grad_ref.shape[-1]
    ends = [
        lax.axis_index("gy") == 0,
        lax.axis_index("gy") == lax.axis_size("gy") - 1,
        lax.axis_index("gz") == 0,
        lax.axis_index("gz") == lax.axis_size("gz") - 1,
    ]

    for f in range(fields):
        low_ref[f] = state_ref[:, :, f].reshape(rows, -1).astype(jnp.bfloat16)
    lanes = lane_index((3 * count_y, 3 * count_y * LANES))
    row = lax.broadcasted_iota(jnp.int32, lanes.shape, 0)
    pick = (lanes // LANES == row).astype(jnp.float32)
    medium = spread(material_ref[...].reshape(3 * count_y, count_z), 3 * count_y, pick)
    lanes = lane_index((6 * count_y, 3 * count_y * LANES))
    row = lax.broadcasted_iota(jnp.int32, lanes.shape, 0)
    block = lanes // LANES
    face = 2 * (block // count_y) + (lanes % LANES) // FACE
    pick = (face * count_y + block % count_y == row).astype(jnp.float32)
    codes = spread(
        orient_ref[...].reshape(6 * count_y, count_z).astype(jnp.float32), 6 * count_y, pick
    )
    kinds = spread(
        flags_ref[...].reshape(6 * count_y, count_z).astype(jnp.float32), 6 * count_y, pick
    )
    lane = lane_index((count_z, LANES))
    upper = lane >= FACE
    half_sign = jnp.where(upper, 0.5, -0.5)
    node = lane % FACE
    near, far = (node // NP, node % NP)
    z_pos = lax.broadcasted_iota(jnp.int32, lane.shape, 0)
    for y in range(count_y):
        lam = medium[:, y * LANES : (y + 1) * LANES]
        mu = medium[:, (count_y + y) * LANES : (count_y + y + 1) * LANES]
        rho = medium[:, (2 * count_y + y) * LANES : (2 * count_y + y + 1) * LANES]
        inv = 1.0 / rho
        wide_ref[0, y] = lam
        wide_ref[1, y] = mu
        wide_ref[2, y] = inv
        coef_ref[0, y] = half_sign * lam
        coef_ref[1, y] = half_sign * mu
        coef_ref[2, y] = half_sign * inv
        coef_ref[3, y] = 0.5 * jnp.sqrt((lam + 2.0 * mu) * inv)
        for d in range(3):
            at = (d * count_y + y) * LANES
            code = jnp.round(codes[:, at : at + LANES]).astype(jnp.int32)
            swap = code >= 4
            lead = jnp.where(swap, far, near)
            trail = jnp.where(swap, near, far)
            lead = jnp.where(code % 2 == 1, NP - 1 - lead, lead)
            trail = jnp.where((code // 2) % 2 == 1, NP - 1 - trail, trail)
            source_ref[d, y] = lead * NP + trail + jnp.where(upper, 0, FACE)
            if d > 0:
                free = jnp.where(jnp.round(kinds[:, at : at + LANES]) == 1.0, 1.0, 0.0)
                if d == 1:
                    low_end = (ends[0]) if y == 0 else False
                    high_end = (ends[1]) if y == count_y - 1 else False
                    rim = jnp.where(
                        upper,
                        jnp.where(high_end, 1.0, 0.0),
                        jnp.where(low_end, 1.0, 0.0),
                    )
                else:
                    low_rim = jnp.where(z_pos == 0, jnp.where(ends[2], 1.0, 0.0), 0.0)
                    high_rim = jnp.where(
                        z_pos == count_z - 1, jnp.where(ends[3], 1.0, 0.0), 0.0
                    )
                    rim = jnp.where(upper, high_rim, low_rim)
                edge_ref[d - 1, 0, y] = rim
                edge_ref[d - 1, 1, y] = free

    def columns_part(n, carry):
        base = n * width

        def operator(d):
            return deriv_ref[:, pl.ds(pl.multiple_of(d * nodes + base, LANES), width)]

        velocity = low_ref[0:3].reshape(3 * rows, nodes)
        for d in range(3):
            grad_ref[d] = jnp.dot(velocity, operator(d), preferred_element_type=jnp.float32)
        total = None
        for d in range(3):
            stress = jnp.concatenate([low_ref[stress_slot[i][d]] for i in range(3)], axis=0)
            part = jnp.dot(stress, operator(d), preferred_element_type=jnp.float32)
            total = part if total is None else total + part
        div_ref[...] = total
        for s in range(2):
            scale = step_size if s == 0 else -step_size
            for y in range(count_y):
                at = (s * count_y + y) * count_z
                lam = scale * wide_ref[0, y]
                mu = scale * wide_ref[1, y]
                inv = scale * wide_ref[2, y]
                for tile in range(width // LANES):
                    columns = slice(tile * LANES, (tile + 1) * LANES)
                    where = pl.ds(pl.multiple_of(base + tile * LANES, LANES), LANES)

                    def g(d, i):
                        return grad_ref[d, i * rows + at : i * rows + at + count_z, columns]

                    def put(f, term):
                        partial_ref[s, y, f, :, where] = state_ref[s, y, f, :, where] + term

                    for i in range(3):
                        put(i, inv * div_ref[i * rows + at : i * rows + at + count_z, columns])
                    diag = [g(i, i) for i in range(3)]
                    common = lam * (diag[0] + diag[1] + diag[2])
                    for i in range(3):
                        put(3 + i, common + (mu + mu) * diag[i])
                    for f, i, j in shear_pairs:
                        put(f, mu * (g(j, i) + g(i, j)))
        return carry

    lax.fori_loop(0, nodes // width, columns_part, 0)


def volume(state, deriv, material, orient, flags):
    _, count_y, fields, count_z, nodes = state.shape
    f32 = jnp.float32
    width = 256
    rows = 2 * count_y * count_z
    outs = (
        jax.ShapeDtypeStruct(state.shape, f32),
        jax.ShapeDtypeStruct((4, count_y, count_z, LANES), f32),
        jax.ShapeDtypeStruct((3, count_y, count_z, LANES), jnp.int32),
        jax.ShapeDtypeStruct((2, 2, count_y, count_z, LANES), f32),
    )
    return pl.pallas_call(
        volume_kernel,
        out_shape=outs,
        in_specs=[pl.BlockSpec(memory_space=pltpu.VMEM)] * 5,
        out_specs=(pl.BlockSpec(memory_space=pltpu.VMEM),) * 4,
        scratch_shapes=[
            pltpu.VMEM((fields, rows, nodes), jnp.bfloat16),
            pltpu.VMEM((3, 3 * rows, width), f32),
            pltpu.VMEM((3 * rows, width), f32),
            pltpu.VMEM((3, count_y, count_z, LANES), f32),
        ],
        compiler_params=pltpu.CompilerParams(vmem_limit_bytes=LIMIT),
        cost_estimate=pl.CostEstimate(
            flops=10**6, bytes_accessed=10**5, transcendentals=0
        ),
        name="volume",
    )(state, deriv, material, orient, flags)


def final_kernel(
    state_ref, trace_ref, far_ref, near_ref, y_two, y_one, z_two, z_one,
    coef_ref, source_ref, edge_ref, partial_ref, stored_ref, lift_ref,
    advanced_ref, kernel_ref,
    flux_ref, sum_ref, out_ref, out_sem,
):
    count_y, fields, count_z, nodes = state_ref.shape[1:]
    last_y = count_y - 1
    odd_x = odd_position("gx")
    odd_y = odd_position("gy")
    odd_z = odd_position("gz")
    lane = lane_index((count_z, LANES))
    upper = lane >= FACE
    z_pos = lax.broadcasted_iota(jnp.int32, lane.shape, 0)
    take_near = upper == odd_x

    def write(y):
        return pltpu.make_async_copy(out_ref.at[:, y], advanced_ref.at[:, y], out_sem.at[y])

    def row(y, carry):
        below = jnp.maximum(y - 1, 0)
        above = jnp.minimum(y + 1, last_y)
        lam, mu, inv, speed = [coef_ref[k, y] for k in range(4)]
        for s in range(2):
            for d in range(3):
                source = source_ref[d, y]
                if d == 0 and s == 1:
                    source = (source + FACE) % LANES
                if d > 0:
                    rim = edge_ref[d - 1, 0, y] > 0.0
                    free = edge_ref[d - 1, 1, y]
                    keep_velocity = free - 1.0
                    keep_stress = -free - 1.0
                jumps = []
                for f in range(fields):
                    if d == 0:
                        inside = jnp.where(
                            upper, state_ref[s, y, f, :, nodes - LANES :], state_ref[s, y, f, :, :LANES]
                        )
                        near, far = (near_ref[y, f], far_ref[y, f])
                        if s == 1:
                            near, far = (far, near)
                        mixed = jnp.where(take_near, near, far)
                    elif d == 1:
                        inside = trace_ref[s, y, f, :, :LANES]
                        two, one = (y_two[f], y_one[f])
                        from_below = jnp.where(odd_y, one, two)
                        from_above = jnp.where(odd_y, two, one)
                        if s == 1:
                            from_below = pltpu.roll(from_below, FACE, 1)
                            from_above = pltpu.roll(from_above, FACE, 1)
                        lower = jnp.where(y == 0, from_below, trace_ref[s, below, f, :, :LANES])
                        higher = jnp.where(y == last_y, from_above, trace_ref[s, above, f, :, :LANES])
                        mixed = jnp.where(upper, lower, higher)
                    else:
                        inside = trace_ref[s, y, f, :, LANES:]
                        two = jnp.broadcast_to(z_two[y, f : f + 1, :], lane.shape)
                        one = jnp.broadcast_to(z_one[y, f : f + 1, :], lane.shape)
                        from_below = jnp.where(odd_z, one, two)
                        from_above = jnp.where(odd_z, two, one)
                        if s == 1:
                            from_below = pltpu.roll(from_below, FACE, 1)
                            from_above = pltpu.roll(from_above, FACE, 1)
                        lower = jnp.where(z_pos == 0, from_below, pltpu.roll(inside, 1, 0))
                        higher = jnp.where(
                            z_pos == count_z - 1, from_above, pltpu.roll(inside, count_z - 1, 0)
                        )
                        mixed = jnp.where(upper, lower, higher)
                    turned = jnp.take_along_axis(mixed, source, axis=1)
                    jump = turned - inside
                    if d > 0:
                        keep = keep_velocity if f < 3 else keep_stress
                        jump = jnp.where(rim, inside * keep, jump)
                    jumps.append(jump)
                    if s == 1:
                        term = stored_ref[y, f, :, d * LANES : (d + 1) * LANES] * jump
                        if d == 0:
                            sum_ref[f] = term
                        else:
                            sum_ref[f] += term
                flux = [speed * jump for jump in jumps]
                for i in range(3):
                    flux[i] = flux[i] + inv * jumps[stress_slot[i][d]]
                common = lam * jumps[d]
                for i in range(3):
                    flux[3 + i] = flux[3 + i] + common
                for i, j, f in ((0, 0, 3), (1, 1, 4), (2, 2, 5), (1, 2, 6), (0, 2, 7), (0, 1, 8)):
                    if j == d:
                        flux[f] = flux[f] + mu * jumps[i]
                    if i == d:
                        flux[f] = flux[f] + mu * jumps[j]
                for f in range(fields):
                    flux_ref[s, f, :, d * LANES : (d + 1) * LANES] = flux[f].astype(jnp.bfloat16)
        lifted = jnp.dot(
            flux_ref[...].reshape(2 * fields * count_z, 3 * LANES),
            lift_ref[...],
            preferred_element_type=jnp.float32,
        ).reshape(2, fields, count_z, nodes)
        for s in range(2):
            scale = step_size if s == 0 else -step_size
            out_ref[s, y] = partial_ref[s, y] + scale * lifted[s]
        write(y).start()
        for f in range(fields):
            sums = jnp.sum(sum_ref[f], axis=1, keepdims=True) * (1.0 / FACE)
            across = jnp.sum(jnp.where(z_pos == lane, sums, 0.0), axis=0, keepdims=True)
            kernel_ref[f, pl.ds(y, 1), :] = across[:, :count_z]
        return carry

    lax.fori_loop(0, count_y, row, 0)
    for y in range(count_y):
        write(y).wait()


def finish(
    state, traces, far, near, y_two, y_one, z_two, z_one, coef, source, edge, part, stored, lift
):
    _, count_y, fields, count_z, nodes = state.shape
    f32 = jnp.float32
    outs = (
        jax.ShapeDtypeStruct(state.shape, f32),
        jax.ShapeDtypeStruct((fields, count_y, count_z), f32),
    )
    return pl.pallas_call(
        final_kernel,
        out_shape=outs,
        in_specs=[pl.BlockSpec(memory_space=pltpu.VMEM)] * 14,
        out_specs=(pl.BlockSpec(memory_space=pl.ANY), pl.BlockSpec(memory_space=pltpu.VMEM)),
        scratch_shapes=[
            pltpu.VMEM((2, fields, count_z, 3 * LANES), jnp.bfloat16),
            pltpu.VMEM((fields, count_z, LANES), f32),
            pltpu.VMEM(state.shape, f32),
            pltpu.SemaphoreType.DMA((count_y,)),
        ],
        compiler_params=pltpu.CompilerParams(vmem_limit_bytes=LIMIT),
        cost_estimate=pl.CostEstimate(flops=9 * 10**8, bytes_accessed=10**7, transcendentals=0),
        name="finish",
    )(state, traces, far, near, y_two, y_one, z_two, z_one, coef, source, edge, part, stored, lift)


def swaps(count, start, wrap):
    pairs = []
    for i in range(start, count if wrap else count - 1, 2):
        j = (i + 1) % count
        pairs += [(i, j), (j, i)]
    return pairs


def local(state, deriv, lift, material, stored, orient, flags):
    view = jnp.transpose(state[:, 0], (0, 1, 3, 2, 4))
    stored_view = jnp.transpose(stored[0], (0, 2, 1, 3))
    orient_view = jnp.transpose(orient[0], (2, 0, 1))
    flags_view = jnp.transpose(flags[0], (2, 0, 1))
    nx, ny, nz = (lax.axis_size(a) for a in ("gx", "gy", "gz"))
    table = jnp.asarray(trace_table(), jnp.bfloat16)
    far, near = pack_faces(view)
    far, near, table, state = lax.optimization_barrier((far, near, table, state))
    view = jnp.transpose(state[:, 0], (0, 1, 3, 2, 4))
    far_in = lax.ppermute(far, "gx", swaps(nx, 1, True))
    near_in = lax.ppermute(near, "gx", swaps(nx, 0, True))
    traces, y_two, y_one, z_two, z_one = extract_traces(view, table)
    y_one = lax.ppermute(y_one, "gy", swaps(ny, 0, False))
    y_two = lax.ppermute(y_two, "gy", swaps(ny, 1, False))
    z_one = lax.ppermute(z_one, "gz", swaps(nz, 0, False))
    medium = material[:, 0]
    z_two, medium, y_one = lax.optimization_barrier((z_two, medium, y_one))
    z_two = lax.ppermute(z_two, "gz", swaps(nz, 1, False))
    part, coef, source, edge = volume(view, deriv, medium, orient_view, flags_view)
    advanced, kernel = finish(
        view, traces, far_in, near_in, y_two, y_one, z_two, z_one, coef, source, edge, part,
        stored_view, lift,
    )
    return (
        jnp.transpose(advanced, (0, 1, 3, 2, 4))[:, None],
        jnp.transpose(kernel, (1, 2, 0))[None],
    )


def solution(mesh):
    placed = (
        P(None, "gx", "gy", "gz", None, None),
        P(),
        P(),
        P(None, "gx", "gy", "gz"),
        P("gx", "gy", "gz", None, None),
        P("gx", "gy", "gz", None),
        P("gx", "gy", "gz", None),
    )
    return jax.shard_map(
        local,
        mesh=mesh,
        in_specs=placed,
        out_specs=(P(None, "gx", "gy", "gz", None, None), P("gx", "gy", "gz", None)),
        check_vma=False,
    )
```

```python
import jax
import jax.numpy as jnp
import numpy as np
from functools import partial
from jax import lax
from jax.experimental import pallas as pl
from jax.experimental.pallas import tpu as pltpu
from jax.sharding import PartitionSpec as P

NP = 8
FACE = NP * NP
LANES = 128
step_size = 0.15
stress_slot = ((3, 8, 7), (8, 4, 6), (7, 6, 5))
shear_pairs = ((6, 1, 2), (7, 0, 2), (8, 0, 1))
LIMIT = 20 * 1024 * 1024
PACK_LIMIT = 50 * 1024 * 1024


def trace_table():
    table = np.zeros((NP**3, 4 * FACE), np.float32)
    for first in range(NP):
        for second in range(NP):
            m = first * NP + second
            table[first * 64 + second, m] = 1.0
            table[first * 64 + 56 + second, FACE + m] = 1.0
            table[first * 64 + second * 8, 2 * FACE + m] = 1.0
            table[first * 64 + second * 8 + 7, 3 * FACE + m] = 1.0
    return table


def lane_index(shape):
    return lax.broadcasted_iota(jnp.int32, shape, len(shape) - 1)


def merged(forward, adjoint, upper):
    rows = forward.shape[:-1]
    flat = (-1, LANES)
    turned = pltpu.roll(adjoint.reshape(flat), FACE, 1)
    own = (lane_index(turned.shape) >= FACE) == upper
    return jnp.where(own, forward.reshape(flat), turned).reshape(rows + (LANES,))


def odd_position(axis):
    return lax.axis_index(axis) % 2 == 1


def pack_kernel(state_ref, held_ref, far_ref, near_ref, sem):
    odd = odd_position("gx")
    tiles = state_ref.shape[-1] // LANES
    order = [0, tiles - 1] + list(range(1, tiles - 1))

    def fetch(t):
        columns = pl.ds(t * LANES, LANES)
        return pltpu.make_async_copy(
            state_ref.at[:, :, :, :, columns], held_ref.at[:, :, :, :, columns], sem.at[t]
        )

    for t in order:
        fetch(t).start()
    for t in order[:2]:
        fetch(t).wait()
    low, high = slice(0, LANES), slice((tiles - 1) * LANES, tiles * LANES)
    for y in range(far_ref.shape[0]):
        down = merged(held_ref[0, y, :, :, low], held_ref[1, y, :, :, low], False)
        up = merged(held_ref[0, y, :, :, high], held_ref[1, y, :, :, high], True)
        far_ref[y] = jnp.where(odd, up, down)
        near_ref[y] = jnp.where(odd, down, up)
    for t in order[2:]:
        fetch(t).wait()


def pack_faces(state):
    _, count_y, fields, count_z, nodes = state.shape
    message = jax.ShapeDtypeStruct((count_y, fields, count_z, LANES), jnp.float32)
    return pl.pallas_call(
        pack_kernel,
        out_shape=(jax.ShapeDtypeStruct(state.shape, jnp.float32), message, message),
        in_specs=[pl.BlockSpec(memory_space=pl.ANY)],
        out_specs=(pl.BlockSpec(memory_space=pltpu.VMEM),) * 3,
        scratch_shapes=[pltpu.SemaphoreType.DMA((nodes // LANES,))],
        compiler_params=pltpu.CompilerParams(vmem_limit_bytes=PACK_LIMIT),
        cost_estimate=pl.CostEstimate(flops=10**6, bytes_accessed=2 * 10**6, transcendentals=0),
        name="pack_faces",
    )(state)


def trace_kernel(state_ref, table_ref, trace_ref, y_two, y_one, z_two, z_one):
    _, count_y, fields, count_z, _ = state_ref.shape

    def one_state(s, carry):
        values = state_ref[s].reshape(count_y * fields * count_z, -1)
        high = values.astype(jnp.bfloat16)
        low = (values - high.astype(jnp.float32)).astype(jnp.bfloat16)
        table = table_ref[...]
        picked = jnp.dot(high, table, preferred_element_type=jnp.float32)
        picked = picked + jnp.dot(low, table, preferred_element_type=jnp.float32)
        trace_ref[s] = picked.reshape(count_y, fields, count_z, 2 * LANES)
        return carry

    lax.fori_loop(0, 2, one_state, 0)
    odd_y = odd_position("gy")
    odd_z = odd_position("gz")
    end = count_y - 1
    down = merged(trace_ref[0, 0, :, :, :LANES], trace_ref[1, 0, :, :, :LANES], False)
    up = merged(trace_ref[0, end, :, :, :LANES], trace_ref[1, end, :, :, :LANES], True)
    y_two[...] = jnp.where(odd_y, up, down)
    y_one[...] = jnp.where(odd_y, down, up)
    for y in range(count_y):
        first = merged(trace_ref[0, y, :, 0, LANES:], trace_ref[1, y, :, 0, LANES:], False)
        last = merged(
            trace_ref[0, y, :, count_z - 1, LANES:], trace_ref[1, y, :, count_z - 1, LANES:], True
        )
        z_two[y] = jnp.where(odd_z, last, first)
        z_one[y] = jnp.where(odd_z, first, last)


def extract_traces(state, table):
    _, count_y, fields, count_z, nodes = state.shape
    f32 = jnp.float32
    y_message = jax.ShapeDtypeStruct((fields, count_z, LANES), f32)
    z_message = jax.ShapeDtypeStruct((count_y, fields, LANES), f32)
    return pl.pallas_call(
        trace_kernel,
        out_shape=(
            jax.ShapeDtypeStruct((2, count_y, fields, count_z, 2 * LANES), f32),
            y_message,
            y_message,
            z_message,
            z_message,
        ),
        in_specs=[pl.BlockSpec(memory_space=pltpu.VMEM)] * 2,
        out_specs=(pl.BlockSpec(memory_space=pltpu.VMEM),) * 5,
        compiler_params=pltpu.CompilerParams(vmem_limit_bytes=LIMIT),
        cost_estimate=pl.CostEstimate(flops=6 * 10**8, bytes_accessed=4 * 10**6, transcendentals=0),
        name="extract_traces",
    )(state, table)


def spread(columns, rows, pick):
    return lax.dot_general(
        columns,
        pick,
        (((0,), (0,)), ((), ())),
        precision=lax.Precision.HIGHEST,
        preferred_element_type=jnp.float32,
    )


def volume_kernel(
    state_ref, deriv_ref, material_ref, orient_ref, flags_ref,
    partial_ref, coef_ref, source_ref, edge_ref,
    low_ref, grad_ref, div_ref, wide_ref,
):
    _, count_y, fields, count_z, _ = state_ref.shape
    rows = 2 * count_y * count_z
    nodes = partial_ref.shape[-1]
    width = grad_ref.shape[-1]
    ends = [
        lax.axis_index("gy") == 0,
        lax.axis_index("gy") == lax.axis_size("gy") - 1,
        lax.axis_index("gz") == 0,
        lax.axis_index("gz") == lax.axis_size("gz") - 1,
    ]

    for f in range(fields):
        low_ref[f] = state_ref[:, :, f].reshape(rows, -1).astype(jnp.bfloat16)
    lanes = lane_index((3 * count_y, 3 * count_y * LANES))
    row = lax.broadcasted_iota(jnp.int32, lanes.shape, 0)
    pick = (lanes // LANES == row).astype(jnp.float32)
    medium = spread(material_ref[...].reshape(3 * count_y, count_z), 3 * count_y, pick)
    lanes = lane_index((6 * count_y, 3 * count_y * LANES))
    row = lax.broadcasted_iota(jnp.int32, lanes.shape, 0)
    block = lanes // LANES
    face = 2 * (block // count_y) + (lanes % LANES) // FACE
    pick = (face * count_y + block % count_y == row).astype(jnp.float32)
    codes = spread(
        orient_ref[...].reshape(6 * count_y, count_z).astype(jnp.float32), 6 * count_y, pick
    )
    kinds = spread(
        flags_ref[...].reshape(6 * count_y, count_z).astype(jnp.float32), 6 * count_y, pick
    )
    lane = lane_index((count_z, LANES))
    upper = lane >= FACE
    half_sign = jnp.where(upper, 0.5, -0.5)
    node = lane % FACE
    near, far = (node // NP, node % NP)
    z_pos = lax.broadcasted_iota(jnp.int32, lane.shape, 0)
    for y in range(count_y):
        lam = medium[:, y * LANES : (y + 1) * LANES]
        mu = medium[:, (count_y + y) * LANES : (count_y + y + 1) * LANES]
        rho = medium[:, (2 * count_y + y) * LANES : (2 * count_y + y + 1) * LANES]
        inv = 1.0 / rho
        wide_ref[0, y] = lam
        wide_ref[1, y] = mu
        wide_ref[2, y] = inv
        coef_ref[0, y] = half_sign * lam
        coef_ref[1, y] = half_sign * mu
        coef_ref[2, y] = half_sign * inv
        coef_ref[3, y] = 0.5 * jnp.sqrt((lam + 2.0 * mu) * inv)
        for d in range(3):
            at = (d * count_y + y) * LANES
            code = jnp.round(codes[:, at : at + LANES]).astype(jnp.int32)
            swap = code >= 4
            lead = jnp.where(swap, far, near)
            trail = jnp.where(swap, near, far)
            lead = jnp.where(code % 2 == 1, NP - 1 - lead, lead)
            trail = jnp.where((code // 2) % 2 == 1, NP - 1 - trail, trail)
            source_ref[d, y] = lead * NP + trail + jnp.where(upper, 0, FACE)
            if d > 0:
                free = jnp.where(jnp.round(kinds[:, at : at + LANES]) == 1.0, 1.0, 0.0)
                if d == 1:
                    low_end = (ends[0]) if y == 0 else False
                    high_end = (ends[1]) if y == count_y - 1 else False
                    rim = jnp.where(
                        upper,
                        jnp.where(high_end, 1.0, 0.0),
                        jnp.where(low_end, 1.0, 0.0),
                    )
                else:
                    low_rim = jnp.where(z_pos == 0, jnp.where(ends[2], 1.0, 0.0), 0.0)
                    high_rim = jnp.where(
                        z_pos == count_z - 1, jnp.where(ends[3], 1.0, 0.0), 0.0
                    )
                    rim = jnp.where(upper, high_rim, low_rim)
                edge_ref[d - 1, 0, y] = rim
                edge_ref[d - 1, 1, y] = free

    def columns_part(n, carry):
        base = n * width

        def operator(d):
            return deriv_ref[:, pl.ds(pl.multiple_of(d * nodes + base, LANES), width)]

        velocity = low_ref[0:3].reshape(3 * rows, nodes)
        for d in range(3):
            grad_ref[d] = jnp.dot(velocity, operator(d), preferred_element_type=jnp.float32)
        total = None
        for d in range(3):
            stress = jnp.concatenate([low_ref[stress_slot[i][d]] for i in range(3)], axis=0)
            part = jnp.dot(stress, operator(d), preferred_element_type=jnp.float32)
            total = part if total is None else total + part
        div_ref[...] = total
        for s in range(2):
            scale = step_size if s == 0 else -step_size
            for y in range(count_y):
                at = (s * count_y + y) * count_z
                lam = scale * wide_ref[0, y]
                mu = scale * wide_ref[1, y]
                inv = scale * wide_ref[2, y]
                for tile in range(width // LANES):
                    columns = slice(tile * LANES, (tile + 1) * LANES)
                    where = pl.ds(pl.multiple_of(base + tile * LANES, LANES), LANES)

                    def g(d, i):
                        return grad_ref[d, i * rows + at : i * rows + at + count_z, columns]

                    def put(f, term):
                        partial_ref[s, y, f, :, where] = state_ref[s, y, f, :, where] + term

                    for i in range(3):
                        put(i, inv * div_ref[i * rows + at : i * rows + at + count_z, columns])
                    diag = [g(i, i) for i in range(3)]
                    common = lam * (diag[0] + diag[1] + diag[2])
                    for i in range(3):
                        put(3 + i, common + (mu + mu) * diag[i])
                    for f, i, j in shear_pairs:
                        put(f, mu * (g(j, i) + g(i, j)))
        return carry

    lax.fori_loop(0, nodes // width, columns_part, 0)


def volume(state, deriv, material, orient, flags):
    _, count_y, fields, count_z, nodes = state.shape
    f32 = jnp.float32
    width = 256
    rows = 2 * count_y * count_z
    outs = (
        jax.ShapeDtypeStruct(state.shape, f32),
        jax.ShapeDtypeStruct((4, count_y, count_z, LANES), f32),
        jax.ShapeDtypeStruct((3, count_y, count_z, LANES), jnp.int32),
        jax.ShapeDtypeStruct((2, 2, count_y, count_z, LANES), f32),
    )
    return pl.pallas_call(
        volume_kernel,
        out_shape=outs,
        in_specs=[pl.BlockSpec(memory_space=pltpu.VMEM)] * 5,
        out_specs=(pl.BlockSpec(memory_space=pltpu.VMEM),) * 4,
        scratch_shapes=[
            pltpu.VMEM((fields, rows, nodes), jnp.bfloat16),
            pltpu.VMEM((3, 3 * rows, width), f32),
            pltpu.VMEM((3 * rows, width), f32),
            pltpu.VMEM((3, count_y, count_z, LANES), f32),
        ],
        compiler_params=pltpu.CompilerParams(vmem_limit_bytes=LIMIT),
        cost_estimate=pl.CostEstimate(
            flops=10**6, bytes_accessed=10**5, transcendentals=0
        ),
        name="volume",
    )(state, deriv, material, orient, flags)


def final_kernel(
    state_ref, trace_ref, far_ref, near_ref, y_two, y_one, z_two, z_one,
    coef_ref, source_ref, edge_ref, partial_ref, stored_ref, lift_ref,
    advanced_ref, kernel_ref,
    flux_ref, sum_ref, out_ref, out_sem,
):
    count_y, fields, count_z, nodes = state_ref.shape[1:]
    last_y = count_y - 1
    odd_x = odd_position("gx")
    odd_y = odd_position("gy")
    odd_z = odd_position("gz")
    lane = lane_index((count_z, LANES))
    upper = lane >= FACE
    z_pos = lax.broadcasted_iota(jnp.int32, lane.shape, 0)
    take_near = upper == odd_x

    def write(y):
        return pltpu.make_async_copy(out_ref.at[:, y], advanced_ref.at[:, y], out_sem.at[y])

    def row(y, carry):
        below = jnp.maximum(y - 1, 0)
        above = jnp.minimum(y + 1, last_y)
        lam, mu, inv, speed = [coef_ref[k, y] for k in range(4)]
        for s in range(2):
            for d in range(3):
                source = source_ref[d, y]
                if d == 0 and s == 1:
                    source = (source + FACE) % LANES
                if d > 0:
                    rim = edge_ref[d - 1, 0, y] > 0.0
                    free = edge_ref[d - 1, 1, y]
                    keep_velocity = free - 1.0
                    keep_stress = -free - 1.0
                jumps = []
                for f in range(fields):
                    if d == 0:
                        inside = jnp.where(
                            upper, state_ref[s, y, f, :, nodes - LANES :], state_ref[s, y, f, :, :LANES]
                        )
                        near, far = (near_ref[y, f], far_ref[y, f])
                        if s == 1:
                            near, far = (far, near)
                        mixed = jnp.where(take_near, near, far)
                    elif d == 1:
                        inside = trace_ref[s, y, f, :, :LANES]
                        two, one = (y_two[f], y_one[f])
                        from_below = jnp.where(odd_y, one, two)
                        from_above = jnp.where(odd_y, two, one)
                        if s == 1:
                            from_below = pltpu.roll(from_below, FACE, 1)
                            from_above = pltpu.roll(from_above, FACE, 1)
                        lower = jnp.where(y == 0, from_below, trace_ref[s, below, f, :, :LANES])
                        higher = jnp.where(y == last_y, from_above, trace_ref[s, above, f, :, :LANES])
                        mixed = jnp.where(upper, lower, higher)
                    else:
                        inside = trace_ref[s, y, f, :, LANES:]
                        two = jnp.broadcast_to(z_two[y, f : f + 1, :], lane.shape)
                        one = jnp.broadcast_to(z_one[y, f : f + 1, :], lane.shape)
                        from_below = jnp.where(odd_z, one, two)
                        from_above = jnp.where(odd_z, two, one)
                        if s == 1:
                            from_below = pltpu.roll(from_below, FACE, 1)
                            from_above = pltpu.roll(from_above, FACE, 1)
                        lower = jnp.where(z_pos == 0, from_below, pltpu.roll(inside, 1, 0))
                        higher = jnp.where(
                            z_pos == count_z - 1, from_above, pltpu.roll(inside, count_z - 1, 0)
                        )
                        mixed = jnp.where(upper, lower, higher)
                    turned = jnp.take_along_axis(mixed, source, axis=1)
                    jump = turned - inside
                    if d > 0:
                        keep = keep_velocity if f < 3 else keep_stress
                        jump = jnp.where(rim, inside * keep, jump)
                    jumps.append(jump)
                    if s == 1:
                        term = stored_ref[y, f, :, d * LANES : (d + 1) * LANES] * jump
                        if d == 0:
                            sum_ref[f] = term
                        else:
                            sum_ref[f] += term
                flux = [speed * jump for jump in jumps]
                for i in range(3):
                    flux[i] = flux[i] + inv * jumps[stress_slot[i][d]]
                common = lam * jumps[d]
                for i in range(3):
                    flux[3 + i] = flux[3 + i] + common
                for i, j, f in ((0, 0, 3), (1, 1, 4), (2, 2, 5), (1, 2, 6), (0, 2, 7), (0, 1, 8)):
                    if j == d:
                        flux[f] = flux[f] + mu * jumps[i]
                    if i == d:
                        flux[f] = flux[f] + mu * jumps[j]
                for f in range(fields):
                    flux_ref[s, f, :, d * LANES : (d + 1) * LANES] = flux[f].astype(jnp.bfloat16)
        lifted = jnp.dot(
            flux_ref[...].reshape(2 * fields * count_z, 3 * LANES),
            lift_ref[...],
            preferred_element_type=jnp.float32,
        ).reshape(2, fields, count_z, nodes)
        for s in range(2):
            scale = step_size if s == 0 else -step_size
            out_ref[s, y] = partial_ref[s, y] + scale * lifted[s]
        write(y).start()
        for f in range(fields):
            sums = jnp.sum(sum_ref[f], axis=1, keepdims=True) * (1.0 / FACE)
            across = jnp.sum(jnp.where(z_pos == lane, sums, 0.0), axis=0, keepdims=True)
            kernel_ref[f, pl.ds(y, 1), :] = across[:, :count_z]
        return carry

    lax.fori_loop(0, count_y, row, 0)
    for y in range(count_y):
        write(y).wait()


def finish(
    state, traces, far, near, y_two, y_one, z_two, z_one, coef, source, edge, part, stored, lift
):
    _, count_y, fields, count_z, nodes = state.shape
    f32 = jnp.float32
    outs = (
        jax.ShapeDtypeStruct(state.shape, f32),
        jax.ShapeDtypeStruct((fields, count_y, count_z), f32),
    )
    return pl.pallas_call(
        final_kernel,
        out_shape=outs,
        in_specs=[pl.BlockSpec(memory_space=pltpu.VMEM)] * 14,
        out_specs=(pl.BlockSpec(memory_space=pl.ANY), pl.BlockSpec(memory_space=pltpu.VMEM)),
        scratch_shapes=[
            pltpu.VMEM((2, fields, count_z, 3 * LANES), jnp.bfloat16),
            pltpu.VMEM((fields, count_z, LANES), f32),
            pltpu.VMEM(state.shape, f32),
            pltpu.SemaphoreType.DMA((count_y,)),
        ],
        compiler_params=pltpu.CompilerParams(vmem_limit_bytes=LIMIT),
        cost_estimate=pl.CostEstimate(flops=9 * 10**8, bytes_accessed=10**7, transcendentals=0),
        name="finish",
    )(state, traces, far, near, y_two, y_one, z_two, z_one, coef, source, edge, part, stored, lift)


def swaps(count, start, wrap):
    pairs = []
    for i in range(start, count if wrap else count - 1, 2):
        j = (i + 1) % count
        pairs += [(i, j), (j, i)]
    return pairs


def local(state, deriv, lift, material, stored, orient, flags):
    view = jnp.transpose(state[:, 0], (0, 1, 3, 2, 4))
    stored_view = jnp.transpose(stored[0], (0, 2, 1, 3))
    orient_view = jnp.transpose(orient[0], (2, 0, 1))
    flags_view = jnp.transpose(flags[0], (2, 0, 1))
    nx, ny, nz = (lax.axis_size(a) for a in ("gx", "gy", "gz"))
    table = jnp.asarray(trace_table(), jnp.bfloat16)
    view, far, near = pack_faces(view)
    far_in = lax.ppermute(far, "gx", swaps(nx, 1, True))
    near_in = lax.ppermute(near, "gx", swaps(nx, 0, True))
    traces, y_two, y_one, z_two, z_one = extract_traces(view, table)
    y_one = lax.ppermute(y_one, "gy", swaps(ny, 0, False))
    y_two = lax.ppermute(y_two, "gy", swaps(ny, 1, True))
    z_one = lax.ppermute(z_one, "gz", swaps(nz, 0, False))
    medium = material[:, 0]
    z_two, medium, y_one = lax.optimization_barrier((z_two, medium, y_one))
    z_two = lax.ppermute(z_two, "gz", swaps(nz, 1, True))
    part, coef, source, edge = volume(view, deriv, medium, orient_view, flags_view)
    advanced, kernel = finish(
        view, traces, far_in, near_in, y_two, y_one, z_two, z_one, coef, source, edge, part,
        stored_view, lift,
    )
    return (
        jnp.transpose(advanced, (0, 1, 3, 2, 4))[:, None],
        jnp.transpose(kernel, (1, 2, 0))[None],
    )


def solution(mesh):
    placed = (
        P(None, "gx", "gy", "gz", None, None),
        P(),
        P(),
        P(None, "gx", "gy", "gz"),
        P("gx", "gy", "gz", None, None),
        P("gx", "gy", "gz", None),
        P("gx", "gy", "gz", None),
    )
    return jax.shard_map(
        local,
        mesh=mesh,
        in_specs=placed,
        out_specs=(P(None, "gx", "gy", "gz", None, None), P("gx", "gy", "gz", None)),
        check_vma=False,
    )
```

```python
import jax
import jax.numpy as jnp
import numpy as np
from functools import partial
from jax import lax
from jax.experimental import pallas as pl
from jax.experimental.pallas import tpu as pltpu
from jax.sharding import PartitionSpec as P

NP = 8
FACE = NP * NP
LANES = 128
step_size = 0.15
stress_slot = ((3, 8, 7), (8, 4, 6), (7, 6, 5))
shear_pairs = ((6, 1, 2), (7, 0, 2), (8, 0, 1))
LIMIT = 20 * 1024 * 1024
PACK_LIMIT = 50 * 1024 * 1024


def trace_table():
    table = np.zeros((NP**3, 4 * FACE), np.float32)
    for first in range(NP):
        for second in range(NP):
            m = first * NP + second
            table[first * 64 + second, m] = 1.0
            table[first * 64 + 56 + second, FACE + m] = 1.0
            table[first * 64 + second * 8, 2 * FACE + m] = 1.0
            table[first * 64 + second * 8 + 7, 3 * FACE + m] = 1.0
    return table


def lane_index(shape):
    return lax.broadcasted_iota(jnp.int32, shape, len(shape) - 1)


def merged(forward, adjoint, upper):
    rows = forward.shape[:-1]
    flat = (-1, LANES)
    turned = pltpu.roll(adjoint.reshape(flat), FACE, 1)
    own = (lane_index(turned.shape) >= FACE) == upper
    return jnp.where(own, forward.reshape(flat), turned).reshape(rows + (LANES,))


def odd_position(axis):
    return lax.axis_index(axis) % 2 == 1


def pack_kernel(state_ref, held_ref, far_ref, near_ref, sem):
    odd = odd_position("gx")
    tiles = state_ref.shape[-1] // LANES
    order = [0, tiles - 1] + list(range(1, tiles - 1))

    def fetch(t):
        columns = pl.ds(t * LANES, LANES)
        return pltpu.make_async_copy(
            state_ref.at[:, :, :, :, columns], held_ref.at[:, :, :, :, columns], sem.at[t]
        )

    for t in order:
        fetch(t).start()
    for t in order[:2]:
        fetch(t).wait()
    low, high = slice(0, LANES), slice((tiles - 1) * LANES, tiles * LANES)
    for y in range(far_ref.shape[0]):
        down = merged(held_ref[0, y, :, :, low], held_ref[1, y, :, :, low], False)
        up = merged(held_ref[0, y, :, :, high], held_ref[1, y, :, :, high], True)
        far_ref[y] = jnp.where(odd, up, down)
        near_ref[y] = jnp.where(odd, down, up)
    for t in order[2:]:
        fetch(t).wait()


def pack_faces(state):
    _, count_y, fields, count_z, nodes = state.shape
    message = jax.ShapeDtypeStruct((count_y, fields, count_z, LANES), jnp.float32)
    return pl.pallas_call(
        pack_kernel,
        out_shape=(jax.ShapeDtypeStruct(state.shape, jnp.float32), message, message),
        in_specs=[pl.BlockSpec(memory_space=pl.ANY)],
        out_specs=(pl.BlockSpec(memory_space=pltpu.VMEM),) * 3,
        scratch_shapes=[pltpu.SemaphoreType.DMA((nodes // LANES,))],
        compiler_params=pltpu.CompilerParams(vmem_limit_bytes=PACK_LIMIT),
        cost_estimate=pl.CostEstimate(flops=10**6, bytes_accessed=2 * 10**6, transcendentals=0),
        name="pack_faces",
    )(state)


def trace_kernel(state_ref, table_ref, trace_ref, y_two, y_one, z_two, z_one):
    _, count_y, fields, count_z, _ = state_ref.shape

    def one_state(s, carry):
        values = state_ref[s].reshape(count_y * fields * count_z, -1)
        high = values.astype(jnp.bfloat16)
        low = (values - high.astype(jnp.float32)).astype(jnp.bfloat16)
        table = table_ref[...]
        picked = jnp.dot(high, table, preferred_element_type=jnp.float32)
        picked = picked + jnp.dot(low, table, preferred_element_type=jnp.float32)
        trace_ref[s] = picked.reshape(count_y, fields, count_z, 2 * LANES)
        return carry

    lax.fori_loop(0, 2, one_state, 0)
    odd_y = odd_position("gy")
    odd_z = odd_position("gz")
    end = count_y - 1
    down = merged(trace_ref[0, 0, :, :, :LANES], trace_ref[1, 0, :, :, :LANES], False)
    up = merged(trace_ref[0, end, :, :, :LANES], trace_ref[1, end, :, :, :LANES], True)
    y_two[...] = jnp.where(odd_y, up, down)
    y_one[...] = jnp.where(odd_y, down, up)
    for y in range(count_y):
        first = merged(trace_ref[0, y, :, 0, LANES:], trace_ref[1, y, :, 0, LANES:], False)
        last = merged(
            trace_ref[0, y, :, count_z - 1, LANES:], trace_ref[1, y, :, count_z - 1, LANES:], True
        )
        z_two[y] = jnp.where(odd_z, last, first)
        z_one[y] = jnp.where(odd_z, first, last)


def extract_traces(state, table):
    _, count_y, fields, count_z, nodes = state.shape
    f32 = jnp.float32
    y_message = jax.ShapeDtypeStruct((fields, count_z, LANES), f32)
    z_message = jax.ShapeDtypeStruct((count_y, fields, LANES), f32)
    return pl.pallas_call(
        trace_kernel,
        out_shape=(
            jax.ShapeDtypeStruct((2, count_y, fields, count_z, 2 * LANES), f32),
            y_message,
            y_message,
            z_message,
            z_message,
        ),
        in_specs=[pl.BlockSpec(memory_space=pltpu.VMEM)] * 2,
        out_specs=(pl.BlockSpec(memory_space=pltpu.VMEM),) * 5,
        compiler_params=pltpu.CompilerParams(vmem_limit_bytes=LIMIT),
        cost_estimate=pl.CostEstimate(flops=6 * 10**8, bytes_accessed=4 * 10**6, transcendentals=0),
        name="extract_traces",
    )(state, table)


def spread(columns, rows, pick):
    return lax.dot_general(
        columns,
        pick,
        (((0,), (0,)), ((), ())),
        precision=lax.Precision.HIGHEST,
        preferred_element_type=jnp.float32,
    )


def volume_kernel(
    state_ref, deriv_ref, material_ref, orient_ref, flags_ref,
    partial_ref, coef_ref, source_ref, edge_ref,
    low_ref, grad_ref, div_ref, wide_ref,
):
    _, count_y, fields, count_z, _ = state_ref.shape
    rows = 2 * count_y * count_z
    nodes = partial_ref.shape[-1]
    width = grad_ref.shape[-1]
    ends = [
        lax.axis_index("gy") == 0,
        lax.axis_index("gy") == lax.axis_size("gy") - 1,
        lax.axis_index("gz") == 0,
        lax.axis_index("gz") == lax.axis_size("gz") - 1,
    ]

    for f in range(fields):
        low_ref[f] = state_ref[:, :, f].reshape(rows, -1).astype(jnp.bfloat16)
    lanes = lane_index((3 * count_y, 3 * count_y * LANES))
    row = lax.broadcasted_iota(jnp.int32, lanes.shape, 0)
    pick = (lanes // LANES == row).astype(jnp.float32)
    medium = spread(material_ref[...].reshape(3 * count_y, count_z), 3 * count_y, pick)
    lanes = lane_index((6 * count_y, 3 * count_y * LANES))
    row = lax.broadcasted_iota(jnp.int32, lanes.shape, 0)
    block = lanes // LANES
    face = 2 * (block // count_y) + (lanes % LANES) // FACE
    pick = (face * count_y + block % count_y == row).astype(jnp.float32)
    codes = spread(
        orient_ref[...].reshape(6 * count_y, count_z).astype(jnp.float32), 6 * count_y, pick
    )
    kinds = spread(
        flags_ref[...].reshape(6 * count_y, count_z).astype(jnp.float32), 6 * count_y, pick
    )
    lane = lane_index((count_z, LANES))
    upper = lane >= FACE
    half_sign = jnp.where(upper, 0.5, -0.5)
    node = lane % FACE
    near, far = (node // NP, node % NP)
    z_pos = lax.broadcasted_iota(jnp.int32, lane.shape, 0)
    for y in range(count_y):
        lam = medium[:, y * LANES : (y + 1) * LANES]
        mu = medium[:, (count_y + y) * LANES : (count_y + y + 1) * LANES]
        rho = medium[:, (2 * count_y + y) * LANES : (2 * count_y + y + 1) * LANES]
        inv = 1.0 / rho
        wide_ref[0, y] = lam
        wide_ref[1, y] = mu
        wide_ref[2, y] = inv
        coef_ref[0, y] = half_sign * lam
        coef_ref[1, y] = half_sign * mu
        coef_ref[2, y] = half_sign * inv
        coef_ref[3, y] = 0.5 * jnp.sqrt((lam + 2.0 * mu) * inv)
        for d in range(3):
            at = (d * count_y + y) * LANES
            code = jnp.round(codes[:, at : at + LANES]).astype(jnp.int32)
            swap = code >= 4
            lead = jnp.where(swap, far, near)
            trail = jnp.where(swap, near, far)
            lead = jnp.where(code % 2 == 1, NP - 1 - lead, lead)
            trail = jnp.where((code // 2) % 2 == 1, NP - 1 - trail, trail)
            source_ref[d, y] = lead * NP + trail + jnp.where(upper, 0, FACE)
            if d > 0:
                free = jnp.where(jnp.round(kinds[:, at : at + LANES]) == 1.0, 1.0, 0.0)
                if d == 1:
                    low_end = (ends[0]) if y == 0 else False
                    high_end = (ends[1]) if y == count_y - 1 else False
                    rim = jnp.where(
                        upper,
                        jnp.where(high_end, 1.0, 0.0),
                        jnp.where(low_end, 1.0, 0.0),
                    )
                else:
                    low_rim = jnp.where(z_pos == 0, jnp.where(ends[2], 1.0, 0.0), 0.0)
                    high_rim = jnp.where(
                        z_pos == count_z - 1, jnp.where(ends[3], 1.0, 0.0), 0.0
                    )
                    rim = jnp.where(upper, high_rim, low_rim)
                edge_ref[d - 1, 0, y] = rim
                edge_ref[d - 1, 1, y] = free

    def columns_part(n, carry):
        base = n * width

        def operator(d):
            return deriv_ref[:, pl.ds(pl.multiple_of(d * nodes + base, LANES), width)]

        velocity = low_ref[0:3].reshape(3 * rows, nodes)
        for d in range(3):
            grad_ref[d] = jnp.dot(velocity, operator(d), preferred_element_type=jnp.float32)
        total = None
        for d in range(3):
            stress = jnp.concatenate([low_ref[stress_slot[i][d]] for i in range(3)], axis=0)
            part = jnp.dot(stress, operator(d), preferred_element_type=jnp.float32)
            total = part if total is None else total + part
        div_ref[...] = total
        for s in range(2):
            scale = step_size if s == 0 else -step_size
            for y in range(count_y):
                at = (s * count_y + y) * count_z
                lam = scale * wide_ref[0, y]
                mu = scale * wide_ref[1, y]
                inv = scale * wide_ref[2, y]
                for tile in range(width // LANES):
                    columns = slice(tile * LANES, (tile + 1) * LANES)
                    where = pl.ds(pl.multiple_of(base + tile * LANES, LANES), LANES)

                    def g(d, i):
                        return grad_ref[d, i * rows + at : i * rows + at + count_z, columns]

                    def put(f, term):
                        partial_ref[s, y, f, :, where] = state_ref[s, y, f, :, where] + term

                    for i in range(3):
                        put(i, inv * div_ref[i * rows + at : i * rows + at + count_z, columns])
                    diag = [g(i, i) for i in range(3)]
                    common = lam * (diag[0] + diag[1] + diag[2])
                    for i in range(3):
                        put(3 + i, common + (mu + mu) * diag[i])
                    for f, i, j in shear_pairs:
                        put(f, mu * (g(j, i) + g(i, j)))
        return carry

    lax.fori_loop(0, nodes // width, columns_part, 0)


def volume(state, deriv, material, orient, flags):
    _, count_y, fields, count_z, nodes = state.shape
    f32 = jnp.float32
    width = 256
    rows = 2 * count_y * count_z
    outs = (
        jax.ShapeDtypeStruct(state.shape, f32),
        jax.ShapeDtypeStruct((4, count_y, count_z, LANES), f32),
        jax.ShapeDtypeStruct((3, count_y, count_z, LANES), jnp.int32),
        jax.ShapeDtypeStruct((2, 2, count_y, count_z, LANES), f32),
    )
    return pl.pallas_call(
        volume_kernel,
        out_shape=outs,
        in_specs=[pl.BlockSpec(memory_space=pltpu.VMEM)] * 5,
        out_specs=(pl.BlockSpec(memory_space=pltpu.VMEM),) * 4,
        scratch_shapes=[
            pltpu.VMEM((fields, rows, nodes), jnp.bfloat16),
            pltpu.VMEM((3, 3 * rows, width), f32),
            pltpu.VMEM((3 * rows, width), f32),
            pltpu.VMEM((3, count_y, count_z, LANES), f32),
        ],
        compiler_params=pltpu.CompilerParams(vmem_limit_bytes=LIMIT),
        cost_estimate=pl.CostEstimate(
            flops=10**6, bytes_accessed=10**5, transcendentals=0
        ),
        name="volume",
    )(state, deriv, material, orient, flags)


def face_flux(jumps, d, coefs):
    lam, mu, inv, speed = coefs
    flux = [speed * jump for jump in jumps]
    for i in range(3):
        flux[i] = flux[i] + inv * jumps[stress_slot[i][d]]
    common = lam * jumps[d]
    for i in range(3):
        flux[3 + i] = flux[3 + i] + common
    for i, j, f in ((0, 0, 3), (1, 1, 4), (2, 2, 5), (1, 2, 6), (0, 2, 7), (0, 1, 8)):
        if j == d:
            flux[f] = flux[f] + mu * jumps[i]
        if i == d:
            flux[f] = flux[f] + mu * jumps[j]
    return [term.astype(jnp.bfloat16) for term in flux]


def side_kernel(
    trace_ref, y_two, y_one, z_two, z_one, coef_ref, source_ref, edge_ref, stored_ref,
    flux_ref, sum_ref,
):
    _, count_y, fields, count_z, _ = trace_ref.shape
    last_y = count_y - 1
    odd_y = odd_position("gy")
    odd_z = odd_position("gz")
    lane = lane_index((count_z, LANES))
    upper = lane >= FACE
    z_pos = lax.broadcasted_iota(jnp.int32, lane.shape, 0)

    def row(y, carry):
        below = jnp.maximum(y - 1, 0)
        above = jnp.minimum(y + 1, last_y)
        coefs = [coef_ref[k, y] for k in range(4)]
        for s in range(2):
            for d in (1, 2):
                source = source_ref[d, y]
                rim = edge_ref[d - 1, 0, y] > 0.0
                free = edge_ref[d - 1, 1, y]
                keep_velocity = free - 1.0
                keep_stress = -free - 1.0
                half = slice((d - 1) * LANES, d * LANES)
                jumps = []
                for f in range(fields):
                    inside = trace_ref[s, y, f, :, half]
                    if d == 1:
                        two, one = (y_two[f], y_one[f])
                        odd = odd_y
                    else:
                        two = jnp.broadcast_to(z_two[y, f : f + 1, :], lane.shape)
                        one = jnp.broadcast_to(z_one[y, f : f + 1, :], lane.shape)
                        odd = odd_z
                    from_below = jnp.where(odd, one, two)
                    from_above = jnp.where(odd, two, one)
                    if s == 1:
                        from_below = pltpu.roll(from_below, FACE, 1)
                        from_above = pltpu.roll(from_above, FACE, 1)
                    if d == 1:
                        lower = jnp.where(y == 0, from_below, trace_ref[s, below, f, :, half])
                        higher = jnp.where(y == last_y, from_above, trace_ref[s, above, f, :, half])
                    else:
                        lower = jnp.where(z_pos == 0, from_below, pltpu.roll(inside, 1, 0))
                        higher = jnp.where(
                            z_pos == count_z - 1, from_above, pltpu.roll(inside, count_z - 1, 0)
                        )
                    mixed = jnp.where(upper, lower, higher)
                    jump = jnp.take_along_axis(mixed, source, axis=1) - inside
                    keep = keep_velocity if f < 3 else keep_stress
                    jump = jnp.where(rim, inside * keep, jump)
                    jumps.append(jump)
                    if s == 1:
                        term = stored_ref[y, f, :, d * LANES : (d + 1) * LANES] * jump
                        if d == 1:
                            sum_ref[y, f] = term
                        else:
                            sum_ref[y, f] += term
                for f, term in enumerate(face_flux(jumps, d, coefs)):
                    flux_ref[y, s, f, :, half] = term
        return carry

    lax.fori_loop(0, count_y, row, 0)


def side_faces(traces, y_two, y_one, z_two, z_one, coef, source, edge, stored):
    _, count_y, fields, count_z, _ = traces.shape
    return pl.pallas_call(
        side_kernel,
        out_shape=(
            jax.ShapeDtypeStruct((count_y, 2, fields, count_z, 2 * LANES), jnp.bfloat16),
            jax.ShapeDtypeStruct((count_y, fields, count_z, LANES), jnp.float32),
        ),
        in_specs=[pl.BlockSpec(memory_space=pltpu.VMEM)] * 9,
        out_specs=(pl.BlockSpec(memory_space=pltpu.VMEM),) * 2,
        compiler_params=pltpu.CompilerParams(vmem_limit_bytes=LIMIT),
        cost_estimate=pl.CostEstimate(flops=10**6, bytes_accessed=10**5, transcendentals=0),
        name="side_faces",
    )(traces, y_two, y_one, z_two, z_one, coef, source, edge, stored)


def final_kernel(
    state_ref, far_ref, near_ref, coef_ref, source_ref, side_ref, side_sum_ref, partial_ref,
    stored_ref, lift_ref,
    advanced_ref, kernel_ref,
    flux_ref, out_ref, out_sem,
):
    _, count_y, fields, count_z, nodes = state_ref.shape
    lane = lane_index((count_z, LANES))
    upper = lane >= FACE
    z_pos = lax.broadcasted_iota(jnp.int32, lane.shape, 0)
    take_near = upper == odd_position("gx")

    def write(s, y):
        return pltpu.make_async_copy(out_ref.at[s, y], advanced_ref.at[s, y], out_sem.at[s, y])

    def row(y, carry):
        coefs = [coef_ref[k, y] for k in range(4)]
        for s in range(2):
            source = source_ref[0, y]
            if s == 1:
                source = (source + FACE) % LANES
            jumps = []
            for f in range(fields):
                inside = jnp.where(
                    upper, state_ref[s, y, f, :, nodes - LANES :], state_ref[s, y, f, :, :LANES]
                )
                near, far = (near_ref[y, f], far_ref[y, f])
                if s == 1:
                    near, far = (far, near)
                mixed = jnp.where(take_near, near, far)
                jump = jnp.take_along_axis(mixed, source, axis=1) - inside
                jumps.append(jump)
                if s == 1:
                    terms = side_sum_ref[y, f] + stored_ref[y, f, :, :LANES] * jump
                    sums = jnp.sum(terms, axis=1, keepdims=True) * (1.0 / FACE)
                    across = jnp.sum(jnp.where(z_pos == lane, sums, 0.0), axis=0, keepdims=True)
                    kernel_ref[f, pl.ds(y, 1), :] = across[:, :count_z]
            for f, term in enumerate(face_flux(jumps, 0, coefs)):
                flux_ref[s, f] = term
        lifted = jnp.dot(
            side_ref[y].reshape(2 * fields * count_z, 2 * LANES),
            lift_ref[LANES:],
            preferred_element_type=jnp.float32,
        ) + jnp.dot(
            flux_ref[...].reshape(2 * fields * count_z, LANES),
            lift_ref[:LANES],
            preferred_element_type=jnp.float32,
        )
        lifted = lifted.reshape(2, fields, count_z, nodes)
        for s in range(2):
            scale = step_size if s == 0 else -step_size
            out_ref[s, y] = partial_ref[s, y] + scale * lifted[s]
            write(s, y).start()
        return carry

    lax.fori_loop(0, count_y, row, 0)
    for y in range(count_y):
        for s in range(2):
            write(s, y).wait()


def finish(state, far, near, coef, source, side, side_sum, part, stored, lift):
    _, count_y, fields, count_z, nodes = state.shape
    f32 = jnp.float32
    outs = (
        jax.ShapeDtypeStruct(state.shape, f32),
        jax.ShapeDtypeStruct((fields, count_y, count_z), f32),
    )
    return pl.pallas_call(
        final_kernel,
        out_shape=outs,
        in_specs=[pl.BlockSpec(memory_space=pltpu.VMEM)] * 10,
        out_specs=(pl.BlockSpec(memory_space=pl.ANY), pl.BlockSpec(memory_space=pltpu.VMEM)),
        scratch_shapes=[
            pltpu.VMEM((2, fields, count_z, LANES), jnp.bfloat16),
            pltpu.VMEM(state.shape, f32),
            pltpu.SemaphoreType.DMA((2, count_y)),
        ],
        compiler_params=pltpu.CompilerParams(vmem_limit_bytes=LIMIT),
        cost_estimate=pl.CostEstimate(flops=9 * 10**8, bytes_accessed=10**7, transcendentals=0),
        name="finish",
    )(state, far, near, coef, source, side, side_sum, part, stored, lift)


def swaps(count, start, wrap):
    pairs = []
    for i in range(start, count if wrap else count - 1, 2):
        j = (i + 1) % count
        pairs += [(i, j), (j, i)]
    return pairs


def inner_swaps(count_y, count_z):
    pairs = []
    for y in range(count_y):
        for z in range(count_z):
            if z in (0, count_z - 1):
                target = (y ^ 1, z)
            else:
                target = (y, z + 1 if z % 2 == 1 else z - 1)
            pairs.append((y * count_z + z, target[0] * count_z + target[1]))
    return pairs


def local(state, deriv, lift, material, stored, orient, flags):
    view = jnp.transpose(state[:, 0], (0, 1, 3, 2, 4))
    stored_view = jnp.transpose(stored[0], (0, 2, 1, 3))
    orient_view = jnp.transpose(orient[0], (2, 0, 1))
    flags_view = jnp.transpose(flags[0], (2, 0, 1))
    nx, ny, nz = (lax.axis_size(a) for a in ("gx", "gy", "gz"))
    table = jnp.asarray(trace_table(), jnp.bfloat16)
    view, far, near = pack_faces(view)
    far_in = lax.ppermute(far, "gx", swaps(nx, 1, True))
    near_in = lax.ppermute(near, "gx", swaps(nx, 0, True))
    traces, y_two, y_one, z_two, z_one = extract_traces(view, table)
    y_one = lax.ppermute(y_one, "gy", swaps(ny, 0, False))
    y_two = lax.ppermute(y_two, "gy", swaps(ny, 1, True))
    z_one = lax.ppermute(z_one, "gz", swaps(nz, 0, False))
    medium = material[:, 0]
    z_two, medium, y_one = lax.optimization_barrier((z_two, medium, y_one))
    z_two = lax.ppermute(z_two, ("gy", "gz"), inner_swaps(ny, nz))
    part, coef, source, edge = volume(view, deriv, medium, orient_view, flags_view)
    side, side_sum = side_faces(
        traces, y_two, y_one, z_two, z_one, coef, source, edge, stored_view
    )
    advanced, kernel = finish(
        view, far_in, near_in, coef, source, side, side_sum, part, stored_view, lift
    )
    return (
        jnp.transpose(advanced, (0, 1, 3, 2, 4))[:, None],
        jnp.transpose(kernel, (1, 2, 0))[None],
    )


def solution(mesh):
    placed = (
        P(None, "gx", "gy", "gz", None, None),
        P(),
        P(),
        P(None, "gx", "gy", "gz"),
        P("gx", "gy", "gz", None, None),
        P("gx", "gy", "gz", None),
        P("gx", "gy", "gz", None),
    )
    return jax.shard_map(
        local,
        mesh=mesh,
        in_specs=placed,
        out_specs=(P(None, "gx", "gy", "gz", None, None), P("gx", "gy", "gz", None)),
        check_vma=False,
    )
```

```python
import jax
import jax.numpy as jnp
import numpy as np
from functools import partial
from jax import lax
from jax.experimental import pallas as pl
from jax.experimental.pallas import tpu as pltpu
from jax.sharding import PartitionSpec as P

NP = 8
FACE = NP * NP
LANES = 128
step_size = 0.15
stress_slot = ((3, 8, 7), (8, 4, 6), (7, 6, 5))
shear_pairs = ((6, 1, 2), (7, 0, 2), (8, 0, 1))
LIMIT = 20 * 1024 * 1024
PACK_LIMIT = 50 * 1024 * 1024


def trace_table():
    table = np.zeros((NP**3, 4 * FACE), np.float32)
    for first in range(NP):
        for second in range(NP):
            m = first * NP + second
            table[first * 64 + second, m] = 1.0
            table[first * 64 + 56 + second, FACE + m] = 1.0
            table[first * 64 + second * 8, 2 * FACE + m] = 1.0
            table[first * 64 + second * 8 + 7, 3 * FACE + m] = 1.0
    return table


def lane_index(shape):
    return lax.broadcasted_iota(jnp.int32, shape, len(shape) - 1)


def merged(forward, adjoint, upper):
    rows = forward.shape[:-1]
    flat = (-1, LANES)
    turned = pltpu.roll(adjoint.reshape(flat), FACE, 1)
    own = (lane_index(turned.shape) >= FACE) == upper
    return jnp.where(own, forward.reshape(flat), turned).reshape(rows + (LANES,))


def odd_position(axis):
    return lax.axis_index(axis) % 2 == 1


def pack_kernel(state_ref, held_ref, far_ref, near_ref, sem):
    odd = odd_position("gx")
    tiles = state_ref.shape[-1] // LANES
    order = [0, tiles - 1] + list(range(1, tiles - 1))

    def fetch(t):
        columns = pl.ds(t * LANES, LANES)
        return pltpu.make_async_copy(
            state_ref.at[:, :, :, :, columns], held_ref.at[:, :, :, :, columns], sem.at[t]
        )

    for t in order:
        fetch(t).start()
    for t in order[:2]:
        fetch(t).wait()
    low, high = slice(0, LANES), slice((tiles - 1) * LANES, tiles * LANES)
    for y in range(far_ref.shape[0]):
        down = merged(held_ref[0, y, :, :, low], held_ref[1, y, :, :, low], False)
        up = merged(held_ref[0, y, :, :, high], held_ref[1, y, :, :, high], True)
        far_ref[y] = jnp.where(odd, up, down)
        near_ref[y] = jnp.where(odd, down, up)
    for t in order[2:]:
        fetch(t).wait()


def pack_faces(state):
    _, count_y, fields, count_z, nodes = state.shape
    message = jax.ShapeDtypeStruct((count_y, fields, count_z, LANES), jnp.float32)
    return pl.pallas_call(
        pack_kernel,
        out_shape=(jax.ShapeDtypeStruct(state.shape, jnp.float32), message, message),
        in_specs=[pl.BlockSpec(memory_space=pl.ANY)],
        out_specs=(pl.BlockSpec(memory_space=pltpu.VMEM),) * 3,
        scratch_shapes=[pltpu.SemaphoreType.DMA((nodes // LANES,))],
        compiler_params=pltpu.CompilerParams(vmem_limit_bytes=PACK_LIMIT),
        cost_estimate=pl.CostEstimate(flops=10**6, bytes_accessed=2 * 10**6, transcendentals=0),
        name="pack_faces",
    )(state)


def trace_kernel(state_ref, table_ref, trace_ref, y_two, y_one, z_two, z_one):
    _, count_y, fields, count_z, _ = state_ref.shape

    def one_state(s, carry):
        values = state_ref[s].reshape(count_y * fields * count_z, -1)
        high = values.astype(jnp.bfloat16)
        low = (values - high.astype(jnp.float32)).astype(jnp.bfloat16)
        table = table_ref[...]
        picked = jnp.dot(high, table, preferred_element_type=jnp.float32)
        picked = picked + jnp.dot(low, table, preferred_element_type=jnp.float32)
        trace_ref[s] = picked.reshape(count_y, fields, count_z, 2 * LANES)
        return carry

    lax.fori_loop(0, 2, one_state, 0)
    odd_y = odd_position("gy")
    odd_z = odd_position("gz")
    end = count_y - 1
    down = merged(trace_ref[0, 0, :, :, :LANES], trace_ref[1, 0, :, :, :LANES], False)
    up = merged(trace_ref[0, end, :, :, :LANES], trace_ref[1, end, :, :, :LANES], True)
    y_two[...] = jnp.where(odd_y, up, down)
    y_one[...] = jnp.where(odd_y, down, up)
    for s in range(2):
        for y in range(count_y):
            first = trace_ref[s, y, :, 0, LANES:]
            last = trace_ref[s, y, :, count_z - 1, LANES:]
            z_two[s, y] = jnp.where(odd_z, last, first)
            z_one[s, y] = jnp.where(odd_z, first, last)


def extract_traces(state, table):
    _, count_y, fields, count_z, nodes = state.shape
    f32 = jnp.float32
    y_message = jax.ShapeDtypeStruct((fields, count_z, LANES), f32)
    z_message = jax.ShapeDtypeStruct((2, count_y, fields, LANES), f32)
    return pl.pallas_call(
        trace_kernel,
        out_shape=(
            jax.ShapeDtypeStruct((2, count_y, fields, count_z, 2 * LANES), f32),
            y_message,
            y_message,
            z_message,
            z_message,
        ),
        in_specs=[pl.BlockSpec(memory_space=pltpu.VMEM)] * 2,
        out_specs=(pl.BlockSpec(memory_space=pltpu.VMEM),) * 5,
        compiler_params=pltpu.CompilerParams(vmem_limit_bytes=LIMIT),
        cost_estimate=pl.CostEstimate(flops=6 * 10**8, bytes_accessed=4 * 10**6, transcendentals=0),
        name="extract_traces",
    )(state, table)


def spread(columns, rows, pick):
    return lax.dot_general(
        columns,
        pick,
        (((0,), (0,)), ((), ())),
        precision=lax.Precision.HIGHEST,
        preferred_element_type=jnp.float32,
    )


def volume_kernel(
    state_ref, deriv_ref, material_ref, orient_ref, flags_ref,
    partial_ref, coef_ref, source_ref, edge_ref,
    low_ref, grad_ref, div_ref, wide_ref,
):
    _, count_y, fields, count_z, _ = state_ref.shape
    rows = 2 * count_y * count_z
    nodes = partial_ref.shape[-1]
    width = grad_ref.shape[-1]
    ends = [
        lax.axis_index("gy") == 0,
        lax.axis_index("gy") == lax.axis_size("gy") - 1,
        lax.axis_index("gz") == 0,
        lax.axis_index("gz") == lax.axis_size("gz") - 1,
    ]

    for f in range(fields):
        low_ref[f] = state_ref[:, :, f].reshape(rows, -1).astype(jnp.bfloat16)
    lanes = lane_index((3 * count_y, 3 * count_y * LANES))
    row = lax.broadcasted_iota(jnp.int32, lanes.shape, 0)
    pick = (lanes // LANES == row).astype(jnp.float32)
    medium = spread(material_ref[...].reshape(3 * count_y, count_z), 3 * count_y, pick)
    lanes = lane_index((6 * count_y, 3 * count_y * LANES))
    row = lax.broadcasted_iota(jnp.int32, lanes.shape, 0)
    block = lanes // LANES
    face = 2 * (block // count_y) + (lanes % LANES) // FACE
    pick = (face * count_y + block % count_y == row).astype(jnp.float32)
    codes = spread(
        orient_ref[...].reshape(6 * count_y, count_z).astype(jnp.float32), 6 * count_y, pick
    )
    kinds = spread(
        flags_ref[...].reshape(6 * count_y, count_z).astype(jnp.float32), 6 * count_y, pick
    )
    lane = lane_index((count_z, LANES))
    upper = lane >= FACE
    half_sign = jnp.where(upper, 0.5, -0.5)
    node = lane % FACE
    near, far = (node // NP, node % NP)
    z_pos = lax.broadcasted_iota(jnp.int32, lane.shape, 0)
    for y in range(count_y):
        lam = medium[:, y * LANES : (y + 1) * LANES]
        mu = medium[:, (count_y + y) * LANES : (count_y + y + 1) * LANES]
        rho = medium[:, (2 * count_y + y) * LANES : (2 * count_y + y + 1) * LANES]
        inv = 1.0 / rho
        wide_ref[0, y] = lam
        wide_ref[1, y] = mu
        wide_ref[2, y] = inv
        coef_ref[0, y] = half_sign * lam
        coef_ref[1, y] = half_sign * mu
        coef_ref[2, y] = half_sign * inv
        coef_ref[3, y] = 0.5 * jnp.sqrt((lam + 2.0 * mu) * inv)
        for d in range(3):
            at = (d * count_y + y) * LANES
            code = jnp.round(codes[:, at : at + LANES]).astype(jnp.int32)
            swap = code >= 4
            lead = jnp.where(swap, far, near)
            trail = jnp.where(swap, near, far)
            lead = jnp.where(code % 2 == 1, NP - 1 - lead, lead)
            trail = jnp.where((code // 2) % 2 == 1, NP - 1 - trail, trail)
            source_ref[d, y] = lead * NP + trail + jnp.where(upper, 0, FACE)
            if d > 0:
                free = jnp.where(jnp.round(kinds[:, at : at + LANES]) == 1.0, 1.0, 0.0)
                if d == 1:
                    low_end = (ends[0]) if y == 0 else False
                    high_end = (ends[1]) if y == count_y - 1 else False
                    rim = jnp.where(
                        upper,
                        jnp.where(high_end, 1.0, 0.0),
                        jnp.where(low_end, 1.0, 0.0),
                    )
                else:
                    low_rim = jnp.where(z_pos == 0, jnp.where(ends[2], 1.0, 0.0), 0.0)
                    high_rim = jnp.where(
                        z_pos == count_z - 1, jnp.where(ends[3], 1.0, 0.0), 0.0
                    )
                    rim = jnp.where(upper, high_rim, low_rim)
                edge_ref[d - 1, 0, y] = rim
                edge_ref[d - 1, 1, y] = free

    def columns_part(n, carry):
        base = n * width

        def operator(d):
            return deriv_ref[:, pl.ds(pl.multiple_of(d * nodes + base, LANES), width)]

        velocity = low_ref[0:3].reshape(3 * rows, nodes)
        for d in range(3):
            grad_ref[d] = jnp.dot(velocity, operator(d), preferred_element_type=jnp.float32)
        total = None
        for d in range(3):
            stress = jnp.concatenate([low_ref[stress_slot[i][d]] for i in range(3)], axis=0)
            part = jnp.dot(stress, operator(d), preferred_element_type=jnp.float32)
            total = part if total is None else total + part
        div_ref[...] = total
        for s in range(2):
            scale = step_size if s == 0 else -step_size
            for y in range(count_y):
                at = (s * count_y + y) * count_z
                lam = scale * wide_ref[0, y]
                mu = scale * wide_ref[1, y]
                inv = scale * wide_ref[2, y]
                for tile in range(width // LANES):
                    columns = slice(tile * LANES, (tile + 1) * LANES)
                    where = pl.ds(pl.multiple_of(base + tile * LANES, LANES), LANES)

                    def g(d, i):
                        return grad_ref[d, i * rows + at : i * rows + at + count_z, columns]

                    def put(f, term):
                        partial_ref[s, y, f, :, where] = state_ref[s, y, f, :, where] + term

                    for i in range(3):
                        put(i, inv * div_ref[i * rows + at : i * rows + at + count_z, columns])
                    diag = [g(i, i) for i in range(3)]
                    common = lam * (diag[0] + diag[1] + diag[2])
                    for i in range(3):
                        put(3 + i, common + (mu + mu) * diag[i])
                    for f, i, j in shear_pairs:
                        put(f, mu * (g(j, i) + g(i, j)))
        return carry

    lax.fori_loop(0, nodes // width, columns_part, 0)


def volume(state, deriv, material, orient, flags):
    _, count_y, fields, count_z, nodes = state.shape
    f32 = jnp.float32
    width = 256
    rows = 2 * count_y * count_z
    outs = (
        jax.ShapeDtypeStruct(state.shape, f32),
        jax.ShapeDtypeStruct((4, count_y, count_z, LANES), f32),
        jax.ShapeDtypeStruct((3, count_y, count_z, LANES), jnp.int32),
        jax.ShapeDtypeStruct((2, 2, count_y, count_z, LANES), f32),
    )
    return pl.pallas_call(
        volume_kernel,
        out_shape=outs,
        in_specs=[pl.BlockSpec(memory_space=pltpu.VMEM)] * 5,
        out_specs=(pl.BlockSpec(memory_space=pltpu.VMEM),) * 4,
        scratch_shapes=[
            pltpu.VMEM((fields, rows, nodes), jnp.bfloat16),
            pltpu.VMEM((3, 3 * rows, width), f32),
            pltpu.VMEM((3 * rows, width), f32),
            pltpu.VMEM((3, count_y, count_z, LANES), f32),
        ],
        compiler_params=pltpu.CompilerParams(vmem_limit_bytes=LIMIT),
        cost_estimate=pl.CostEstimate(
            flops=10**6, bytes_accessed=10**5, transcendentals=0
        ),
        name="volume",
    )(state, deriv, material, orient, flags)


def face_flux(jumps, d, coefs):
    lam, mu, inv, speed = coefs
    flux = [speed * jump for jump in jumps]
    for i in range(3):
        flux[i] = flux[i] + inv * jumps[stress_slot[i][d]]
    common = lam * jumps[d]
    for i in range(3):
        flux[3 + i] = flux[3 + i] + common
    for i, j, f in ((0, 0, 3), (1, 1, 4), (2, 2, 5), (1, 2, 6), (0, 2, 7), (0, 1, 8)):
        if j == d:
            flux[f] = flux[f] + mu * jumps[i]
        if i == d:
            flux[f] = flux[f] + mu * jumps[j]
    return [term.astype(jnp.bfloat16) for term in flux]


def rim_jump(turned, inside, edge, f):
    rim, free = edge
    keep = free - 1.0 if f < 3 else -free - 1.0
    return jnp.where(rim > 0.0, inside * keep, turned - inside)


def side_kernel(
    trace_ref, z_two, z_one, coef_ref, source_ref, edge_ref, stored_ref, flux_ref, sum_ref
):
    _, count_y, fields, count_z, _ = trace_ref.shape
    last_y = count_y - 1
    odd_z = odd_position("gz")
    lane = lane_index((count_z, LANES))
    upper = lane >= FACE
    z_pos = lax.broadcasted_iota(jnp.int32, lane.shape, 0)
    at_low = jnp.logical_and(z_pos == 0, upper)
    at_high = jnp.logical_and(z_pos == count_z - 1, jnp.logical_not(upper))

    def row(y, carry):
        coefs = [coef_ref[k, y] for k in range(4)]
        edge = (edge_ref[1, 0, y], edge_ref[1, 1, y])
        source = source_ref[2, y]
        for s in range(2):
            jumps = []
            for f in range(fields):
                inside = trace_ref[s, y, f, :, LANES:]
                two = z_two[s, y, f : f + 1, :]
                one = z_one[s, y, f : f + 1, :]
                from_below = jnp.where(odd_z, one, two)
                from_above = jnp.where(odd_z, two, one)
                mixed = jnp.where(upper, pltpu.roll(inside, 1, 0), pltpu.roll(inside, count_z - 1, 0))
                mixed = jnp.where(at_low, from_below, jnp.where(at_high, from_above, mixed))
                turned = jnp.take_along_axis(mixed, source, axis=1)
                jump = rim_jump(turned, inside, edge, f)
                jumps.append(jump)
                if s == 1:
                    sum_ref[y, f] = stored_ref[y, f, :, 2 * LANES :] * jump
            for f, term in enumerate(face_flux(jumps, 2, coefs)):
                flux_ref[y, s, f, :, LANES:] = term

        @pl.when(jnp.logical_and(y > 0, y < last_y))
        def _():
            turn = source_ref[1, y]
            for s in range(2):
                jumps = []
                for f in range(fields):
                    inside = trace_ref[s, y, f, :, :LANES]
                    mixed = jnp.where(
                        upper, trace_ref[s, y - 1, f, :, :LANES], trace_ref[s, y + 1, f, :, :LANES]
                    )
                    jump = jnp.take_along_axis(mixed, turn, axis=1) - inside
                    jumps.append(jump)
                    if s == 1:
                        sum_ref[y, f] += stored_ref[y, f, :, LANES : 2 * LANES] * jump
                for f, term in enumerate(face_flux(jumps, 1, coefs)):
                    flux_ref[y, s, f, :, :LANES] = term

        return carry

    lax.fori_loop(0, count_y, row, 0)


def side_faces(traces, z_two, z_one, coef, source, edge, stored):
    _, count_y, fields, count_z, _ = traces.shape
    return pl.pallas_call(
        side_kernel,
        out_shape=(
            jax.ShapeDtypeStruct((count_y, 2, fields, count_z, 2 * LANES), jnp.bfloat16),
            jax.ShapeDtypeStruct((count_y, fields, count_z, LANES), jnp.float32),
        ),
        in_specs=[pl.BlockSpec(memory_space=pltpu.VMEM)] * 7,
        out_specs=(pl.BlockSpec(memory_space=pltpu.VMEM),) * 2,
        compiler_params=pltpu.CompilerParams(vmem_limit_bytes=LIMIT),
        cost_estimate=pl.CostEstimate(flops=10**6, bytes_accessed=10**5, transcendentals=0),
        name="side_faces",
    )(traces, z_two, z_one, coef, source, edge, stored)


def final_kernel(
    state_ref, trace_ref, far_ref, near_ref, y_two, y_one, coef_ref, source_ref, edge_ref,
    side_ref, side_sum_ref, partial_ref, stored_ref, lift_ref,
    advanced_ref, kernel_ref,
    flux_ref, sum_ref, out_ref, out_sem,
):
    _, count_y, fields, count_z, nodes = state_ref.shape
    last_y = count_y - 1
    lane = lane_index((count_z, LANES))
    upper = lane >= FACE
    z_pos = lax.broadcasted_iota(jnp.int32, lane.shape, 0)
    take_near = upper == odd_position("gx")
    odd_y = odd_position("gy")

    def write(s, y):
        return pltpu.make_async_copy(out_ref.at[s, y], advanced_ref.at[s, y], out_sem.at[s, y])

    def row(y, carry):
        coefs = [coef_ref[k, y] for k in range(4)]
        for s in range(2):
            source = source_ref[0, y]
            if s == 1:
                source = (source + FACE) % LANES
            jumps = []
            for f in range(fields):
                inside = jnp.where(
                    upper, state_ref[s, y, f, :, nodes - LANES :], state_ref[s, y, f, :, :LANES]
                )
                near, far = (near_ref[y, f], far_ref[y, f])
                if s == 1:
                    near, far = (far, near)
                mixed = jnp.where(take_near, near, far)
                jump = jnp.take_along_axis(mixed, source, axis=1) - inside
                jumps.append(jump)
                if s == 1:
                    sum_ref[f] = side_sum_ref[y, f] + stored_ref[y, f, :, :LANES] * jump
            for f, term in enumerate(face_flux(jumps, 0, coefs)):
                flux_ref[s, f, :, :LANES] = term
        at_rim = jnp.logical_or(y == 0, y == last_y)

        @pl.when(jnp.logical_not(at_rim))
        def _():
            flux_ref[:, :, :, LANES:] = side_ref[y, :, :, :, :LANES]

        @pl.when(at_rim)
        def _():
            edge = (edge_ref[0, 0, y], edge_ref[0, 1, y])
            turn = source_ref[1, y]
            first = y == 0
            take_two = jnp.logical_xor(first, odd_y)
            outer = upper == first
            inner_row = jnp.where(first, jnp.minimum(1, last_y), last_y - 1)
            for s in range(2):
                jumps = []
                for f in range(fields):
                    received = jnp.where(take_two, y_two[f], y_one[f])
                    if s == 1:
                        received = pltpu.roll(received, FACE, 1)
                    inside = trace_ref[s, y, f, :, :LANES]
                    mixed = jnp.where(outer, received, trace_ref[s, inner_row, f, :, :LANES])
                    turned = jnp.take_along_axis(mixed, turn, axis=1)
                    jump = rim_jump(turned, inside, edge, f)
                    jumps.append(jump)
                    if s == 1:
                        sum_ref[f] += stored_ref[y, f, :, LANES : 2 * LANES] * jump
                for f, term in enumerate(face_flux(jumps, 1, coefs)):
                    flux_ref[s, f, :, LANES:] = term

        lifted = jnp.dot(
            flux_ref[...].reshape(2 * fields * count_z, 2 * LANES),
            lift_ref[: 2 * LANES],
            preferred_element_type=jnp.float32,
        ) + jnp.dot(
            side_ref[y, :, :, :, LANES:].reshape(2 * fields * count_z, LANES),
            lift_ref[2 * LANES :],
            preferred_element_type=jnp.float32,
        )
        lifted = lifted.reshape(2, fields, count_z, nodes)
        for s in range(2):
            scale = step_size if s == 0 else -step_size
            out_ref[s, y] = partial_ref[s, y] + scale * lifted[s]
            write(s, y).start()
        for f in range(fields):
            sums = jnp.sum(sum_ref[f], axis=1, keepdims=True) * (1.0 / FACE)
            across = jnp.sum(jnp.where(z_pos == lane, sums, 0.0), axis=0, keepdims=True)
            kernel_ref[f, pl.ds(y, 1), :] = across[:, :count_z]
        return carry

    lax.fori_loop(0, count_y, row, 0)
    for y in range(count_y):
        for s in range(2):
            write(s, y).wait()


def finish(
    state, traces, far, near, y_two, y_one, coef, source, edge, side, side_sum, part, stored, lift
):
    _, count_y, fields, count_z, nodes = state.shape
    f32 = jnp.float32
    outs = (
        jax.ShapeDtypeStruct(state.shape, f32),
        jax.ShapeDtypeStruct((fields, count_y, count_z), f32),
    )
    return pl.pallas_call(
        final_kernel,
        out_shape=outs,
        in_specs=[pl.BlockSpec(memory_space=pltpu.VMEM)] * 14,
        out_specs=(pl.BlockSpec(memory_space=pl.ANY), pl.BlockSpec(memory_space=pltpu.VMEM)),
        scratch_shapes=[
            pltpu.VMEM((2, fields, count_z, 2 * LANES), jnp.bfloat16),
            pltpu.VMEM((fields, count_z, LANES), f32),
            pltpu.VMEM(state.shape, f32),
            pltpu.SemaphoreType.DMA((2, count_y)),
        ],
        compiler_params=pltpu.CompilerParams(vmem_limit_bytes=LIMIT),
        cost_estimate=pl.CostEstimate(flops=9 * 10**8, bytes_accessed=10**7, transcendentals=0),
        name="finish",
    )(state, traces, far, near, y_two, y_one, coef, source, edge, side, side_sum, part, stored, lift)


def swaps(count, start, wrap):
    pairs = []
    for i in range(start, count if wrap else count - 1, 2):
        j = (i + 1) % count
        pairs += [(i, j), (j, i)]
    return pairs


def inner_swaps(count, other):
    pairs = []
    for i in range(count):
        for k in range(other):
            if i in (0, count - 1):
                pairs.append((i, k, i, k ^ 1))
            else:
                pairs.append((i, k, i + 1 if i % 2 == 1 else i - 1, k))
    return pairs


def local(state, deriv, lift, material, stored, orient, flags):
    view = jnp.transpose(state[:, 0], (0, 1, 3, 2, 4))
    stored_view = jnp.transpose(stored[0], (0, 2, 1, 3))
    orient_view = jnp.transpose(orient[0], (2, 0, 1))
    flags_view = jnp.transpose(flags[0], (2, 0, 1))
    nx, ny, nz = (lax.axis_size(a) for a in ("gx", "gy", "gz"))
    table = jnp.asarray(trace_table(), jnp.bfloat16)
    view, far, near = pack_faces(view)
    far_in = lax.ppermute(far, "gx", swaps(nx, 1, True))
    near_in = lax.ppermute(near, "gx", swaps(nx, 0, True))
    traces, y_two, y_one, z_two, z_one = extract_traces(view, table)
    y_one = lax.ppermute(y_one, "gy", swaps(ny, 0, False))
    pairs = [(y * nz + z, b * nz + a) for y, z, b, a in inner_swaps(ny, nz)]
    y_two = lax.ppermute(y_two, ("gy", "gz"), pairs)
    z_one = lax.ppermute(z_one, "gz", swaps(nz, 0, False))
    medium = material[:, 0]
    z_two, medium, y_one = lax.optimization_barrier((z_two, medium, y_one))
    pairs = [(y * nz + z, b * nz + a) for z, y, a, b in inner_swaps(nz, ny)]
    z_two = lax.ppermute(z_two, ("gy", "gz"), pairs)
    part, coef, source, edge = volume(view, deriv, medium, orient_view, flags_view)
    side, side_sum = side_faces(traces, z_two, z_one, coef, source, edge, stored_view)
    advanced, kernel = finish(
        view, traces, far_in, near_in, y_two, y_one, coef, source, edge, side, side_sum, part,
        stored_view, lift,
    )
    return (
        jnp.transpose(advanced, (0, 1, 3, 2, 4))[:, None],
        jnp.transpose(kernel, (1, 2, 0))[None],
    )


def solution(mesh):
    placed = (
        P(None, "gx", "gy", "gz", None, None),
        P(),
        P(),
        P(None, "gx", "gy", "gz"),
        P("gx", "gy", "gz", None, None),
        P("gx", "gy", "gz", None),
        P("gx", "gy", "gz", None),
    )
    return jax.shard_map(
        local,
        mesh=mesh,
        in_specs=placed,
        out_specs=(P(None, "gx", "gy", "gz", None, None), P("gx", "gy", "gz", None)),
        check_vma=False,
    )
```

```python
import jax
import jax.numpy as jnp
import numpy as np
from functools import partial
from jax import lax
from jax.experimental import pallas as pl
from jax.experimental.pallas import tpu as pltpu
from jax.sharding import PartitionSpec as P

NP = 8
FACE = NP * NP
LANES = 128
step_size = 0.15
stress_slot = ((3, 8, 7), (8, 4, 6), (7, 6, 5))
shear_pairs = ((6, 1, 2), (7, 0, 2), (8, 0, 1))
LIMIT = 20 * 1024 * 1024
PACK_LIMIT = 50 * 1024 * 1024


def trace_table():
    table = np.zeros((NP**3, 4 * FACE), np.float32)
    for first in range(NP):
        for second in range(NP):
            m = first * NP + second
            table[first * 64 + second, m] = 1.0
            table[first * 64 + 56 + second, FACE + m] = 1.0
            table[first * 64 + second * 8, 2 * FACE + m] = 1.0
            table[first * 64 + second * 8 + 7, 3 * FACE + m] = 1.0
    return table


def lane_index(shape):
    return lax.broadcasted_iota(jnp.int32, shape, len(shape) - 1)


def merged(forward, adjoint, upper):
    rows = forward.shape[:-1]
    flat = (-1, LANES)
    turned = pltpu.roll(adjoint.reshape(flat), FACE, 1)
    own = (lane_index(turned.shape) >= FACE) == upper
    return jnp.where(own, forward.reshape(flat), turned).reshape(rows + (LANES,))


def odd_position(axis):
    return lax.axis_index(axis) % 2 == 1


def pack_kernel(state_ref, held_ref, far_ref, near_ref, sem):
    odd = odd_position("gx")
    tiles = state_ref.shape[-1] // LANES
    order = [0, tiles - 1] + list(range(1, tiles - 1))

    def fetch(t):
        columns = pl.ds(t * LANES, LANES)
        return pltpu.make_async_copy(
            state_ref.at[:, :, :, :, columns], held_ref.at[:, :, :, :, columns], sem.at[t]
        )

    for t in order:
        fetch(t).start()
    for t in order[:2]:
        fetch(t).wait()
    low, high = slice(0, LANES), slice((tiles - 1) * LANES, tiles * LANES)
    for y in range(far_ref.shape[0]):
        down = merged(held_ref[0, y, :, :, low], held_ref[1, y, :, :, low], False)
        up = merged(held_ref[0, y, :, :, high], held_ref[1, y, :, :, high], True)
        far_ref[y] = jnp.where(odd, up, down)
        near_ref[y] = jnp.where(odd, down, up)
    for t in order[2:]:
        fetch(t).wait()


def pack_faces(state):
    _, count_y, fields, count_z, nodes = state.shape
    message = jax.ShapeDtypeStruct((count_y, fields, count_z, LANES), jnp.float32)
    return pl.pallas_call(
        pack_kernel,
        out_shape=(jax.ShapeDtypeStruct(state.shape, jnp.float32), message, message),
        in_specs=[pl.BlockSpec(memory_space=pl.ANY)],
        out_specs=(pl.BlockSpec(memory_space=pltpu.VMEM),) * 3,
        scratch_shapes=[pltpu.SemaphoreType.DMA((nodes // LANES,))],
        compiler_params=pltpu.CompilerParams(vmem_limit_bytes=PACK_LIMIT),
        cost_estimate=pl.CostEstimate(flops=10**6, bytes_accessed=2 * 10**6, transcendentals=0),
        name="pack_faces",
    )(state)


def trace_kernel(state_ref, table_ref, trace_ref, y_two, y_one, z_two, z_one):
    _, count_y, fields, count_z, _ = state_ref.shape

    def one_state(s, carry):
        values = state_ref[s].reshape(count_y * fields * count_z, -1)
        high = values.astype(jnp.bfloat16)
        low = (values - high.astype(jnp.float32)).astype(jnp.bfloat16)
        table = table_ref[...]
        picked = jnp.dot(high, table, preferred_element_type=jnp.float32)
        picked = picked + jnp.dot(low, table, preferred_element_type=jnp.float32)
        trace_ref[s] = picked.reshape(count_y, fields, count_z, 2 * LANES)
        return carry

    lax.fori_loop(0, 2, one_state, 0)
    odd_y = odd_position("gy")
    odd_z = odd_position("gz")
    end = count_y - 1
    down = merged(trace_ref[0, 0, :, :, :LANES], trace_ref[1, 0, :, :, :LANES], False)
    up = merged(trace_ref[0, end, :, :, :LANES], trace_ref[1, end, :, :, :LANES], True)
    y_two[...] = jnp.where(odd_y, up, down)
    y_one[...] = jnp.where(odd_y, down, up)
    for s in range(2):
        for y in range(count_y):
            first = trace_ref[s, y, :, 0, LANES:]
            last = trace_ref[s, y, :, count_z - 1, LANES:]
            z_two[s, y] = jnp.where(odd_z, last, first)
            z_one[s, y] = jnp.where(odd_z, first, last)


def extract_traces(state, table):
    _, count_y, fields, count_z, nodes = state.shape
    f32 = jnp.float32
    y_message = jax.ShapeDtypeStruct((fields, count_z, LANES), f32)
    z_message = jax.ShapeDtypeStruct((2, count_y, fields, LANES), f32)
    return pl.pallas_call(
        trace_kernel,
        out_shape=(
            jax.ShapeDtypeStruct((2, count_y, fields, count_z, 2 * LANES), f32),
            y_message,
            y_message,
            z_message,
            z_message,
        ),
        in_specs=[pl.BlockSpec(memory_space=pltpu.VMEM)] * 2,
        out_specs=(pl.BlockSpec(memory_space=pltpu.VMEM),) * 5,
        compiler_params=pltpu.CompilerParams(vmem_limit_bytes=LIMIT),
        cost_estimate=pl.CostEstimate(flops=6 * 10**8, bytes_accessed=4 * 10**6, transcendentals=0),
        name="extract_traces",
    )(state, table)


def spread(columns, rows, pick):
    return lax.dot_general(
        columns,
        pick,
        (((0,), (0,)), ((), ())),
        precision=lax.Precision.HIGHEST,
        preferred_element_type=jnp.float32,
    )


def volume_kernel(
    state_ref, deriv_ref, material_ref, orient_ref, flags_ref,
    partial_ref, coef_ref, source_ref, edge_ref,
    low_ref, grad_ref, div_ref, wide_ref,
):
    _, count_y, fields, count_z, _ = state_ref.shape
    rows = 2 * count_y * count_z
    nodes = partial_ref.shape[-1]
    width = grad_ref.shape[-1]
    ends = [
        lax.axis_index("gy") == 0,
        lax.axis_index("gy") == lax.axis_size("gy") - 1,
        lax.axis_index("gz") == 0,
        lax.axis_index("gz") == lax.axis_size("gz") - 1,
    ]

    for f in range(fields):
        low_ref[f] = state_ref[:, :, f].reshape(rows, -1).astype(jnp.bfloat16)
    lanes = lane_index((3 * count_y, 3 * count_y * LANES))
    row = lax.broadcasted_iota(jnp.int32, lanes.shape, 0)
    pick = (lanes // LANES == row).astype(jnp.float32)
    medium = spread(material_ref[...].reshape(3 * count_y, count_z), 3 * count_y, pick)
    lanes = lane_index((6 * count_y, 3 * count_y * LANES))
    row = lax.broadcasted_iota(jnp.int32, lanes.shape, 0)
    block = lanes // LANES
    face = 2 * (block // count_y) + (lanes % LANES) // FACE
    pick = (face * count_y + block % count_y == row).astype(jnp.float32)
    codes = spread(
        orient_ref[...].reshape(6 * count_y, count_z).astype(jnp.float32), 6 * count_y, pick
    )
    kinds = spread(
        flags_ref[...].reshape(6 * count_y, count_z).astype(jnp.float32), 6 * count_y, pick
    )
    lane = lane_index((count_z, LANES))
    upper = lane >= FACE
    half_sign = jnp.where(upper, 0.5, -0.5)
    node = lane % FACE
    near, far = (node // NP, node % NP)
    z_pos = lax.broadcasted_iota(jnp.int32, lane.shape, 0)
    for y in range(count_y):
        lam = medium[:, y * LANES : (y + 1) * LANES]
        mu = medium[:, (count_y + y) * LANES : (count_y + y + 1) * LANES]
        rho = medium[:, (2 * count_y + y) * LANES : (2 * count_y + y + 1) * LANES]
        inv = 1.0 / rho
        wide_ref[0, y] = lam
        wide_ref[1, y] = mu
        wide_ref[2, y] = inv
        coef_ref[0, y] = half_sign * lam
        coef_ref[1, y] = half_sign * mu
        coef_ref[2, y] = half_sign * inv
        coef_ref[3, y] = 0.5 * jnp.sqrt((lam + 2.0 * mu) * inv)
        for d in range(3):
            at = (d * count_y + y) * LANES
            code = jnp.round(codes[:, at : at + LANES]).astype(jnp.int32)
            swap = code >= 4
            lead = jnp.where(swap, far, near)
            trail = jnp.where(swap, near, far)
            lead = jnp.where(code % 2 == 1, NP - 1 - lead, lead)
            trail = jnp.where((code // 2) % 2 == 1, NP - 1 - trail, trail)
            source_ref[d, y] = lead * NP + trail + jnp.where(upper, 0, FACE)
            if d > 0:
                free = jnp.where(jnp.round(kinds[:, at : at + LANES]) == 1.0, 1.0, 0.0)
                if d == 1:
                    low_end = (ends[0]) if y == 0 else False
                    high_end = (ends[1]) if y == count_y - 1 else False
                    rim = jnp.where(
                        upper,
                        jnp.where(high_end, 1.0, 0.0),
                        jnp.where(low_end, 1.0, 0.0),
                    )
                else:
                    low_rim = jnp.where(z_pos == 0, jnp.where(ends[2], 1.0, 0.0), 0.0)
                    high_rim = jnp.where(
                        z_pos == count_z - 1, jnp.where(ends[3], 1.0, 0.0), 0.0
                    )
                    rim = jnp.where(upper, high_rim, low_rim)
                edge_ref[d - 1, 0, y] = rim
                edge_ref[d - 1, 1, y] = free

    def columns_part(n, carry):
        base = n * width

        def operator(d):
            return deriv_ref[:, pl.ds(pl.multiple_of(d * nodes + base, LANES), width)]

        velocity = low_ref[0:3].reshape(3 * rows, nodes)
        for d in range(3):
            grad_ref[d] = jnp.dot(velocity, operator(d), preferred_element_type=jnp.float32)
        total = None
        for d in range(3):
            stress = jnp.concatenate([low_ref[stress_slot[i][d]] for i in range(3)], axis=0)
            part = jnp.dot(stress, operator(d), preferred_element_type=jnp.float32)
            total = part if total is None else total + part
        div_ref[...] = total
        for s in range(2):
            scale = step_size if s == 0 else -step_size
            for y in range(count_y):
                at = (s * count_y + y) * count_z
                lam = scale * wide_ref[0, y]
                mu = scale * wide_ref[1, y]
                inv = scale * wide_ref[2, y]
                for tile in range(width // LANES):
                    columns = slice(tile * LANES, (tile + 1) * LANES)
                    where = pl.ds(pl.multiple_of(base + tile * LANES, LANES), LANES)

                    def g(d, i):
                        return grad_ref[d, i * rows + at : i * rows + at + count_z, columns]

                    def put(f, term):
                        partial_ref[s, y, f, :, where] = state_ref[s, y, f, :, where] + term

                    for i in range(3):
                        put(i, inv * div_ref[i * rows + at : i * rows + at + count_z, columns])
                    diag = [g(i, i) for i in range(3)]
                    common = lam * (diag[0] + diag[1] + diag[2])
                    for i in range(3):
                        put(3 + i, common + (mu + mu) * diag[i])
                    for f, i, j in shear_pairs:
                        put(f, mu * (g(j, i) + g(i, j)))
        return carry

    lax.fori_loop(0, nodes // width, columns_part, 0)


def volume(state, deriv, material, orient, flags):
    _, count_y, fields, count_z, nodes = state.shape
    f32 = jnp.float32
    width = 256
    rows = 2 * count_y * count_z
    outs = (
        jax.ShapeDtypeStruct(state.shape, f32),
        jax.ShapeDtypeStruct((4, count_y, count_z, LANES), f32),
        jax.ShapeDtypeStruct((3, count_y, count_z, LANES), jnp.int32),
        jax.ShapeDtypeStruct((2, 2, count_y, count_z, LANES), f32),
    )
    return pl.pallas_call(
        volume_kernel,
        out_shape=outs,
        in_specs=[pl.BlockSpec(memory_space=pltpu.VMEM)] * 5,
        out_specs=(pl.BlockSpec(memory_space=pltpu.VMEM),) * 4,
        scratch_shapes=[
            pltpu.VMEM((fields, rows, nodes), jnp.bfloat16),
            pltpu.VMEM((3, 3 * rows, width), f32),
            pltpu.VMEM((3 * rows, width), f32),
            pltpu.VMEM((3, count_y, count_z, LANES), f32),
        ],
        compiler_params=pltpu.CompilerParams(vmem_limit_bytes=LIMIT),
        cost_estimate=pl.CostEstimate(
            flops=10**6, bytes_accessed=10**5, transcendentals=0
        ),
        name="volume",
    )(state, deriv, material, orient, flags)


def face_flux(jumps, d, coefs):
    lam, mu, inv, speed = coefs
    flux = [speed * jump for jump in jumps]
    for i in range(3):
        flux[i] = flux[i] + inv * jumps[stress_slot[i][d]]
    common = lam * jumps[d]
    for i in range(3):
        flux[3 + i] = flux[3 + i] + common
    for i, j, f in ((0, 0, 3), (1, 1, 4), (2, 2, 5), (1, 2, 6), (0, 2, 7), (0, 1, 8)):
        if j == d:
            flux[f] = flux[f] + mu * jumps[i]
        if i == d:
            flux[f] = flux[f] + mu * jumps[j]
    return [term.astype(jnp.bfloat16) for term in flux]


def rim_jump(turned, inside, edge, f):
    rim, free = edge
    keep = free - 1.0 if f < 3 else -free - 1.0
    return jnp.where(rim > 0.0, inside * keep, turned - inside)


def side_kernel(
    trace_ref, z_two, z_one, coef_ref, source_ref, edge_ref, stored_ref, flux_ref, sum_ref
):
    _, count_y, fields, count_z, _ = trace_ref.shape
    last_y = count_y - 1
    odd_z = odd_position("gz")
    lane = lane_index((count_z, LANES))
    upper = lane >= FACE
    z_pos = lax.broadcasted_iota(jnp.int32, lane.shape, 0)
    at_low = jnp.logical_and(z_pos == 0, upper)
    at_high = jnp.logical_and(z_pos == count_z - 1, jnp.logical_not(upper))

    def row(y, carry):
        coefs = [coef_ref[k, y] for k in range(4)]
        edge = (edge_ref[1, 0, y], edge_ref[1, 1, y])
        source = source_ref[2, y]
        for s in range(2):
            jumps = []
            for f in range(fields):
                inside = trace_ref[s, y, f, :, LANES:]
                two = z_two[s, y, f : f + 1, :]
                one = z_one[s, y, f : f + 1, :]
                from_below = jnp.where(odd_z, one, two)
                from_above = jnp.where(odd_z, two, one)
                mixed = jnp.where(upper, pltpu.roll(inside, 1, 0), pltpu.roll(inside, count_z - 1, 0))
                mixed = jnp.where(at_low, from_below, jnp.where(at_high, from_above, mixed))
                turned = jnp.take_along_axis(mixed, source, axis=1)
                jump = rim_jump(turned, inside, edge, f)
                jumps.append(jump)
                if s == 1:
                    sum_ref[y, f] = stored_ref[y, f, :, 2 * LANES :] * jump
            for f, term in enumerate(face_flux(jumps, 2, coefs)):
                flux_ref[y, s, f, :, LANES:] = term

        @pl.when(jnp.logical_and(y > 0, y < last_y))
        def _():
            turn = source_ref[1, y]
            for s in range(2):
                jumps = []
                for f in range(fields):
                    inside = trace_ref[s, y, f, :, :LANES]
                    mixed = jnp.where(
                        upper, trace_ref[s, y - 1, f, :, :LANES], trace_ref[s, y + 1, f, :, :LANES]
                    )
                    jump = jnp.take_along_axis(mixed, turn, axis=1) - inside
                    jumps.append(jump)
                    if s == 1:
                        sum_ref[y, f] += stored_ref[y, f, :, LANES : 2 * LANES] * jump
                for f, term in enumerate(face_flux(jumps, 1, coefs)):
                    flux_ref[y, s, f, :, :LANES] = term

        return carry

    lax.fori_loop(0, count_y, row, 0)


def side_faces(traces, z_two, z_one, coef, source, edge, stored):
    _, count_y, fields, count_z, _ = traces.shape
    return pl.pallas_call(
        side_kernel,
        out_shape=(
            jax.ShapeDtypeStruct((count_y, 2, fields, count_z, 2 * LANES), jnp.bfloat16),
            jax.ShapeDtypeStruct((count_y, fields, count_z, LANES), jnp.float32),
        ),
        in_specs=[pl.BlockSpec(memory_space=pltpu.VMEM)] * 7,
        out_specs=(pl.BlockSpec(memory_space=pltpu.VMEM),) * 2,
        compiler_params=pltpu.CompilerParams(vmem_limit_bytes=LIMIT),
        cost_estimate=pl.CostEstimate(flops=10**6, bytes_accessed=10**5, transcendentals=0),
        name="side_faces",
    )(traces, z_two, z_one, coef, source, edge, stored)


def final_kernel(
    state_ref, trace_ref, far_ref, near_ref, y_two, y_one, coef_ref, source_ref, edge_ref,
    side_ref, side_sum_ref, partial_ref, stored_ref, lift_ref,
    advanced_ref, kernel_ref,
    flux_ref, sum_ref, out_ref, out_sem,
):
    _, count_y, fields, count_z, nodes = state_ref.shape
    last_y = count_y - 1
    lane = lane_index((count_z, LANES))
    upper = lane >= FACE
    z_pos = lax.broadcasted_iota(jnp.int32, lane.shape, 0)
    take_near = upper == odd_position("gx")
    odd_y = odd_position("gy")

    def write(s, y):
        return pltpu.make_async_copy(out_ref.at[s, y], advanced_ref.at[s, y], out_sem.at[s, y])

    order = list(range(1, last_y)) + [0, last_y]

    def fluxes(y):
        slot = order.index(y) % 2
        coefs = [coef_ref[k, y] for k in range(4)]
        for s in range(2):
            source = source_ref[0, y]
            if s == 1:
                source = (source + FACE) % LANES
            jumps = []
            for f in range(fields):
                inside = jnp.where(
                    upper, state_ref[s, y, f, :, nodes - LANES :], state_ref[s, y, f, :, :LANES]
                )
                near, far = (near_ref[y, f], far_ref[y, f])
                if s == 1:
                    near, far = (far, near)
                mixed = jnp.where(take_near, near, far)
                jump = jnp.take_along_axis(mixed, source, axis=1) - inside
                jumps.append(jump)
                if s == 1:
                    sum_ref[slot, f] = side_sum_ref[y, f] + stored_ref[y, f, :, :LANES] * jump
            for f, term in enumerate(face_flux(jumps, 0, coefs)):
                flux_ref[slot, s, f, :, :LANES] = term
        if 0 < y < last_y:
            flux_ref[slot, :, :, :, LANES:] = side_ref[y, :, :, :, :LANES]
            return
        edge = (edge_ref[0, 0, y], edge_ref[0, 1, y])
        turn = source_ref[1, y]
        take_two = jnp.logical_not(odd_y) if y == 0 else odd_y
        outer = upper if y == 0 else jnp.logical_not(upper)
        inner_row = 1 if y == 0 else last_y - 1
        for s in range(2):
            jumps = []
            for f in range(fields):
                received = jnp.where(take_two, y_two[f], y_one[f])
                if s == 1:
                    received = pltpu.roll(received, FACE, 1)
                inside = trace_ref[s, y, f, :, :LANES]
                mixed = jnp.where(outer, received, trace_ref[s, inner_row, f, :, :LANES])
                turned = jnp.take_along_axis(mixed, turn, axis=1)
                jump = rim_jump(turned, inside, edge, f)
                jumps.append(jump)
                if s == 1:
                    sum_ref[slot, f] += stored_ref[y, f, :, LANES : 2 * LANES] * jump
            for f, term in enumerate(face_flux(jumps, 1, coefs)):
                flux_ref[slot, s, f, :, LANES:] = term

    def results(y):
        slot = order.index(y) % 2
        for s in range(2):
            lifted = jnp.dot(
                flux_ref[slot, s].reshape(fields * count_z, 2 * LANES),
                lift_ref[: 2 * LANES],
                preferred_element_type=jnp.float32,
            ) + jnp.dot(
                side_ref[y, s, :, :, LANES:].reshape(fields * count_z, LANES),
                lift_ref[2 * LANES :],
                preferred_element_type=jnp.float32,
            )
            scale = step_size if s == 0 else -step_size
            out_ref[s, y] = partial_ref[s, y] + scale * lifted.reshape(fields, count_z, nodes)
            write(s, y).start()
        for f in range(fields):
            sums = jnp.sum(sum_ref[slot, f], axis=1, keepdims=True) * (1.0 / FACE)
            across = jnp.sum(jnp.where(z_pos == lane, sums, 0.0), axis=0, keepdims=True)
            kernel_ref[f, pl.ds(y, 1), :] = across[:, :count_z]

    fluxes(order[0])
    for k, y in enumerate(order):
        if k + 1 < count_y:
            fluxes(order[k + 1])
        results(y)
    for y in range(count_y):
        for s in range(2):
            write(s, y).wait()


def finish(
    state, traces, far, near, y_two, y_one, coef, source, edge, side, side_sum, part, stored, lift
):
    _, count_y, fields, count_z, nodes = state.shape
    f32 = jnp.float32
    outs = (
        jax.ShapeDtypeStruct(state.shape, f32),
        jax.ShapeDtypeStruct((fields, count_y, count_z), f32),
    )
    return pl.pallas_call(
        final_kernel,
        out_shape=outs,
        in_specs=[pl.BlockSpec(memory_space=pltpu.VMEM)] * 14,
        out_specs=(pl.BlockSpec(memory_space=pl.ANY), pl.BlockSpec(memory_space=pltpu.VMEM)),
        scratch_shapes=[
            pltpu.VMEM((2, 2, fields, count_z, 2 * LANES), jnp.bfloat16),
            pltpu.VMEM((2, fields, count_z, LANES), f32),
            pltpu.VMEM(state.shape, f32),
            pltpu.SemaphoreType.DMA((2, count_y)),
        ],
        compiler_params=pltpu.CompilerParams(vmem_limit_bytes=LIMIT),
        cost_estimate=pl.CostEstimate(flops=9 * 10**8, bytes_accessed=10**7, transcendentals=0),
        name="finish",
    )(state, traces, far, near, y_two, y_one, coef, source, edge, side, side_sum, part, stored, lift)


def swaps(count, start, wrap):
    pairs = []
    for i in range(start, count if wrap else count - 1, 2):
        j = (i + 1) % count
        pairs += [(i, j), (j, i)]
    return pairs


def inner_swaps(count, other):
    pairs = []
    for i in range(count):
        for k in range(other):
            if i in (0, count - 1):
                pairs.append((i, k, i, k ^ 1))
            else:
                pairs.append((i, k, i + 1 if i % 2 == 1 else i - 1, k))
    return pairs


def local(state, deriv, lift, material, stored, orient, flags):
    view = jnp.transpose(state[:, 0], (0, 1, 3, 2, 4))
    stored_view = jnp.transpose(stored[0], (0, 2, 1, 3))
    orient_view = jnp.transpose(orient[0], (2, 0, 1))
    flags_view = jnp.transpose(flags[0], (2, 0, 1))
    nx, ny, nz = (lax.axis_size(a) for a in ("gx", "gy", "gz"))
    table = jnp.asarray(trace_table(), jnp.bfloat16)
    view, far, near = pack_faces(view)
    far_in = lax.ppermute(far, "gx", swaps(nx, 1, True))
    near_in = lax.ppermute(near, "gx", swaps(nx, 0, True))
    traces, y_two, y_one, z_two, z_one = extract_traces(view, table)
    y_one = lax.ppermute(y_one, "gy", swaps(ny, 0, False))
    pairs = [(y * nz + z, b * nz + a) for y, z, b, a in inner_swaps(ny, nz)]
    y_two = lax.ppermute(y_two, ("gy", "gz"), pairs)
    z_one = lax.ppermute(z_one, "gz", swaps(nz, 0, False))
    medium = material[:, 0]
    z_two, medium, y_one = lax.optimization_barrier((z_two, medium, y_one))
    pairs = [(y * nz + z, b * nz + a) for z, y, a, b in inner_swaps(nz, ny)]
    z_two = lax.ppermute(z_two, ("gy", "gz"), pairs)
    part, coef, source, edge = volume(view, deriv, medium, orient_view, flags_view)
    side, side_sum = side_faces(traces, z_two, z_one, coef, source, edge, stored_view)
    advanced, kernel = finish(
        view, traces, far_in, near_in, y_two, y_one, coef, source, edge, side, side_sum, part,
        stored_view, lift,
    )
    return (
        jnp.transpose(advanced, (0, 1, 3, 2, 4))[:, None],
        jnp.transpose(kernel, (1, 2, 0))[None],
    )


def solution(mesh):
    placed = (
        P(None, "gx", "gy", "gz", None, None),
        P(),
        P(),
        P(None, "gx", "gy", "gz"),
        P("gx", "gy", "gz", None, None),
        P("gx", "gy", "gz", None),
        P("gx", "gy", "gz", None),
    )
    return jax.shard_map(
        local,
        mesh=mesh,
        in_specs=placed,
        out_specs=(P(None, "gx", "gy", "gz", None, None), P("gx", "gy", "gz", None)),
        check_vma=False,
    )
```

```python
import jax
import jax.numpy as jnp
import numpy as np
from functools import partial
from jax import lax
from jax.experimental import pallas as pl
from jax.experimental.pallas import tpu as pltpu
from jax.sharding import PartitionSpec as P

NP = 8
FACE = NP * NP
LANES = 128
step_size = 0.15
stress_slot = ((3, 8, 7), (8, 4, 6), (7, 6, 5))
shear_pairs = ((6, 1, 2), (7, 0, 2), (8, 0, 1))
LIMIT = 20 * 1024 * 1024
PACK_LIMIT = 50 * 1024 * 1024


def trace_table():
    table = np.zeros((NP**3, 4 * FACE), np.float32)
    for first in range(NP):
        for second in range(NP):
            m = first * NP + second
            table[first * 64 + second, m] = 1.0
            table[first * 64 + 56 + second, FACE + m] = 1.0
            table[first * 64 + second * 8, 2 * FACE + m] = 1.0
            table[first * 64 + second * 8 + 7, 3 * FACE + m] = 1.0
    return table


def lane_index(shape):
    return lax.broadcasted_iota(jnp.int32, shape, len(shape) - 1)


def merged(forward, adjoint, upper):
    rows = forward.shape[:-1]
    flat = (-1, LANES)
    turned = pltpu.roll(adjoint.reshape(flat), FACE, 1)
    own = (lane_index(turned.shape) >= FACE) == upper
    return jnp.where(own, forward.reshape(flat), turned).reshape(rows + (LANES,))


def odd_position(axis):
    return lax.axis_index(axis) % 2 == 1


def pack_kernel(state_ref, held_ref, far_ref, near_ref, sem):
    odd = odd_position("gx")
    tiles = state_ref.shape[-1] // LANES
    order = [0, tiles - 1] + list(range(1, tiles - 1))

    def fetch(t):
        columns = pl.ds(t * LANES, LANES)
        return pltpu.make_async_copy(
            state_ref.at[:, :, :, :, columns], held_ref.at[:, :, :, :, columns], sem.at[t]
        )

    for t in order:
        fetch(t).start()
    for t in order[:2]:
        fetch(t).wait()
    low, high = slice(0, LANES), slice((tiles - 1) * LANES, tiles * LANES)
    for y in range(far_ref.shape[0]):
        down = merged(held_ref[0, y, :, :, low], held_ref[1, y, :, :, low], False)
        up = merged(held_ref[0, y, :, :, high], held_ref[1, y, :, :, high], True)
        far_ref[y] = jnp.where(odd, up, down)
        near_ref[y] = jnp.where(odd, down, up)
    for t in order[2:]:
        fetch(t).wait()


def pack_faces(state):
    _, count_y, fields, count_z, nodes = state.shape
    message = jax.ShapeDtypeStruct((count_y, fields, count_z, LANES), jnp.float32)
    return pl.pallas_call(
        pack_kernel,
        out_shape=(jax.ShapeDtypeStruct(state.shape, jnp.float32), message, message),
        in_specs=[pl.BlockSpec(memory_space=pl.ANY)],
        out_specs=(pl.BlockSpec(memory_space=pltpu.VMEM),) * 3,
        scratch_shapes=[pltpu.SemaphoreType.DMA((nodes // LANES,))],
        compiler_params=pltpu.CompilerParams(vmem_limit_bytes=PACK_LIMIT),
        cost_estimate=pl.CostEstimate(flops=10**6, bytes_accessed=2 * 10**6, transcendentals=0),
        name="pack_faces",
    )(state)


def trace_kernel(state_ref, table_ref, trace_ref, y_two, y_one, z_two, z_one):
    _, count_y, fields, count_z, _ = state_ref.shape

    def one_state(s):
        values = state_ref[s].reshape(count_y * fields * count_z, -1)
        high = values.astype(jnp.bfloat16)
        low = (values - high.astype(jnp.float32)).astype(jnp.bfloat16)
        table = table_ref[...]
        picked = jnp.dot(high, table, preferred_element_type=jnp.float32)
        picked = picked + jnp.dot(low, table, preferred_element_type=jnp.float32)
        trace_ref[s] = picked.reshape(count_y, fields, count_z, 2 * LANES)

    for s in range(2):
        one_state(s)
    odd_y = odd_position("gy")
    odd_z = odd_position("gz")
    end = count_y - 1
    down = merged(trace_ref[0, 0, :, :, :LANES], trace_ref[1, 0, :, :, :LANES], False)
    up = merged(trace_ref[0, end, :, :, :LANES], trace_ref[1, end, :, :, :LANES], True)
    y_two[...] = jnp.where(odd_y, up, down)
    y_one[...] = jnp.where(odd_y, down, up)
    for s in range(2):
        for y in range(count_y):
            first = trace_ref[s, y, :, 0, LANES:]
            last = trace_ref[s, y, :, count_z - 1, LANES:]
            z_two[s, y] = jnp.where(odd_z, last, first)
            z_one[s, y] = jnp.where(odd_z, first, last)


def extract_traces(state, table):
    _, count_y, fields, count_z, nodes = state.shape
    f32 = jnp.float32
    y_message = jax.ShapeDtypeStruct((fields, count_z, LANES), f32)
    z_message = jax.ShapeDtypeStruct((2, count_y, fields, LANES), f32)
    return pl.pallas_call(
        trace_kernel,
        out_shape=(
            jax.ShapeDtypeStruct((2, count_y, fields, count_z, 2 * LANES), f32),
            y_message,
            y_message,
            z_message,
            z_message,
        ),
        in_specs=[pl.BlockSpec(memory_space=pltpu.VMEM)] * 2,
        out_specs=(pl.BlockSpec(memory_space=pltpu.VMEM),) * 5,
        compiler_params=pltpu.CompilerParams(vmem_limit_bytes=LIMIT),
        cost_estimate=pl.CostEstimate(flops=6 * 10**8, bytes_accessed=4 * 10**6, transcendentals=0),
        name="extract_traces",
    )(state, table)


def spread(columns, rows, pick):
    return lax.dot_general(
        columns,
        pick,
        (((0,), (0,)), ((), ())),
        precision=lax.Precision.HIGHEST,
        preferred_element_type=jnp.float32,
    )


def volume_kernel(
    state_ref, deriv_ref, material_ref, orient_ref, flags_ref,
    partial_ref, coef_ref, source_ref, edge_ref,
    low_ref, grad_ref, div_ref, wide_ref,
):
    _, count_y, fields, count_z, _ = state_ref.shape
    rows = 2 * count_y * count_z
    nodes = partial_ref.shape[-1]
    width = grad_ref.shape[-1]
    ends = [
        lax.axis_index("gy") == 0,
        lax.axis_index("gy") == lax.axis_size("gy") - 1,
        lax.axis_index("gz") == 0,
        lax.axis_index("gz") == lax.axis_size("gz") - 1,
    ]

    for f in range(fields):
        low_ref[f] = state_ref[:, :, f].reshape(rows, -1).astype(jnp.bfloat16)
    lanes = lane_index((3 * count_y, 3 * count_y * LANES))
    row = lax.broadcasted_iota(jnp.int32, lanes.shape, 0)
    pick = (lanes // LANES == row).astype(jnp.float32)
    medium = spread(material_ref[...].reshape(3 * count_y, count_z), 3 * count_y, pick)
    lanes = lane_index((6 * count_y, 3 * count_y * LANES))
    row = lax.broadcasted_iota(jnp.int32, lanes.shape, 0)
    block = lanes // LANES
    face = 2 * (block // count_y) + (lanes % LANES) // FACE
    pick = (face * count_y + block % count_y == row).astype(jnp.float32)
    codes = spread(
        orient_ref[...].reshape(6 * count_y, count_z).astype(jnp.float32), 6 * count_y, pick
    )
    kinds = spread(
        flags_ref[...].reshape(6 * count_y, count_z).astype(jnp.float32), 6 * count_y, pick
    )
    lane = lane_index((count_z, LANES))
    upper = lane >= FACE
    half_sign = jnp.where(upper, 0.5, -0.5)
    node = lane % FACE
    near, far = (node // NP, node % NP)
    z_pos = lax.broadcasted_iota(jnp.int32, lane.shape, 0)
    for y in range(count_y):
        lam = medium[:, y * LANES : (y + 1) * LANES]
        mu = medium[:, (count_y + y) * LANES : (count_y + y + 1) * LANES]
        rho = medium[:, (2 * count_y + y) * LANES : (2 * count_y + y + 1) * LANES]
        inv = 1.0 / rho
        wide_ref[0, y] = lam
        wide_ref[1, y] = mu
        wide_ref[2, y] = inv
        coef_ref[0, y] = half_sign * lam
        coef_ref[1, y] = half_sign * mu
        coef_ref[2, y] = half_sign * inv
        coef_ref[3, y] = 0.5 * jnp.sqrt((lam + 2.0 * mu) * inv)
        for d in range(3):
            at = (d * count_y + y) * LANES
            code = jnp.round(codes[:, at : at + LANES]).astype(jnp.int32)
            swap = code >= 4
            lead = jnp.where(swap, far, near)
            trail = jnp.where(swap, near, far)
            lead = jnp.where(code % 2 == 1, NP - 1 - lead, lead)
            trail = jnp.where((code // 2) % 2 == 1, NP - 1 - trail, trail)
            source_ref[d, y] = lead * NP + trail + jnp.where(upper, 0, FACE)
            if d > 0:
                free = jnp.where(jnp.round(kinds[:, at : at + LANES]) == 1.0, 1.0, 0.0)
                if d == 1:
                    low_end = (ends[0]) if y == 0 else False
                    high_end = (ends[1]) if y == count_y - 1 else False
                    rim = jnp.where(
                        upper,
                        jnp.where(high_end, 1.0, 0.0),
                        jnp.where(low_end, 1.0, 0.0),
                    )
                else:
                    low_rim = jnp.where(z_pos == 0, jnp.where(ends[2], 1.0, 0.0), 0.0)
                    high_rim = jnp.where(
                        z_pos == count_z - 1, jnp.where(ends[3], 1.0, 0.0), 0.0
                    )
                    rim = jnp.where(upper, high_rim, low_rim)
                edge_ref[d - 1, 0, y] = rim
                edge_ref[d - 1, 1, y] = free

    def columns_part(n):
        base = n * width

        def operator(d):
            return deriv_ref[:, d * nodes + base : d * nodes + base + width]

        velocity = low_ref[0:3].reshape(3 * rows, nodes)
        for d in range(3):
            grad_ref[d] = jnp.dot(velocity, operator(d), preferred_element_type=jnp.float32)
        total = None
        for d in range(3):
            stress = jnp.concatenate([low_ref[stress_slot[i][d]] for i in range(3)], axis=0)
            part = jnp.dot(stress, operator(d), preferred_element_type=jnp.float32)
            total = part if total is None else total + part
        div_ref[...] = total
        for s in range(2):
            scale = step_size if s == 0 else -step_size
            for y in range(count_y):
                at = (s * count_y + y) * count_z
                lam = scale * wide_ref[0, y]
                mu = scale * wide_ref[1, y]
                inv = scale * wide_ref[2, y]
                for tile in range(width // LANES):
                    columns = slice(tile * LANES, (tile + 1) * LANES)
                    where = slice(base + tile * LANES, base + (tile + 1) * LANES)

                    def g(d, i):
                        return grad_ref[d, i * rows + at : i * rows + at + count_z, columns]

                    def put(f, term):
                        partial_ref[s, y, f, :, where] = state_ref[s, y, f, :, where] + term

                    for i in range(3):
                        put(i, inv * div_ref[i * rows + at : i * rows + at + count_z, columns])
                    diag = [g(i, i) for i in range(3)]
                    common = lam * (diag[0] + diag[1] + diag[2])
                    for i in range(3):
                        put(3 + i, common + (mu + mu) * diag[i])
                    for f, i, j in shear_pairs:
                        put(f, mu * (g(j, i) + g(i, j)))

    for n in range(nodes // width):
        columns_part(n)


def volume(state, deriv, material, orient, flags):
    _, count_y, fields, count_z, nodes = state.shape
    f32 = jnp.float32
    width = 256
    rows = 2 * count_y * count_z
    outs = (
        jax.ShapeDtypeStruct(state.shape, f32),
        jax.ShapeDtypeStruct((4, count_y, count_z, LANES), f32),
        jax.ShapeDtypeStruct((3, count_y, count_z, LANES), jnp.int32),
        jax.ShapeDtypeStruct((2, 2, count_y, count_z, LANES), f32),
    )
    return pl.pallas_call(
        volume_kernel,
        out_shape=outs,
        in_specs=[pl.BlockSpec(memory_space=pltpu.VMEM)] * 5,
        out_specs=(pl.BlockSpec(memory_space=pltpu.VMEM),) * 4,
        scratch_shapes=[
            pltpu.VMEM((fields, rows, nodes), jnp.bfloat16),
            pltpu.VMEM((3, 3 * rows, width), f32),
            pltpu.VMEM((3 * rows, width), f32),
            pltpu.VMEM((3, count_y, count_z, LANES), f32),
        ],
        compiler_params=pltpu.CompilerParams(vmem_limit_bytes=LIMIT),
        cost_estimate=pl.CostEstimate(
            flops=10**6, bytes_accessed=10**5, transcendentals=0
        ),
        name="volume",
    )(state, deriv, material, orient, flags)


def face_flux(jumps, d, coefs):
    lam, mu, inv, speed = coefs
    flux = [speed * jump for jump in jumps]
    for i in range(3):
        flux[i] = flux[i] + inv * jumps[stress_slot[i][d]]
    common = lam * jumps[d]
    for i in range(3):
        flux[3 + i] = flux[3 + i] + common
    for i, j, f in ((0, 0, 3), (1, 1, 4), (2, 2, 5), (1, 2, 6), (0, 2, 7), (0, 1, 8)):
        if j == d:
            flux[f] = flux[f] + mu * jumps[i]
        if i == d:
            flux[f] = flux[f] + mu * jumps[j]
    return [term.astype(jnp.bfloat16) for term in flux]


def rim_jump(turned, inside, edge, f):
    rim, free = edge
    keep = free - 1.0 if f < 3 else -free - 1.0
    return jnp.where(rim > 0.0, inside * keep, turned - inside)


def side_kernel(
    trace_ref, z_two, z_one, coef_ref, source_ref, edge_ref, stored_ref, flux_ref, sum_ref
):
    _, count_y, fields, count_z, _ = trace_ref.shape
    last_y = count_y - 1
    odd_z = odd_position("gz")
    lane = lane_index((count_z, LANES))
    upper = lane >= FACE
    z_pos = lax.broadcasted_iota(jnp.int32, lane.shape, 0)
    at_low = jnp.logical_and(z_pos == 0, upper)
    at_high = jnp.logical_and(z_pos == count_z - 1, jnp.logical_not(upper))

    def row(y):
        coefs = [coef_ref[k, y] for k in range(4)]
        edge = (edge_ref[1, 0, y], edge_ref[1, 1, y])
        source = source_ref[2, y]
        for s in range(2):
            jumps = []
            for f in range(fields):
                inside = trace_ref[s, y, f, :, LANES:]
                two = z_two[s, y, f : f + 1, :]
                one = z_one[s, y, f : f + 1, :]
                from_below = jnp.where(odd_z, one, two)
                from_above = jnp.where(odd_z, two, one)
                mixed = jnp.where(upper, pltpu.roll(inside, 1, 0), pltpu.roll(inside, count_z - 1, 0))
                mixed = jnp.where(at_low, from_below, jnp.where(at_high, from_above, mixed))
                turned = jnp.take_along_axis(mixed, source, axis=1)
                jump = rim_jump(turned, inside, edge, f)
                jumps.append(jump)
                if s == 1:
                    sum_ref[y, f] = stored_ref[y, f, :, 2 * LANES :] * jump
            for f, term in enumerate(face_flux(jumps, 2, coefs)):
                flux_ref[y, s, f, :, LANES:] = term

        if 0 < y < last_y:
            turn = source_ref[1, y]
            for s in range(2):
                jumps = []
                for f in range(fields):
                    inside = trace_ref[s, y, f, :, :LANES]
                    mixed = jnp.where(
                        upper, trace_ref[s, y - 1, f, :, :LANES], trace_ref[s, y + 1, f, :, :LANES]
                    )
                    jump = jnp.take_along_axis(mixed, turn, axis=1) - inside
                    jumps.append(jump)
                    if s == 1:
                        sum_ref[y, f] += stored_ref[y, f, :, LANES : 2 * LANES] * jump
                for f, term in enumerate(face_flux(jumps, 1, coefs)):
                    flux_ref[y, s, f, :, :LANES] = term

    for y in range(count_y):
        row(y)


def side_faces(traces, z_two, z_one, coef, source, edge, stored):
    _, count_y, fields, count_z, _ = traces.shape
    return pl.pallas_call(
        side_kernel,
        out_shape=(
            jax.ShapeDtypeStruct((count_y, 2, fields, count_z, 2 * LANES), jnp.bfloat16),
            jax.ShapeDtypeStruct((count_y, fields, count_z, LANES), jnp.float32),
        ),
        in_specs=[pl.BlockSpec(memory_space=pltpu.VMEM)] * 7,
        out_specs=(pl.BlockSpec(memory_space=pltpu.VMEM),) * 2,
        compiler_params=pltpu.CompilerParams(vmem_limit_bytes=LIMIT),
        cost_estimate=pl.CostEstimate(flops=10**6, bytes_accessed=10**5, transcendentals=0),
        name="side_faces",
    )(traces, z_two, z_one, coef, source, edge, stored)


def final_kernel(
    state_ref, trace_ref, far_ref, near_ref, y_two, y_one, coef_ref, source_ref, edge_ref,
    side_ref, side_sum_ref, partial_ref, stored_ref, lift_ref,
    advanced_ref, kernel_ref,
    flux_ref, sum_ref, out_ref, out_sem,
):
    _, count_y, fields, count_z, nodes = state_ref.shape
    last_y = count_y - 1
    lane = lane_index((count_z, LANES))
    upper = lane >= FACE
    z_pos = lax.broadcasted_iota(jnp.int32, lane.shape, 0)
    take_near = upper == odd_position("gx")
    odd_y = odd_position("gy")

    def write(s, y):
        return pltpu.make_async_copy(out_ref.at[s, y], advanced_ref.at[s, y], out_sem.at[s, y])

    order = list(range(1, last_y)) + [0, last_y]

    def fluxes(y):
        slot = order.index(y) % 2
        coefs = [coef_ref[k, y] for k in range(4)]
        for s in range(2):
            source = source_ref[0, y]
            if s == 1:
                source = (source + FACE) % LANES
            jumps = []
            for f in range(fields):
                inside = jnp.where(
                    upper, state_ref[s, y, f, :, nodes - LANES :], state_ref[s, y, f, :, :LANES]
                )
                near, far = (near_ref[y, f], far_ref[y, f])
                if s == 1:
                    near, far = (far, near)
                mixed = jnp.where(take_near, near, far)
                jump = jnp.take_along_axis(mixed, source, axis=1) - inside
                jumps.append(jump)
                if s == 1:
                    sum_ref[slot, f] = side_sum_ref[y, f] + stored_ref[y, f, :, :LANES] * jump
            for f, term in enumerate(face_flux(jumps, 0, coefs)):
                flux_ref[slot, s, f, :, :LANES] = term
        if 0 < y < last_y:
            flux_ref[slot, :, :, :, LANES:] = side_ref[y, :, :, :, :LANES]
            return
        edge = (edge_ref[0, 0, y], edge_ref[0, 1, y])
        turn = source_ref[1, y]
        take_two = jnp.logical_not(odd_y) if y == 0 else odd_y
        outer = upper if y == 0 else jnp.logical_not(upper)
        inner_row = 1 if y == 0 else last_y - 1
        for s in range(2):
            jumps = []
            for f in range(fields):
                received = jnp.where(take_two, y_two[f], y_one[f])
                if s == 1:
                    received = pltpu.roll(received, FACE, 1)
                inside = trace_ref[s, y, f, :, :LANES]
                mixed = jnp.where(outer, received, trace_ref[s, inner_row, f, :, :LANES])
                turned = jnp.take_along_axis(mixed, turn, axis=1)
                jump = rim_jump(turned, inside, edge, f)
                jumps.append(jump)
                if s == 1:
                    sum_ref[slot, f] += stored_ref[y, f, :, LANES : 2 * LANES] * jump
            for f, term in enumerate(face_flux(jumps, 1, coefs)):
                flux_ref[slot, s, f, :, LANES:] = term

    def results(y):
        slot = order.index(y) % 2
        for s in range(2):
            lifted = jnp.dot(
                flux_ref[slot, s].reshape(fields * count_z, 2 * LANES),
                lift_ref[: 2 * LANES],
                preferred_element_type=jnp.float32,
            ) + jnp.dot(
                side_ref[y, s, :, :, LANES:].reshape(fields * count_z, LANES),
                lift_ref[2 * LANES :],
                preferred_element_type=jnp.float32,
            )
            scale = step_size if s == 0 else -step_size
            out_ref[s, y] = partial_ref[s, y] + scale * lifted.reshape(fields, count_z, nodes)
            write(s, y).start()
        for f in range(fields):
            sums = jnp.sum(sum_ref[slot, f], axis=1, keepdims=True) * (1.0 / FACE)
            across = jnp.sum(jnp.where(z_pos == lane, sums, 0.0), axis=0, keepdims=True)
            kernel_ref[f, pl.ds(y, 1), :] = across[:, :count_z]

    fluxes(order[0])
    for k, y in enumerate(order):
        if k + 1 < count_y:
            fluxes(order[k + 1])
        results(y)
    for y in range(count_y):
        for s in range(2):
            write(s, y).wait()


def finish(
    state, traces, far, near, y_two, y_one, coef, source, edge, side, side_sum, part, stored, lift
):
    _, count_y, fields, count_z, nodes = state.shape
    f32 = jnp.float32
    outs = (
        jax.ShapeDtypeStruct(state.shape, f32),
        jax.ShapeDtypeStruct((fields, count_y, count_z), f32),
    )
    return pl.pallas_call(
        final_kernel,
        out_shape=outs,
        in_specs=[pl.BlockSpec(memory_space=pltpu.VMEM)] * 14,
        out_specs=(pl.BlockSpec(memory_space=pl.ANY), pl.BlockSpec(memory_space=pltpu.VMEM)),
        scratch_shapes=[
            pltpu.VMEM((2, 2, fields, count_z, 2 * LANES), jnp.bfloat16),
            pltpu.VMEM((2, fields, count_z, LANES), f32),
            pltpu.VMEM(state.shape, f32),
            pltpu.SemaphoreType.DMA((2, count_y)),
        ],
        compiler_params=pltpu.CompilerParams(vmem_limit_bytes=LIMIT),
        cost_estimate=pl.CostEstimate(flops=9 * 10**8, bytes_accessed=10**7, transcendentals=0),
        name="finish",
    )(state, traces, far, near, y_two, y_one, coef, source, edge, side, side_sum, part, stored, lift)


def swaps(count, start, wrap):
    pairs = []
    for i in range(start, count if wrap else count - 1, 2):
        j = (i + 1) % count
        pairs += [(i, j), (j, i)]
    return pairs


def inner_swaps(count, other):
    pairs = []
    for i in range(count):
        for k in range(other):
            if i in (0, count - 1):
                pairs.append((i, k, i, k ^ 1))
            else:
                pairs.append((i, k, i + 1 if i % 2 == 1 else i - 1, k))
    return pairs


def local(state, deriv, lift, material, stored, orient, flags):
    view = jnp.transpose(state[:, 0], (0, 1, 3, 2, 4))
    stored_view = jnp.transpose(stored[0], (0, 2, 1, 3))
    orient_view = jnp.transpose(orient[0], (2, 0, 1))
    flags_view = jnp.transpose(flags[0], (2, 0, 1))
    nx, ny, nz = (lax.axis_size(a) for a in ("gx", "gy", "gz"))
    table = jnp.asarray(trace_table(), jnp.bfloat16)
    view, far, near = pack_faces(view)
    far_in = lax.ppermute(far, "gx", swaps(nx, 1, True))
    near_in = lax.ppermute(near, "gx", swaps(nx, 0, True))
    traces, y_two, y_one, z_two, z_one = extract_traces(view, table)
    y_one = lax.ppermute(y_one, "gy", swaps(ny, 0, False))
    pairs = [(y * nz + z, b * nz + a) for y, z, b, a in inner_swaps(ny, nz)]
    y_two = lax.ppermute(y_two, ("gy", "gz"), pairs)
    z_one = lax.ppermute(z_one, "gz", swaps(nz, 0, False))
    medium = material[:, 0]
    z_two, medium, y_one = lax.optimization_barrier((z_two, medium, y_one))
    pairs = [(y * nz + z, b * nz + a) for z, y, a, b in inner_swaps(nz, ny)]
    z_two = lax.ppermute(z_two, ("gy", "gz"), pairs)
    part, coef, source, edge = volume(view, deriv, medium, orient_view, flags_view)
    side, side_sum = side_faces(traces, z_two, z_one, coef, source, edge, stored_view)
    advanced, kernel = finish(
        view, traces, far_in, near_in, y_two, y_one, coef, source, edge, side, side_sum, part,
        stored_view, lift,
    )
    return (
        jnp.transpose(advanced, (0, 1, 3, 2, 4))[:, None],
        jnp.transpose(kernel, (1, 2, 0))[None],
    )


def solution(mesh):
    placed = (
        P(None, "gx", "gy", "gz", None, None),
        P(),
        P(),
        P(None, "gx", "gy", "gz"),
        P("gx", "gy", "gz", None, None),
        P("gx", "gy", "gz", None),
        P("gx", "gy", "gz", None),
    )
    return jax.shard_map(
        local,
        mesh=mesh,
        in_specs=placed,
        out_specs=(P(None, "gx", "gy", "gz", None, None), P("gx", "gy", "gz", None)),
        check_vma=False,
    )
```

```python
import jax
import jax.numpy as jnp
import numpy as np
from functools import partial
from jax import lax
from jax.experimental import pallas as pl
from jax.experimental.pallas import tpu as pltpu
from jax.sharding import PartitionSpec as P

NP = 8
FACE = NP * NP
LANES = 128
step_size = 0.15
stress_slot = ((3, 8, 7), (8, 4, 6), (7, 6, 5))
shear_pairs = ((6, 1, 2), (7, 0, 2), (8, 0, 1))
LIMIT = 20 * 1024 * 1024
PACK_LIMIT = 50 * 1024 * 1024


def trace_table():
    table = np.zeros((NP**3, 4 * FACE), np.float32)
    for first in range(NP):
        for second in range(NP):
            m = first * NP + second
            table[first * 64 + second, m] = 1.0
            table[first * 64 + 56 + second, FACE + m] = 1.0
            table[first * 64 + second * 8, 2 * FACE + m] = 1.0
            table[first * 64 + second * 8 + 7, 3 * FACE + m] = 1.0
    return table


def lane_index(shape):
    return lax.broadcasted_iota(jnp.int32, shape, len(shape) - 1)


def merged(forward, adjoint, upper):
    rows = forward.shape[:-1]
    flat = (-1, LANES)
    turned = pltpu.roll(adjoint.reshape(flat), FACE, 1)
    own = (lane_index(turned.shape) >= FACE) == upper
    return jnp.where(own, forward.reshape(flat), turned).reshape(rows + (LANES,))


def odd_position(axis):
    return lax.axis_index(axis) % 2 == 1


def pack_kernel(state_ref, held_ref, far_ref, near_ref, sem):
    odd = odd_position("gx")
    tiles = state_ref.shape[-1] // LANES
    order = [0, tiles - 1] + list(range(1, tiles - 1))

    def fetch(t):
        columns = pl.ds(t * LANES, LANES)
        return pltpu.make_async_copy(
            state_ref.at[:, :, :, :, columns], held_ref.at[:, :, :, :, columns], sem.at[t]
        )

    for t in order:
        fetch(t).start()
    low, high = slice(0, LANES), slice((tiles - 1) * LANES, tiles * LANES)

    def put(message, upper):
        def faces(columns):
            for y in range(message.shape[0]):
                message[y] = merged(
                    held_ref[0, y, :, :, columns], held_ref[1, y, :, :, columns], upper
                )

        faces(high if upper else low)

    for t, upper in ((order[0], False), (order[1], True)):
        fetch(t).wait()

        @pl.when(odd == upper)
        def _():
            put(far_ref, upper)

        @pl.when(odd != upper)
        def _():
            put(near_ref, upper)

    for t in order[2:]:
        fetch(t).wait()


def pack_faces(state):
    _, count_y, fields, count_z, nodes = state.shape
    message = jax.ShapeDtypeStruct((count_y, fields, count_z, LANES), jnp.float32)
    return pl.pallas_call(
        pack_kernel,
        out_shape=(jax.ShapeDtypeStruct(state.shape, jnp.float32), message, message),
        in_specs=[pl.BlockSpec(memory_space=pl.ANY)],
        out_specs=(pl.BlockSpec(memory_space=pltpu.VMEM),) * 3,
        scratch_shapes=[pltpu.SemaphoreType.DMA((nodes // LANES,))],
        compiler_params=pltpu.CompilerParams(vmem_limit_bytes=PACK_LIMIT),
        cost_estimate=pl.CostEstimate(flops=10**6, bytes_accessed=2 * 10**6, transcendentals=0),
        name="pack_faces",
    )(state)


def trace_kernel(state_ref, table_ref, trace_ref, y_two, y_one, z_two, z_one):
    _, count_y, fields, count_z, _ = state_ref.shape

    def one_state(s):
        values = state_ref[s].reshape(count_y * fields * count_z, -1)
        high = values.astype(jnp.bfloat16)
        low = (values - high.astype(jnp.float32)).astype(jnp.bfloat16)
        table = table_ref[...]
        picked = jnp.dot(high, table, preferred_element_type=jnp.float32)
        picked = picked + jnp.dot(low, table, preferred_element_type=jnp.float32)
        trace_ref[s] = picked.reshape(count_y, fields, count_z, 2 * LANES)

    for s in range(2):
        one_state(s)
    odd_y = odd_position("gy")
    odd_z = odd_position("gz")
    end = count_y - 1
    down = merged(trace_ref[0, 0, :, :, :LANES], trace_ref[1, 0, :, :, :LANES], False)
    up = merged(trace_ref[0, end, :, :, :LANES], trace_ref[1, end, :, :, :LANES], True)
    y_two[...] = jnp.where(odd_y, up, down)
    y_one[...] = jnp.where(odd_y, down, up)
    for s in range(2):
        for y in range(count_y):
            first = trace_ref[s, y, :, 0, LANES:]
            last = trace_ref[s, y, :, count_z - 1, LANES:]
            z_two[s, y] = jnp.where(odd_z, last, first)
            z_one[s, y] = jnp.where(odd_z, first, last)


def extract_traces(state, table):
    _, count_y, fields, count_z, nodes = state.shape
    f32 = jnp.float32
    y_message = jax.ShapeDtypeStruct((fields, count_z, LANES), f32)
    z_message = jax.ShapeDtypeStruct((2, count_y, fields, LANES), f32)
    return pl.pallas_call(
        trace_kernel,
        out_shape=(
            jax.ShapeDtypeStruct((2, count_y, fields, count_z, 2 * LANES), f32),
            y_message,
            y_message,
            z_message,
            z_message,
        ),
        in_specs=[pl.BlockSpec(memory_space=pltpu.VMEM)] * 2,
        out_specs=(pl.BlockSpec(memory_space=pltpu.VMEM),) * 5,
        compiler_params=pltpu.CompilerParams(vmem_limit_bytes=LIMIT),
        cost_estimate=pl.CostEstimate(flops=6 * 10**8, bytes_accessed=4 * 10**6, transcendentals=0),
        name="extract_traces",
    )(state, table)


def spread(columns, rows, pick):
    return lax.dot_general(
        columns,
        pick,
        (((0,), (0,)), ((), ())),
        precision=lax.Precision.HIGHEST,
        preferred_element_type=jnp.float32,
    )


def volume_kernel(
    state_ref, deriv_ref, material_ref, orient_ref, flags_ref,
    partial_ref, coef_ref, source_ref, edge_ref,
    low_ref, grad_ref, div_ref, wide_ref,
):
    _, count_y, fields, count_z, _ = state_ref.shape
    rows = 2 * count_y * count_z
    nodes = partial_ref.shape[-1]
    width = grad_ref.shape[-1]
    ends = [
        lax.axis_index("gy") == 0,
        lax.axis_index("gy") == lax.axis_size("gy") - 1,
        lax.axis_index("gz") == 0,
        lax.axis_index("gz") == lax.axis_size("gz") - 1,
    ]

    for f in range(fields):
        low_ref[f] = state_ref[:, :, f].reshape(rows, -1).astype(jnp.bfloat16)
    lanes = lane_index((3 * count_y, 3 * count_y * LANES))
    row = lax.broadcasted_iota(jnp.int32, lanes.shape, 0)
    pick = (lanes // LANES == row).astype(jnp.float32)
    medium = spread(material_ref[...].reshape(3 * count_y, count_z), 3 * count_y, pick)
    lanes = lane_index((6 * count_y, 3 * count_y * LANES))
    row = lax.broadcasted_iota(jnp.int32, lanes.shape, 0)
    block = lanes // LANES
    face = 2 * (block // count_y) + (lanes % LANES) // FACE
    pick = (face * count_y + block % count_y == row).astype(jnp.float32)
    codes = spread(
        orient_ref[...].reshape(6 * count_y, count_z).astype(jnp.float32), 6 * count_y, pick
    )
    kinds = spread(
        flags_ref[...].reshape(6 * count_y, count_z).astype(jnp.float32), 6 * count_y, pick
    )
    lane = lane_index((count_z, LANES))
    upper = lane >= FACE
    half_sign = jnp.where(upper, 0.5, -0.5)
    node = lane % FACE
    near, far = (node // NP, node % NP)
    z_pos = lax.broadcasted_iota(jnp.int32, lane.shape, 0)
    for y in range(count_y):
        lam = medium[:, y * LANES : (y + 1) * LANES]
        mu = medium[:, (count_y + y) * LANES : (count_y + y + 1) * LANES]
        rho = medium[:, (2 * count_y + y) * LANES : (2 * count_y + y + 1) * LANES]
        inv = 1.0 / rho
        wide_ref[0, y] = lam
        wide_ref[1, y] = mu
        wide_ref[2, y] = inv
        coef_ref[0, y] = half_sign * lam
        coef_ref[1, y] = half_sign * mu
        coef_ref[2, y] = half_sign * inv
        coef_ref[3, y] = 0.5 * jnp.sqrt((lam + 2.0 * mu) * inv)
        for d in range(3):
            at = (d * count_y + y) * LANES
            code = jnp.round(codes[:, at : at + LANES]).astype(jnp.int32)
            swap = code >= 4
            lead = jnp.where(swap, far, near)
            trail = jnp.where(swap, near, far)
            lead = jnp.where(code % 2 == 1, NP - 1 - lead, lead)
            trail = jnp.where((code // 2) % 2 == 1, NP - 1 - trail, trail)
            source_ref[d, y] = lead * NP + trail + jnp.where(upper, 0, FACE)
            if d > 0:
                free = jnp.where(jnp.round(kinds[:, at : at + LANES]) == 1.0, 1.0, 0.0)
                if d == 1:
                    low_end = (ends[0]) if y == 0 else False
                    high_end = (ends[1]) if y == count_y - 1 else False
                    rim = jnp.where(
                        upper,
                        jnp.where(high_end, 1.0, 0.0),
                        jnp.where(low_end, 1.0, 0.0),
                    )
                else:
                    low_rim = jnp.where(z_pos == 0, jnp.where(ends[2], 1.0, 0.0), 0.0)
                    high_rim = jnp.where(
                        z_pos == count_z - 1, jnp.where(ends[3], 1.0, 0.0), 0.0
                    )
                    rim = jnp.where(upper, high_rim, low_rim)
                edge_ref[d - 1, 0, y] = rim
                edge_ref[d - 1, 1, y] = free

    def columns_part(n):
        base = n * width

        def operator(d):
            return deriv_ref[:, d * nodes + base : d * nodes + base + width]

        velocity = low_ref[0:3].reshape(3 * rows, nodes)
        for d in range(3):
            grad_ref[d] = jnp.dot(velocity, operator(d), preferred_element_type=jnp.float32)
        total = None
        for d in range(3):
            stress = jnp.concatenate([low_ref[stress_slot[i][d]] for i in range(3)], axis=0)
            part = jnp.dot(stress, operator(d), preferred_element_type=jnp.float32)
            total = part if total is None else total + part
        div_ref[...] = total
        for s in range(2):
            scale = step_size if s == 0 else -step_size
            for y in range(count_y):
                at = (s * count_y + y) * count_z
                lam = scale * wide_ref[0, y]
                mu = scale * wide_ref[1, y]
                inv = scale * wide_ref[2, y]
                for tile in range(width // LANES):
                    columns = slice(tile * LANES, (tile + 1) * LANES)
                    where = slice(base + tile * LANES, base + (tile + 1) * LANES)

                    def g(d, i):
                        return grad_ref[d, i * rows + at : i * rows + at + count_z, columns]

                    def put(f, term):
                        partial_ref[s, y, f, :, where] = state_ref[s, y, f, :, where] + term

                    for i in range(3):
                        put(i, inv * div_ref[i * rows + at : i * rows + at + count_z, columns])
                    diag = [g(i, i) for i in range(3)]
                    common = lam * (diag[0] + diag[1] + diag[2])
                    for i in range(3):
                        put(3 + i, common + (mu + mu) * diag[i])
                    for f, i, j in shear_pairs:
                        put(f, mu * (g(j, i) + g(i, j)))

    for n in range(nodes // width):
        columns_part(n)


def volume(state, deriv, material, orient, flags):
    _, count_y, fields, count_z, nodes = state.shape
    f32 = jnp.float32
    width = 256
    rows = 2 * count_y * count_z
    outs = (
        jax.ShapeDtypeStruct(state.shape, f32),
        jax.ShapeDtypeStruct((4, count_y, count_z, LANES), f32),
        jax.ShapeDtypeStruct((3, count_y, count_z, LANES), jnp.int32),
        jax.ShapeDtypeStruct((2, 2, count_y, count_z, LANES), f32),
    )
    return pl.pallas_call(
        volume_kernel,
        out_shape=outs,
        in_specs=[pl.BlockSpec(memory_space=pltpu.VMEM)] * 5,
        out_specs=(pl.BlockSpec(memory_space=pltpu.VMEM),) * 4,
        scratch_shapes=[
            pltpu.VMEM((fields, rows, nodes), jnp.bfloat16),
            pltpu.VMEM((3, 3 * rows, width), f32),
            pltpu.VMEM((3 * rows, width), f32),
            pltpu.VMEM((3, count_y, count_z, LANES), f32),
        ],
        compiler_params=pltpu.CompilerParams(vmem_limit_bytes=LIMIT),
        cost_estimate=pl.CostEstimate(
            flops=10**6, bytes_accessed=10**5, transcendentals=0
        ),
        name="volume",
    )(state, deriv, material, orient, flags)


def face_flux(jumps, d, coefs):
    lam, mu, inv, speed = coefs
    flux = [speed * jump for jump in jumps]
    for i in range(3):
        flux[i] = flux[i] + inv * jumps[stress_slot[i][d]]
    common = lam * jumps[d]
    for i in range(3):
        flux[3 + i] = flux[3 + i] + common
    for i, j, f in ((0, 0, 3), (1, 1, 4), (2, 2, 5), (1, 2, 6), (0, 2, 7), (0, 1, 8)):
        if j == d:
            flux[f] = flux[f] + mu * jumps[i]
        if i == d:
            flux[f] = flux[f] + mu * jumps[j]
    return [term.astype(jnp.bfloat16) for term in flux]


def rim_jump(turned, inside, edge, f):
    rim, free = edge
    keep = free - 1.0 if f < 3 else -free - 1.0
    return jnp.where(rim > 0.0, inside * keep, turned - inside)


def side_kernel(
    trace_ref, z_two, z_one, coef_ref, source_ref, edge_ref, stored_ref, flux_ref, sum_ref
):
    _, count_y, fields, count_z, _ = trace_ref.shape
    last_y = count_y - 1
    odd_z = odd_position("gz")
    lane = lane_index((count_z, LANES))
    upper = lane >= FACE
    z_pos = lax.broadcasted_iota(jnp.int32, lane.shape, 0)
    at_low = jnp.logical_and(z_pos == 0, upper)
    at_high = jnp.logical_and(z_pos == count_z - 1, jnp.logical_not(upper))

    def row(y):
        coefs = [coef_ref[k, y] for k in range(4)]
        edge = (edge_ref[1, 0, y], edge_ref[1, 1, y])
        source = source_ref[2, y]
        for s in range(2):
            jumps = []
            for f in range(fields):
                inside = trace_ref[s, y, f, :, LANES:]
                two = z_two[s, y, f : f + 1, :]
                one = z_one[s, y, f : f + 1, :]
                from_below = jnp.where(odd_z, one, two)
                from_above = jnp.where(odd_z, two, one)
                mixed = jnp.where(upper, pltpu.roll(inside, 1, 0), pltpu.roll(inside, count_z - 1, 0))
                mixed = jnp.where(at_low, from_below, jnp.where(at_high, from_above, mixed))
                turned = jnp.take_along_axis(mixed, source, axis=1)
                jump = rim_jump(turned, inside, edge, f)
                jumps.append(jump)
                if s == 1:
                    sum_ref[y, f] = stored_ref[y, f, :, 2 * LANES :] * jump
            for f, term in enumerate(face_flux(jumps, 2, coefs)):
                flux_ref[y, s, f, :, LANES:] = term

        if 0 < y < last_y:
            turn = source_ref[1, y]
            for s in range(2):
                jumps = []
                for f in range(fields):
                    inside = trace_ref[s, y, f, :, :LANES]
                    mixed = jnp.where(
                        upper, trace_ref[s, y - 1, f, :, :LANES], trace_ref[s, y + 1, f, :, :LANES]
                    )
                    jump = jnp.take_along_axis(mixed, turn, axis=1) - inside
                    jumps.append(jump)
                    if s == 1:
                        sum_ref[y, f] += stored_ref[y, f, :, LANES : 2 * LANES] * jump
                for f, term in enumerate(face_flux(jumps, 1, coefs)):
                    flux_ref[y, s, f, :, :LANES] = term

    for y in range(count_y):
        row(y)


def side_faces(traces, z_two, z_one, coef, source, edge, stored):
    _, count_y, fields, count_z, _ = traces.shape
    return pl.pallas_call(
        side_kernel,
        out_shape=(
            jax.ShapeDtypeStruct((count_y, 2, fields, count_z, 2 * LANES), jnp.bfloat16),
            jax.ShapeDtypeStruct((count_y, fields, count_z, LANES), jnp.float32),
        ),
        in_specs=[pl.BlockSpec(memory_space=pltpu.VMEM)] * 7,
        out_specs=(pl.BlockSpec(memory_space=pltpu.VMEM),) * 2,
        compiler_params=pltpu.CompilerParams(vmem_limit_bytes=LIMIT),
        cost_estimate=pl.CostEstimate(flops=10**6, bytes_accessed=10**5, transcendentals=0),
        name="side_faces",
    )(traces, z_two, z_one, coef, source, edge, stored)


def final_kernel(
    state_ref, trace_ref, far_ref, near_ref, y_two, y_one, coef_ref, source_ref, edge_ref,
    side_ref, side_sum_ref, partial_ref, stored_ref, lift_ref,
    advanced_ref, kernel_ref,
    flux_ref, sum_ref, out_ref, out_sem,
):
    _, count_y, fields, count_z, nodes = state_ref.shape
    last_y = count_y - 1
    lane = lane_index((count_z, LANES))
    upper = lane >= FACE
    z_pos = lax.broadcasted_iota(jnp.int32, lane.shape, 0)
    take_near = upper == odd_position("gx")
    odd_y = odd_position("gy")

    def write(s, y):
        return pltpu.make_async_copy(out_ref.at[s, y], advanced_ref.at[s, y], out_sem.at[s, y])

    order = list(range(1, last_y)) + [0, last_y]

    def fluxes(y):
        slot = order.index(y) % 2
        coefs = [coef_ref[k, y] for k in range(4)]
        for s in range(2):
            source = source_ref[0, y]
            if s == 1:
                source = (source + FACE) % LANES
            jumps = []
            for f in range(fields):
                inside = jnp.where(
                    upper, state_ref[s, y, f, :, nodes - LANES :], state_ref[s, y, f, :, :LANES]
                )
                near, far = (near_ref[y, f], far_ref[y, f])
                if s == 1:
                    near, far = (far, near)
                mixed = jnp.where(take_near, near, far)
                jump = jnp.take_along_axis(mixed, source, axis=1) - inside
                jumps.append(jump)
                if s == 1:
                    sum_ref[slot, f] = side_sum_ref[y, f] + stored_ref[y, f, :, :LANES] * jump
            for f, term in enumerate(face_flux(jumps, 0, coefs)):
                flux_ref[slot, s, f, :, :LANES] = term
        if 0 < y < last_y:
            flux_ref[slot, :, :, :, LANES:] = side_ref[y, :, :, :, :LANES]
            return
        edge = (edge_ref[0, 0, y], edge_ref[0, 1, y])
        turn = source_ref[1, y]
        take_two = jnp.logical_not(odd_y) if y == 0 else odd_y
        outer = upper if y == 0 else jnp.logical_not(upper)
        inner_row = 1 if y == 0 else last_y - 1
        for s in range(2):
            jumps = []
            for f in range(fields):
                received = jnp.where(take_two, y_two[f], y_one[f])
                if s == 1:
                    received = pltpu.roll(received, FACE, 1)
                inside = trace_ref[s, y, f, :, :LANES]
                mixed = jnp.where(outer, received, trace_ref[s, inner_row, f, :, :LANES])
                turned = jnp.take_along_axis(mixed, turn, axis=1)
                jump = rim_jump(turned, inside, edge, f)
                jumps.append(jump)
                if s == 1:
                    sum_ref[slot, f] += stored_ref[y, f, :, LANES : 2 * LANES] * jump
            for f, term in enumerate(face_flux(jumps, 1, coefs)):
                flux_ref[slot, s, f, :, LANES:] = term

    def results(y):
        slot = order.index(y) % 2
        for s in range(2):
            lifted = jnp.dot(
                flux_ref[slot, s].reshape(fields * count_z, 2 * LANES),
                lift_ref[: 2 * LANES],
                preferred_element_type=jnp.float32,
            ) + jnp.dot(
                side_ref[y, s, :, :, LANES:].reshape(fields * count_z, LANES),
                lift_ref[2 * LANES :],
                preferred_element_type=jnp.float32,
            )
            scale = step_size if s == 0 else -step_size
            out_ref[s, y] = partial_ref[s, y] + scale * lifted.reshape(fields, count_z, nodes)
            write(s, y).start()
        for f in range(fields):
            sums = jnp.sum(sum_ref[slot, f], axis=1, keepdims=True) * (1.0 / FACE)
            across = jnp.sum(jnp.where(z_pos == lane, sums, 0.0), axis=0, keepdims=True)
            kernel_ref[f, pl.ds(y, 1), :] = across[:, :count_z]

    fluxes(order[0])
    for k, y in enumerate(order):
        if k + 1 < count_y:
            fluxes(order[k + 1])
        results(y)
    for y in range(count_y):
        for s in range(2):
            write(s, y).wait()


def finish(
    state, traces, far, near, y_two, y_one, coef, source, edge, side, side_sum, part, stored, lift
):
    _, count_y, fields, count_z, nodes = state.shape
    f32 = jnp.float32
    outs = (
        jax.ShapeDtypeStruct(state.shape, f32),
        jax.ShapeDtypeStruct((fields, count_y, count_z), f32),
    )
    return pl.pallas_call(
        final_kernel,
        out_shape=outs,
        in_specs=[pl.BlockSpec(memory_space=pltpu.VMEM)] * 14,
        out_specs=(pl.BlockSpec(memory_space=pl.ANY), pl.BlockSpec(memory_space=pltpu.VMEM)),
        scratch_shapes=[
            pltpu.VMEM((2, 2, fields, count_z, 2 * LANES), jnp.bfloat16),
            pltpu.VMEM((2, fields, count_z, LANES), f32),
            pltpu.VMEM(state.shape, f32),
            pltpu.SemaphoreType.DMA((2, count_y)),
        ],
        compiler_params=pltpu.CompilerParams(vmem_limit_bytes=LIMIT),
        cost_estimate=pl.CostEstimate(flops=9 * 10**8, bytes_accessed=10**7, transcendentals=0),
        name="finish",
    )(state, traces, far, near, y_two, y_one, coef, source, edge, side, side_sum, part, stored, lift)


def swaps(count, start, wrap):
    pairs = []
    for i in range(start, count if wrap else count - 1, 2):
        j = (i + 1) % count
        pairs += [(i, j), (j, i)]
    return pairs


def inner_swaps(count, other):
    pairs = []
    for i in range(count):
        for k in range(other):
            if i in (0, count - 1):
                pairs.append((i, k, i, k ^ 1))
            else:
                pairs.append((i, k, i + 1 if i % 2 == 1 else i - 1, k))
    return pairs


def local(state, deriv, lift, material, stored, orient, flags):
    view = jnp.transpose(state[:, 0], (0, 1, 3, 2, 4))
    stored_view = jnp.transpose(stored[0], (0, 2, 1, 3))
    orient_view = jnp.transpose(orient[0], (2, 0, 1))
    flags_view = jnp.transpose(flags[0], (2, 0, 1))
    nx, ny, nz = (lax.axis_size(a) for a in ("gx", "gy", "gz"))
    table = jnp.asarray(trace_table(), jnp.bfloat16)
    view, far, near = pack_faces(view)
    far_in = lax.ppermute(far, "gx", swaps(nx, 1, True))
    near_in = lax.ppermute(near, "gx", swaps(nx, 0, True))
    traces, y_two, y_one, z_two, z_one = extract_traces(view, table)
    y_one = lax.ppermute(y_one, "gy", swaps(ny, 0, False))
    pairs = [(y * nz + z, b * nz + a) for y, z, b, a in inner_swaps(ny, nz)]
    y_two = lax.ppermute(y_two, ("gy", "gz"), pairs)
    z_one = lax.ppermute(z_one, "gz", swaps(nz, 0, False))
    medium = material[:, 0]
    z_two, medium, y_one = lax.optimization_barrier((z_two, medium, y_one))
    pairs = [(y * nz + z, b * nz + a) for z, y, a, b in inner_swaps(nz, ny)]
    z_two = lax.ppermute(z_two, ("gy", "gz"), pairs)
    part, coef, source, edge = volume(view, deriv, medium, orient_view, flags_view)
    side, side_sum = side_faces(traces, z_two, z_one, coef, source, edge, stored_view)
    advanced, kernel = finish(
        view, traces, far_in, near_in, y_two, y_one, coef, source, edge, side, side_sum, part,
        stored_view, lift,
    )
    return (
        jnp.transpose(advanced, (0, 1, 3, 2, 4))[:, None],
        jnp.transpose(kernel, (1, 2, 0))[None],
    )


def solution(mesh):
    placed = (
        P(None, "gx", "gy", "gz", None, None),
        P(),
        P(),
        P(None, "gx", "gy", "gz"),
        P("gx", "gy", "gz", None, None),
        P("gx", "gy", "gz", None),
        P("gx", "gy", "gz", None),
    )
    return jax.shard_map(
        local,
        mesh=mesh,
        in_specs=placed,
        out_specs=(P(None, "gx", "gy", "gz", None, None), P("gx", "gy", "gz", None)),
        check_vma=False,
    )
```
